32 devices in a mesh: dp: 4 (over y, x), seq: 8 (over z, core).
Axes of the slice: x: 2, y: 2, z: 4, core: 2. Of those that a mesh axis runs over, the one named last changes fastest.
Arguments:
- hidden_input: bfloat16 [4, 1024, 768], P('dp', 'seq'), may hold values from -7.2 to 7.2
- triple_weight: bfloat16 [2, 768, 2304], P(None, ('dp', 'seq')), may hold values from -0.21875 to 0.21875
- mixer_weight: bfloat16 [2, 768, 768], P(None, ('dp', 'seq')), may hold values from -0.21875 to 0.21875
- expand_weight: bfloat16 [2, 768, 3072], P(None, ('dp', 'seq')), may hold values from -0.21875 to 0.21875
- shrink_weight: bfloat16 [2, 3072, 768], P(None, ('dp', 'seq')), may hold values from -0.109375 to 0.109375
- vector_params: bfloat16 [2, 12, 768], P(None, None, ('dp', 'seq')), may hold values from -1.5 to 1.5
- output_grad: bfloat16 [4, 1024, 768], P('dp', 'seq'), may hold values from -6 to 6
Outputs:
- hidden_output: bfloat16 [4, 1024, 768], P('dp', 'seq')
- input_grad: bfloat16 [4, 1024, 768], P('dp', 'seq')
- triple_grad: float32 [2, 768, 2304], P(None, ('dp', 'seq'))
- mixer_grad: float32 [2, 768, 768], P(None, ('dp', 'seq'))
- expand_grad: float32 [2, 768, 3072], P(None, ('dp', 'seq'))
- shrink_grad: float32 [2, 3072, 768], P(None, ('dp', 'seq'))
- vector_grad: float32 [2, 12, 768], P(None, None, ('dp', 'seq'))
- root_squares: float32 [2, 3], replicated
The draws below stay inside these ranges and needn't reach their ends.
All inputs are finite; a program needn't handle non-finite values.
Results may differ from the reference program's by a relative error of at most 0.014.
Values may be sent and summed in bfloat16 or wider, within the bound.
No kernel may reach another device: no remote copies, remote signals or barrier semaphores. Data moves between devices by JAX's collectives and lax.ppermute only.
A program may use at most 448 MiB of HBM per device.

```python
import jax
import jax.numpy as jnp
from jax import lax

D = 768
HEADS = 12
HEAD = 64
FF = 3072
LAYERS = 2
BATCH = 4
LEN = 1024


def draw_hidden_input(key, part):
    row_place = jnp.arange(BATCH, dtype=jnp.float32)[:, None] * LEN
    token_place = jnp.arange(LEN, dtype=jnp.float32)[None, :]
    place = ((row_place + token_place) / (BATCH * LEN))[:, :, None]
    rising = 0.6 * jnp.exp(jnp.log(3.0) * place)
    base = jnp.clip(jax.random.normal(key, (BATCH, LEN, D), jnp.float32), -4.0, 4.0)
    return (base * rising).astype(jnp.bfloat16)


def draw_vector_params(key, part):
    biases = 0.3 * jnp.clip(jax.random.normal(jax.random.fold_in(key, 11), (LAYERS, 12, D), jnp.float32), -5.0, 5.0)
    gains = jax.random.uniform(jax.random.fold_in(key, 12), (LAYERS, 12, D), jnp.float32, 0.6, 1.4)
    row_number = jnp.arange(12)[None, :, None]
    is_gain = (row_number == 3) | (row_number == 10)
    return jnp.where(is_gain, gains, biases).astype(jnp.bfloat16)


def block_scale(key, shape, pieces, least, high):
    def one(axis_at, shards_of):
        steps = jax.random.uniform(jax.random.fold_in(jax.random.fold_in(key, 6), axis_at), (shards_of,), jnp.float32, least / len(pieces), high / len(pieces))
        return jnp.repeat(jnp.exp(steps), shape[axis_at] // shards_of).reshape((-1,) + (1,) * (len(shape) - axis_at - 1))

    factor_of = one(*pieces[0])
    for cut in pieces[1:]:
        factor_of = factor_of * one(*cut)
    return factor_of


def scatter_about(rng, shape, scale, reach, cuts=(), kind=jnp.bfloat16):
    array = jax.random.normal(rng, shape, jnp.float32) * scale
    if len(cuts) > 0:
        array = block_scale(rng, shape, cuts, -0.22, 0.18) * array
    return jnp.clip(array, min=-reach, max=reach).astype(kind)


def setup_inputs(seed: int = 0) -> dict:
    arg_keys = jax.random.split(jax.random.key(seed), 8)
    return {
        "hidden_input": draw_hidden_input(jax.random.fold_in(arg_keys[7], 71), 0),
        "triple_weight": scatter_about(arg_keys[1], (LAYERS, D, 3 * D), D ** -0.5, 0.21875, ((1, 32),)),
        "mixer_weight": scatter_about(arg_keys[2], (LAYERS, D, D), D ** -0.5, 0.21875, ((1, 32),)),
        "expand_weight": scatter_about(arg_keys[3], (LAYERS, D, FF), D ** -0.5, 0.21875, ((1, 32),)),
        "shrink_weight": scatter_about(arg_keys[4], (LAYERS, FF, D), FF ** -0.5, 0.109375, ((1, 32),)),
        "vector_params": draw_vector_params(jax.random.fold_in(arg_keys[7], 71), 0),
        "output_grad": scatter_about(arg_keys[6], (BATCH, LEN, D), 1.0, 6.0, ((0, 4), (1, 8))),
    }


@jax.custom_vjp
def low(v):
    return lax.optimization_barrier(v.astype(jnp.bfloat16)).astype(jnp.float32)

@jax.custom_vjp
def low_back(v):
    return v

def low_keep(v):
    return (low(v), None)

def low_pass(kept, grad):
    return (grad,)

def back_keep(v):
    return (v, None)

def back_low(kept, grad):
    return (low(grad),)
low.defvjp(low_keep, low_pass)
low_back.defvjp(back_keep, back_low)
EPSILON = 1e-12

def matmul(left, right):
    return jnp.dot(left, right, precision=lax.Precision.HIGHEST, preferred_element_type=jnp.float32)

def layer_norm(residual, gain_row, shift_row):
    center = residual - lax.optimization_barrier(jnp.mean(residual, -1, keepdims=True))
    spread = lax.optimization_barrier(jnp.mean(center * center, -1, keepdims=True))
    return center * lax.rsqrt(spread + EPSILON) * gain_row + shift_row

def head_attend(trio):
    query_head, key_head, value_head = trio
    scores = low_back(matmul(query_head, key_head.T))
    probability = low(jax.nn.softmax(scores, axis=-1))
    return matmul(probability, value_head)

def layer_forward(stream, triple, mixer, expand, shrink, vectors):
    length = stream.shape[0]
    model_width = stream.shape[1]
    project = matmul(low(stream), triple)
    queries = low_back(low((project[:, :model_width] + vectors[0]) * 0.125))
    key_rows = low_back(low(project[:, model_width:2 * model_width]))
    value_rows = low_back(low(project[:, 2 * model_width:] + vectors[1]))

    def to_heads(matrix):
        return matrix.reshape(length, HEADS, HEAD).transpose(1, 0, 2)
    mixed = lax.map(jax.checkpoint(head_attend), (to_heads(queries), to_heads(key_rows), to_heads(value_rows)))
    attended = low_back(low(mixed.transpose(1, 0, 2).reshape(length, model_width)))
    attn_out = low_back(matmul(attended, mixer) + vectors[2])
    normed = layer_norm(stream + attn_out, vectors[3], vectors[4])
    pre_act = low_back(matmul(low(normed), expand) + vectors[5:9].reshape(-1))
    activated = low(jax.nn.gelu(pre_act, approximate=False))
    ffn_out = low_back(matmul(activated, shrink) + vectors[9])
    output = layer_norm(normed + ffn_out, vectors[10], vectors[11])
    square_sums = jnp.stack([jnp.sum(stream * stream), jnp.sum(attn_out * attn_out), jnp.sum(ffn_out * ffn_out)])
    return (output, square_sums)

def reference(hidden_input, triple_weight, mixer_weight, expand_weight, shrink_weight, vector_params, output_grad):
    inputs = hidden_input.astype(jnp.float32)
    params = (triple_weight.astype(jnp.float32), mixer_weight.astype(jnp.float32), expand_weight.astype(jnp.float32), shrink_weight.astype(jnp.float32), vector_params.astype(jnp.float32))

    def forward(values, weights):

        def one_sequence(sequence):
            stream = sequence
            collected = []
            for layer_index in range(LAYERS):
                stream, square_sums = layer_forward(stream, *[member[layer_index] for member in weights])
                collected.append(square_sums)
            return (stream, jnp.stack(collected))
        outputs, squares = lax.map(jax.checkpoint(one_sequence), values)
        return (outputs, lax.optimization_barrier(jnp.sum(squares, 0)))
    (outputs, squares), pull = jax.vjp(forward, inputs, params)
    grad_inputs, grad_params = pull((output_grad.astype(jnp.float32), jnp.zeros_like(squares)))
    root_squares = jnp.sqrt(squares / (BATCH * LEN * D))
    return (outputs.astype(jnp.bfloat16), grad_inputs.astype(jnp.bfloat16), grad_params[0], grad_params[1], grad_params[2], grad_params[3], grad_params[4], root_squares)
```

```python
import jax
import jax.numpy as jnp
import numpy as np
from jax import lax
from jax.sharding import PartitionSpec as P

HEADS = 12
HEAD = 64
LAYERS = 2
VECS = 12
LANES = 128

EPSILON = 1e-12

BF = jnp.bfloat16
F32 = jnp.float32


def layer_norm(residual, gain_row, shift_row):
    center = residual - jnp.mean(residual, -1, keepdims=True)
    spread = jnp.mean(center * center, -1, keepdims=True)
    return center * lax.rsqrt(spread + EPSILON) * gain_row + shift_row


def gelu_exact(values):
    return jax.nn.gelu(values, approximate=False)


def matmul(left, right):
    return jnp.dot(left, right, preferred_element_type=F32)


def matmul_t(left, right):
    return lax.dot_general(left, right, (((1,), (1,)), ((), ())), preferred_element_type=F32)


def grad_matmul(left, right):
    return lax.dot_general(left, right, (((0,), (0,)), ((), ())), preferred_element_type=F32)


def chips_of():
    return lax.axis_size("seq") // 2


def core_swap(array):
    size = lax.axis_size("seq")
    return lax.ppermute(array, "seq", [(i, i ^ 1) for i in range(size)])


def chip_shift(array, step):
    size = lax.axis_size("seq")
    chips = size // 2
    pairs = [(i, ((i // 2 + step) % chips) * 2 + i % 2) for i in range(size)]
    return lax.ppermute(array, "seq", pairs)


def core_groups():
    size = lax.axis_size("seq")
    return [list(range(0, size, 2)), list(range(1, size, 2))]


def place():
    spot = lax.axis_index("seq")
    return spot // 2, spot % 2


def gather_chips(array):
    chips = chips_of()
    if chips > 4:
        return lax.all_gather(
            array, "seq", axis=0, tiled=True, axis_index_groups=core_groups()
        )
    chip, _ = place()
    rows = array.shape[0]
    whole = jnp.zeros((chips * rows, array.shape[1]), array.dtype)
    for step in range(chips):
        part = array if step == 0 else chip_shift(array, step)
        whole = lax.dynamic_update_slice(whole, part, (((chip - step) % chips) * rows, 0))
    return whole


def gather_weight(array):
    own = lax.all_gather(gather_chips(array), "dp", axis=0, tiled=True)
    return join_cores(own, core_swap(own), 0)


def join_cores(own, other, axis):
    _, core = place()
    return jnp.where(
        core == 0,
        jnp.concatenate([own, other], axis),
        jnp.concatenate([other, own], axis),
    )


def scatter_chips(array):
    chips = chips_of()
    if chips > 4:
        return lax.psum_scatter(
            array, "seq", scatter_dimension=0, tiled=True, axis_index_groups=core_groups()
        ).astype(F32)
    chip, _ = place()
    rows = array.shape[0] // chips
    total = None
    for step in range(chips):
        part = lax.dynamic_slice(
            array, (((chip + step) % chips) * rows, 0), (rows, array.shape[1])
        )
        if step > 0:
            part = chip_shift(part, step)
        total = part.astype(F32) if total is None else total + part.astype(F32)
    return total


def scatter_grad(array):
    part = lax.psum_scatter(array.astype(BF), "dp", scatter_dimension=0, tiled=True)
    return scatter_chips(part)


def half_of(array, index):
    width = array.shape[1] // 2
    return lax.dynamic_slice(array, (0, index * width), (array.shape[0], width))


def swap_matrix(width, block):
    spot = np.arange(width)
    target = ((spot // block) % 2) * (width // 2) + (spot // (2 * block)) * block + spot % block
    rows = lax.broadcasted_iota(jnp.int32, (width, width), 0)
    columns = lax.broadcasted_iota(jnp.int32, (width, width), 1)
    goal = ((rows // block) % 2) * (width // 2) + (rows // (2 * block)) * block + rows % block
    return (goal == columns).astype(BF)


def move(array, matrix):
    return jnp.dot(array, matrix, preferred_element_type=F32).astype(BF)


def move_back(array, matrix):
    return matmul_t(array, matrix).astype(BF)


def attend(queries, key_rows, value_rows):
    count = queries.shape[1] // HEAD
    outs = []
    logs = []
    for head in range(count):
        cut = slice(head * HEAD, (head + 1) * HEAD)
        scores = matmul_t(queries[:, cut], key_rows[:, cut])
        top = jnp.max(scores, -1, keepdims=True)
        log_total = top + jnp.log(jnp.sum(jnp.exp(scores - top), -1, keepdims=True))
        probability = jnp.exp(scores - log_total).astype(BF)
        outs.append(matmul(probability, value_rows[:, cut]))
        logs.append(log_total)
    return jnp.concatenate(outs, 1), jnp.concatenate(logs, 1)


def attend_back(queries, key_rows, value_rows, logs, mixed, grad_mixed):
    count = queries.shape[1] // HEAD
    grad_q, grad_k, grad_v = [], [], []
    for head in range(count):
        cut = slice(head * HEAD, (head + 1) * HEAD)
        grad_head = grad_mixed[:, cut]
        delta = jnp.sum(grad_head.astype(F32) * mixed[:, cut], -1, keepdims=True)
        probability = jnp.exp(
            matmul_t(queries[:, cut], key_rows[:, cut]) - logs[:, head : head + 1]
        )
        grad_prob = matmul_t(grad_head, value_rows[:, cut])
        grad_scores = (probability * (grad_prob - delta)).astype(BF)
        grad_q.append(matmul(grad_scores, key_rows[:, cut]))
        grad_k.append(grad_matmul(grad_scores, queries[:, cut]))
        grad_v.append(grad_matmul(probability.astype(BF), grad_head))
    return (
        jnp.concatenate(grad_q, 1).astype(BF),
        jnp.concatenate(grad_k + grad_v, 1).astype(BF),
    )


def forward_layer(hidden, params, perm):
    triple, mixer, expand, shrink, vectors, head_bias, ffn_bias = params
    rows, width = hidden.shape
    half = width // 2
    _, core = place()
    low = hidden.astype(BF)
    project = matmul(low, triple)
    queries = ((project[:, :width] + head_bias[0]) * 0.125).astype(BF)
    key_rows = project[:, width : 2 * width].astype(BF)
    value_rows = (project[:, 2 * width :] + head_bias[1]).astype(BF)
    trio = (queries, key_rows, value_rows)
    mine = jnp.concatenate([half_of(member, core) for member in trio], 1)
    sent = jnp.concatenate([half_of(member, 1 - core) for member in trio], 1)
    pair = jnp.concatenate([mine, core_swap(sent)], 0)
    pair_queries = pair[:, :half]
    pair_rest = pair[:, half:]
    chips = chips_of()
    if chips > 4:
        keyed = gather_chips(pair_rest)
    else:
        keyed = jnp.concatenate(
            [pair_rest] + [chip_shift(pair_rest, step) for step in range(1, chips)], 0
        )
    mixed, logs = attend(pair_queries, keyed[:, :half], keyed[:, half:])
    mixed_low = mixed.astype(BF)
    other = core_swap(mixed_low[rows:])
    attended = move(join_cores(mixed_low[:rows], other, 1), perm)
    attn_out = matmul(attended, mixer) + vectors[2]
    residual_one = hidden + attn_out
    normed = layer_norm(residual_one, vectors[3], vectors[4])
    normed_low = normed.astype(BF)
    pre_act = matmul(normed_low, expand) + ffn_bias
    act_low = gelu_exact(pre_act).astype(BF)
    ffn_out = matmul(act_low, shrink) + vectors[9]
    residual_two = normed + ffn_out
    output = layer_norm(residual_two, vectors[10], vectors[11])
    squares = jnp.stack(
        [jnp.sum(hidden * hidden), jnp.sum(attn_out * attn_out), jnp.sum(ffn_out * ffn_out)]
    )
    saved = (
        low, pair_queries, keyed, logs, mixed, attended,
        residual_one, normed_low, pre_act, act_low, residual_two,
    )
    return output, saved, squares


def backward_layer(grad_output, params, saved, perm, perm_wide):
    triple, mixer, expand, shrink, vectors, head_bias, ffn_bias = params
    (
        low, pair_queries, keyed, logs, mixed, attended,
        residual_one, normed_low, pre_act, act_low, residual_two,
    ) = saved
    rows, width = low.shape
    half = width // 2
    chips = chips_of()
    _, core = place()
    acts = jnp.concatenate(
        [half_of(member, 1 - core) for member in (low, attended, normed_low, act_low)], 1
    )
    acts = core_swap(acts)
    low_pair = jnp.concatenate([half_of(low, core), acts[:, :half]], 0)
    attended_pair = jnp.concatenate([half_of(attended, core), acts[:, half : 2 * half]], 0)
    normed_pair = jnp.concatenate([half_of(normed_low, core), acts[:, 2 * half : 3 * half]], 0)
    act_pair = jnp.concatenate([half_of(act_low, core), acts[:, 3 * half :]], 0)

    _, pull_two = jax.vjp(layer_norm, residual_two, vectors[10], vectors[11])
    grad_two, grad_gain_two, grad_shift_two = pull_two(grad_output)
    grad_ffn = grad_two.astype(BF)
    grad_act = matmul_t(grad_ffn, shrink)
    _, pull_gelu = jax.vjp(gelu_exact, pre_act)
    grad_pre = pull_gelu(grad_act)[0].astype(BF)
    grad_normed = grad_two + matmul_t(grad_pre, expand)
    _, pull_one = jax.vjp(layer_norm, residual_one, vectors[3], vectors[4])
    grad_one, grad_gain_one, grad_shift_one = pull_one(grad_normed)
    grad_attn = grad_one.astype(BF)
    grad_attended = move_back(matmul_t(grad_attn, mixer).astype(BF), perm)

    grad_ffn_nat = move_back(grad_ffn, perm)
    grad_attn_nat = move_back(grad_attn, perm)
    quarter = grad_pre.reshape(rows, 2, -1, half).transpose(0, 2, 1, 3).reshape(-1, width)
    grad_pre_nat = move_back(quarter, perm_wide).reshape(rows, -1)
    gave = jnp.concatenate([grad_ffn_nat, grad_pre_nat], 1)
    pair_ffn = jnp.concatenate([gave, core_swap(gave)], 0)
    grad_shrink = grad_matmul(act_pair, pair_ffn[:, :width])
    grad_expand = grad_matmul(normed_pair, pair_ffn[:, width:])

    other = core_swap(half_of(grad_attended, 1 - core))
    pair_grad = jnp.concatenate([half_of(grad_attended, core), other], 0)
    grad_q, grad_kv = attend_back(
        pair_queries, keyed[:, :half], keyed[:, half:], logs, mixed, pair_grad
    )
    span = 2 * rows
    if chips > 4:
        grad_kv = scatter_chips(grad_kv)
    else:
        total = grad_kv[:span].astype(F32)
        for step in range(1, chips):
            total = total + chip_shift(
                grad_kv[step * span : (step + 1) * span], -step
            ).astype(F32)
        grad_kv = total
    mine = jnp.concatenate([grad_q * 0.125, grad_kv.astype(BF)], 1)
    theirs = core_swap(mine)
    theirs = jnp.concatenate([theirs[rows:], theirs[:rows]], 0)
    pair_project = jnp.concatenate(
        [
            join_cores(mine[:, i * half : (i + 1) * half], theirs[:, i * half : (i + 1) * half], 1)
            for i in range(3)
        ],
        1,
    )
    grad_hidden = grad_one + matmul_t(pair_project[:rows], triple)
    grad_triple = grad_matmul(low_pair, pair_project)
    attn_pair = jnp.concatenate([grad_attn_nat, core_swap(grad_attn_nat)], 0)
    grad_mixer = grad_matmul(attended_pair, attn_pair)

    def sums(array):
        return jnp.sum(array.astype(F32), 0)

    bias_rows = jnp.concatenate(
        [
            sums(pair_project[:rows, :width])[None],
            sums(pair_project[:rows, 2 * width :])[None],
            sums(grad_pre_nat).reshape(-1, width),
        ],
        0,
    )
    count = width // (2 * lax.axis_size("dp") * chips)
    bias_rows = (
        bias_rows.reshape(bias_rows.shape[0], -1, 2, count)
        .transpose(0, 2, 1, 3)
        .reshape(bias_rows.shape)
    )
    grad_vector = jnp.concatenate(
        [
            bias_rows[:2],
            sums(grad_attn)[None],
            grad_gain_one[None],
            grad_shift_one[None],
            bias_rows[2:],
            sums(grad_ffn)[None],
            grad_gain_two[None],
            grad_shift_two[None],
        ],
        0,
    )
    grad_vector = half_of(grad_vector, core) + core_swap(half_of(grad_vector, 1 - core))
    high = grad_vector.astype(BF)
    rest = (grad_vector - high.astype(F32)).astype(BF)
    extra = jnp.concatenate([high, rest], 0).T
    extra = jnp.pad(extra, ((0, 0), (0, LANES - extra.shape[1])))
    attn_terms = jnp.concatenate([grad_triple.astype(BF), grad_mixer.astype(BF), extra], 1)
    return grad_hidden, attn_terms, grad_expand.astype(BF), grad_shrink.astype(BF)


def total_of(value):
    for axis in ("seq", "dp"):
        size = lax.axis_size(axis)
        step = 1
        while step < size:
            value = value + lax.ppermute(value, axis, [(i, i ^ step) for i in range(size)])
            step *= 2
    return value


def per_device(
    hidden_input,
    triple_weight,
    mixer_weight,
    expand_weight,
    shrink_weight,
    vector_params,
    output_grad,
):
    _, count, width = hidden_input.shape
    share = triple_weight.shape[1]
    wide_share = shrink_weight.shape[1]
    wide = expand_weight.shape[2]
    groups = wide // width
    perm = swap_matrix(width, share)
    perm_wide = swap_matrix(width, wide_share)

    mixer_moved = move(mixer_weight.reshape(-1, width), perm).reshape(mixer_weight.shape)
    shrink_moved = move(shrink_weight.reshape(-1, width), perm).reshape(shrink_weight.shape)
    expand_moved = move(expand_weight.reshape(-1, width), perm_wide)
    expand_moved = (
        expand_moved.reshape(LAYERS * share, groups, 2, width // 2)
        .transpose(0, 2, 1, 3)
        .reshape(expand_weight.shape)
    )
    vector_columns = vector_params.reshape(LAYERS * VECS, share).T
    vector_columns = jnp.pad(vector_columns, ((0, 0), (0, LANES - LAYERS * VECS)))
    packs = []
    for layer in range(LAYERS):
        attn = [triple_weight[layer], mixer_moved[layer]]
        if layer == 0:
            attn.append(vector_columns)
        packs.append(
            (
                gather_weight(jnp.concatenate(attn, 1)),
                gather_weight(expand_moved[layer]),
                gather_weight(shrink_moved[layer]),
            )
        )
    vectors = packs[0][0][:, 4 * width : 4 * width + LAYERS * VECS].T
    natural = move_back(vectors, perm)
    params = []
    for layer in range(LAYERS):
        rows = vectors[layer * VECS : (layer + 1) * VECS].astype(F32)
        plain = natural[layer * VECS : (layer + 1) * VECS]
        ffn_bias = (
            move(plain[5 : 5 + groups], perm_wide)
            .reshape(groups, 2, width // 2)
            .transpose(1, 0, 2)
            .reshape(1, wide)
        ).astype(F32)
        attn, expand, shrink = packs[layer]
        params.append(
            (
                attn[:, : 3 * width],
                attn[:, 3 * width : 4 * width],
                expand,
                shrink,
                rows,
                plain[:2].astype(F32),
                ffn_bias,
            )
        )

    hidden = matmul(hidden_input[0], perm)
    kept = []
    collected = []
    for layer in range(LAYERS):
        hidden, saved, squares = forward_layer(hidden, params[layer], perm)
        kept.append(saved)
        collected.append(squares)
    elements = count * width * lax.axis_size("dp") * lax.axis_size("seq")
    root_squares = jnp.sqrt(total_of(jnp.stack(collected)) / elements)
    hidden_output = move_back(hidden.astype(BF), perm)

    grad = matmul(output_grad[0], perm)
    terms = [None] * LAYERS
    for layer in reversed(range(LAYERS)):
        grad, attn, expand, shrink = backward_layer(
            grad, params[layer], kept[layer], perm, perm_wide
        )
        terms[layer] = (scatter_grad(attn), scatter_grad(expand), scatter_grad(shrink))
    input_grad = move_back(grad.astype(BF), perm)
    vector_grad = jnp.stack(
        [
            (
                terms[layer][0][:, 4 * width : 4 * width + VECS]
                + terms[layer][0][:, 4 * width + VECS : 4 * width + 2 * VECS]
            ).T
            for layer in range(LAYERS)
        ]
    )
    return (
        hidden_output[None],
        input_grad[None],
        jnp.stack([terms[layer][0][:, : 3 * width] for layer in range(LAYERS)]),
        jnp.stack([terms[layer][0][:, 3 * width : 4 * width] for layer in range(LAYERS)]),
        jnp.stack([terms[layer][1] for layer in range(LAYERS)]),
        jnp.stack([terms[layer][2] for layer in range(LAYERS)]),
        vector_grad,
        root_squares,
    )


def solution(mesh):
    return jax.shard_map(
        per_device,
        mesh=mesh,
        in_specs=(
            P("dp", "seq", None),
            P(None, ("dp", "seq"), None),
            P(None, ("dp", "seq"), None),
            P(None, ("dp", "seq"), None),
            P(None, ("dp", "seq"), None),
            P(None, None, ("dp", "seq")),
            P("dp", "seq", None),
        ),
        out_specs=(
            P("dp", "seq", None),
            P("dp", "seq", None),
            P(None, ("dp", "seq"), None),
            P(None, ("dp", "seq"), None),
            P(None, ("dp", "seq"), None),
            P(None, ("dp", "seq"), None),
            P(None, None, ("dp", "seq")),
            P(),
        ),
        check_vma=False,
    )
```

```python
import functools
import math

import jax
import jax.numpy as jnp
import numpy as np
from jax import lax
from jax.experimental import pallas as pl
from jax.experimental.pallas import tpu as pltpu
from jax.sharding import PartitionSpec as P

HEADS = 12
HEAD = 64
LAYERS = 2
VECS = 12
LANES = 128

EPSILON = 1e-12
ROOT_HALF = 2.0 ** -0.5
ROOT_TAU = (2.0 * math.pi) ** -0.5

BF = jnp.bfloat16
F32 = jnp.float32


def layer_norm(residual, gain_row, shift_row):
    center = residual - jnp.mean(residual, -1, keepdims=True)
    spread = jnp.mean(center * center, -1, keepdims=True)
    return center * lax.rsqrt(spread + EPSILON) * gain_row + shift_row


def gelu_exact(values):
    return jax.nn.gelu(values, approximate=False)


def matmul(left, right):
    return jnp.dot(left, right, preferred_element_type=F32)


def matmul_t(left, right):
    return lax.dot_general(left, right, (((1,), (1,)), ((), ())), preferred_element_type=F32)


def grad_matmul(left, right):
    return lax.dot_general(left, right, (((0,), (0,)), ((), ())), preferred_element_type=F32)


def chips_of():
    return lax.axis_size("seq") // 2


def core_swap(array):
    size = lax.axis_size("seq")
    return lax.ppermute(array, "seq", [(i, i ^ 1) for i in range(size)])


def chip_shift(array, step):
    size = lax.axis_size("seq")
    chips = size // 2
    pairs = [(i, ((i // 2 + step) % chips) * 2 + i % 2) for i in range(size)]
    return lax.ppermute(array, "seq", pairs)


def core_groups():
    size = lax.axis_size("seq")
    return [list(range(0, size, 2)), list(range(1, size, 2))]


def place():
    spot = lax.axis_index("seq")
    return spot // 2, spot % 2


def gather_chips(array):
    chips = chips_of()
    if chips > 4:
        return lax.all_gather(
            array, "seq", axis=0, tiled=True, axis_index_groups=core_groups()
        )
    chip, _ = place()
    rows = array.shape[0]
    whole = jnp.zeros((chips * rows, array.shape[1]), array.dtype)
    for step in range(chips):
        part = array if step == 0 else chip_shift(array, step)
        whole = lax.dynamic_update_slice(whole, part, (((chip - step) % chips) * rows, 0))
    return whole


def gather_weight(array):
    own = lax.all_gather(gather_chips(array), "dp", axis=0, tiled=True)
    return join_cores(own, core_swap(own), 0)


def join_cores(own, other, axis):
    _, core = place()
    return jnp.where(
        core == 0,
        jnp.concatenate([own, other], axis),
        jnp.concatenate([other, own], axis),
    )


def scatter_chips(array):
    chips = chips_of()
    if chips > 4:
        return lax.psum_scatter(
            array, "seq", scatter_dimension=0, tiled=True, axis_index_groups=core_groups()
        ).astype(F32)
    chip, _ = place()
    rows = array.shape[0] // chips
    total = None
    for step in range(chips):
        part = lax.dynamic_slice(
            array, (((chip + step) % chips) * rows, 0), (rows, array.shape[1])
        )
        if step > 0:
            part = chip_shift(part, step)
        total = part.astype(F32) if total is None else total + part.astype(F32)
    return total


def scatter_grad(array):
    part = lax.psum_scatter(array.astype(BF), "dp", scatter_dimension=0, tiled=True)
    return scatter_chips(part)


def half_of(array, index):
    width = array.shape[1] // 2
    return lax.dynamic_slice(array, (0, index * width), (array.shape[0], width))


def one_hot(goal):
    return jnp.asarray(np.asarray(goal[:, None] == np.arange(goal.size)[None], np.float32), BF)


def swap_matrix(width, block):
    spot = np.arange(width)
    return one_hot(
        ((spot // block) % 2) * (width // 2) + (spot // (2 * block)) * block + spot % block
    )


def move(array, matrix):
    return jnp.dot(array, matrix, preferred_element_type=F32).astype(BF)


def move_back(array, matrix):
    return matmul_t(array, matrix).astype(BF)


def attend(queries, key_rows, value_rows):
    count = queries.shape[1] // HEAD
    outs = []
    logs = []
    for head in range(count):
        cut = slice(head * HEAD, (head + 1) * HEAD)
        scores = matmul_t(queries[:, cut], key_rows[:, cut])
        top = jnp.max(scores, -1, keepdims=True)
        log_total = top + jnp.log(jnp.sum(jnp.exp(scores - top), -1, keepdims=True))
        probability = jnp.exp(scores - log_total).astype(BF)
        outs.append(matmul(probability, value_rows[:, cut]))
        logs.append(log_total)
    return jnp.concatenate(outs, 1), jnp.concatenate(logs, 1)


def attend_back(queries, key_rows, value_rows, logs, mixed, grad_mixed):
    count = queries.shape[1] // HEAD
    grad_q, grad_k, grad_v = [], [], []
    for head in range(count):
        cut = slice(head * HEAD, (head + 1) * HEAD)
        grad_head = grad_mixed[:, cut]
        delta = jnp.sum(grad_head.astype(F32) * mixed[:, cut], -1, keepdims=True)
        probability = jnp.exp(
            matmul_t(queries[:, cut], key_rows[:, cut]) - logs[:, head : head + 1]
        )
        grad_prob = matmul_t(grad_head, value_rows[:, cut])
        grad_scores = (probability * (grad_prob - delta)).astype(BF)
        grad_q.append(matmul(grad_scores, key_rows[:, cut]))
        grad_k.append(grad_matmul(grad_scores, queries[:, cut]))
        grad_v.append(grad_matmul(probability.astype(BF), grad_head))
    return (
        jnp.concatenate(grad_q, 1).astype(BF),
        jnp.concatenate(grad_k + grad_v, 1).astype(BF),
    )


def forward_layer(hidden, params, perm):
    triple, mixer, expand, shrink, vectors, head_bias, ffn_bias = params
    rows, width = hidden.shape
    half = width // 2
    _, core = place()
    low = hidden.astype(BF)
    project = matmul(low, triple)
    queries = ((project[:, :width] + head_bias[0]) * 0.125).astype(BF)
    key_rows = project[:, width : 2 * width].astype(BF)
    value_rows = (project[:, 2 * width :] + head_bias[1]).astype(BF)
    trio = (queries, key_rows, value_rows)
    mine = jnp.concatenate([half_of(member, core) for member in trio], 1)
    sent = jnp.concatenate([half_of(member, 1 - core) for member in trio], 1)
    pair = jnp.concatenate([mine, core_swap(sent)], 0)
    pair_queries = pair[:, :half]
    pair_rest = pair[:, half:]
    chips = chips_of()
    if chips > 4:
        keyed = gather_chips(pair_rest)
    else:
        keyed = jnp.concatenate(
            [pair_rest] + [chip_shift(pair_rest, step) for step in range(1, chips)], 0
        )
    mixed, logs = attend(pair_queries, keyed[:, :half], keyed[:, half:])
    mixed_low = mixed.astype(BF)
    other = core_swap(mixed_low[rows:])
    attended = move(join_cores(mixed_low[:rows], other, 1), perm)
    attn_out = matmul(attended, mixer) + vectors[2]
    residual_one = hidden + attn_out
    normed = layer_norm(residual_one, vectors[3], vectors[4])
    normed_low = normed.astype(BF)
    pre_act = matmul(normed_low, expand) + ffn_bias
    act_low = gelu_exact(pre_act).astype(BF)
    ffn_out = matmul(act_low, shrink) + vectors[9]
    residual_two = normed + ffn_out
    output = layer_norm(residual_two, vectors[10], vectors[11])
    squares = jnp.stack(
        [jnp.sum(hidden * hidden), jnp.sum(attn_out * attn_out), jnp.sum(ffn_out * ffn_out)]
    )
    saved = (
        low, pair_queries, keyed, logs, mixed, attended,
        residual_one, normed_low, pre_act, act_low, residual_two,
    )
    return output, saved, squares


def backward_layer(grad_output, params, saved, perm, perm_wide):
    triple, mixer, expand, shrink, vectors, head_bias, ffn_bias = params
    (
        low, pair_queries, keyed, logs, mixed, attended,
        residual_one, normed_low, pre_act, act_low, residual_two,
    ) = saved
    rows, width = low.shape
    half = width // 2
    chips = chips_of()
    _, core = place()
    acts = jnp.concatenate(
        [half_of(member, 1 - core) for member in (low, attended, normed_low, act_low)], 1
    )
    acts = core_swap(acts)
    low_pair = jnp.concatenate([half_of(low, core), acts[:, :half]], 0)
    attended_pair = jnp.concatenate([half_of(attended, core), acts[:, half : 2 * half]], 0)
    normed_pair = jnp.concatenate([half_of(normed_low, core), acts[:, 2 * half : 3 * half]], 0)
    act_pair = jnp.concatenate([half_of(act_low, core), acts[:, 3 * half :]], 0)

    _, pull_two = jax.vjp(layer_norm, residual_two, vectors[10], vectors[11])
    grad_two, grad_gain_two, grad_shift_two = pull_two(grad_output)
    grad_ffn = grad_two.astype(BF)
    grad_act = matmul_t(grad_ffn, shrink)
    _, pull_gelu = jax.vjp(gelu_exact, pre_act)
    grad_pre = pull_gelu(grad_act)[0].astype(BF)
    grad_normed = grad_two + matmul_t(grad_pre, expand)
    _, pull_one = jax.vjp(layer_norm, residual_one, vectors[3], vectors[4])
    grad_one, grad_gain_one, grad_shift_one = pull_one(grad_normed)
    grad_attn = grad_one.astype(BF)
    grad_attended = move_back(matmul_t(grad_attn, mixer).astype(BF), perm)

    grad_ffn_nat = move_back(grad_ffn, perm)
    grad_attn_nat = move_back(grad_attn, perm)
    quarter = grad_pre.reshape(rows, 2, -1, half).transpose(0, 2, 1, 3).reshape(-1, width)
    grad_pre_nat = move_back(quarter, perm_wide).reshape(rows, -1)
    gave = jnp.concatenate([grad_ffn_nat, grad_pre_nat], 1)
    pair_ffn = jnp.concatenate([gave, core_swap(gave)], 0)
    grad_shrink = grad_matmul(act_pair, pair_ffn[:, :width])
    grad_expand = grad_matmul(normed_pair, pair_ffn[:, width:])

    other = core_swap(half_of(grad_attended, 1 - core))
    pair_grad = jnp.concatenate([half_of(grad_attended, core), other], 0)
    grad_q, grad_kv = attend_back(
        pair_queries, keyed[:, :half], keyed[:, half:], logs, mixed, pair_grad
    )
    span = 2 * rows
    if chips > 4:
        grad_kv = scatter_chips(grad_kv)
    else:
        total = grad_kv[:span].astype(F32)
        for step in range(1, chips):
            total = total + chip_shift(
                grad_kv[step * span : (step + 1) * span], -step
            ).astype(F32)
        grad_kv = total
    mine = jnp.concatenate([grad_q * 0.125, grad_kv.astype(BF)], 1)
    theirs = core_swap(mine)
    theirs = jnp.concatenate([theirs[rows:], theirs[:rows]], 0)
    pair_project = jnp.concatenate(
        [
            join_cores(mine[:, i * half : (i + 1) * half], theirs[:, i * half : (i + 1) * half], 1)
            for i in range(3)
        ],
        1,
    )
    grad_hidden = grad_one + matmul_t(pair_project[:rows], triple)
    grad_triple = grad_matmul(low_pair, pair_project)
    attn_pair = jnp.concatenate([grad_attn_nat, core_swap(grad_attn_nat)], 0)
    grad_mixer = grad_matmul(attended_pair, attn_pair)

    def sums(array):
        return jnp.sum(array.astype(F32), 0)

    bias_rows = jnp.concatenate(
        [
            sums(pair_project[:rows, :width])[None],
            sums(pair_project[:rows, 2 * width :])[None],
            sums(grad_pre_nat).reshape(-1, width),
        ],
        0,
    )
    count = width // (2 * lax.axis_size("dp") * chips)
    bias_rows = (
        bias_rows.reshape(bias_rows.shape[0], -1, 2, count)
        .transpose(0, 2, 1, 3)
        .reshape(bias_rows.shape)
    )
    grad_vector = jnp.concatenate(
        [
            bias_rows[:2],
            sums(grad_attn)[None],
            grad_gain_one[None],
            grad_shift_one[None],
            bias_rows[2:],
            sums(grad_ffn)[None],
            grad_gain_two[None],
            grad_shift_two[None],
        ],
        0,
    )
    grad_vector = half_of(grad_vector, core) + core_swap(half_of(grad_vector, 1 - core))
    high = grad_vector.astype(BF)
    rest = (grad_vector - high.astype(F32)).astype(BF)
    extra = jnp.concatenate([high, rest], 0).T
    extra = jnp.pad(extra, ((0, 0), (0, LANES - extra.shape[1])))
    attn_terms = jnp.concatenate([grad_triple.astype(BF), grad_mixer.astype(BF), extra], 1)
    return grad_hidden, attn_terms, grad_expand.astype(BF), grad_shrink.astype(BF)


def total_of(value):
    for axis in ("seq", "dp"):
        size = lax.axis_size(axis)
        step = 1
        while step < size:
            value = value + lax.ppermute(value, axis, [(i, i ^ step) for i in range(size)])
            step *= 2
    return value


def plain_device(
    hidden_input,
    triple_weight,
    mixer_weight,
    expand_weight,
    shrink_weight,
    vector_params,
    output_grad,
):
    _, count, width = hidden_input.shape
    share = triple_weight.shape[1]
    wide_share = shrink_weight.shape[1]
    wide = expand_weight.shape[2]
    groups = wide // width
    perm = swap_matrix(width, share)
    perm_wide = swap_matrix(width, wide_share)

    mixer_moved = move(mixer_weight.reshape(-1, width), perm).reshape(mixer_weight.shape)
    shrink_moved = move(shrink_weight.reshape(-1, width), perm).reshape(shrink_weight.shape)
    expand_moved = move(expand_weight.reshape(-1, width), perm_wide)
    expand_moved = (
        expand_moved.reshape(LAYERS * share, groups, 2, width // 2)
        .transpose(0, 2, 1, 3)
        .reshape(expand_weight.shape)
    )
    vector_columns = vector_params.reshape(LAYERS * VECS, share).T
    vector_columns = jnp.pad(vector_columns, ((0, 0), (0, LANES - LAYERS * VECS)))
    packs = []
    for layer in range(LAYERS):
        attn = [triple_weight[layer], mixer_moved[layer]]
        if layer == 0:
            attn.append(vector_columns)
        packs.append(
            (
                gather_weight(jnp.concatenate(attn, 1)),
                gather_weight(expand_moved[layer]),
                gather_weight(shrink_moved[layer]),
            )
        )
    vectors = packs[0][0][:, 4 * width : 4 * width + LAYERS * VECS].T
    natural = move_back(vectors, perm)
    params = []
    for layer in range(LAYERS):
        rows = vectors[layer * VECS : (layer + 1) * VECS].astype(F32)
        plain = natural[layer * VECS : (layer + 1) * VECS]
        ffn_bias = (
            move(plain[5 : 5 + groups], perm_wide)
            .reshape(groups, 2, width // 2)
            .transpose(1, 0, 2)
            .reshape(1, wide)
        ).astype(F32)
        attn, expand, shrink = packs[layer]
        params.append(
            (
                attn[:, : 3 * width],
                attn[:, 3 * width : 4 * width],
                expand,
                shrink,
                rows,
                plain[:2].astype(F32),
                ffn_bias,
            )
        )

    hidden = matmul(hidden_input[0], perm)
    kept = []
    collected = []
    for layer in range(LAYERS):
        hidden, saved, squares = forward_layer(hidden, params[layer], perm)
        kept.append(saved)
        collected.append(squares)
    elements = count * width * lax.axis_size("dp") * lax.axis_size("seq")
    root_squares = jnp.sqrt(total_of(jnp.stack(collected)) / elements)
    hidden_output = move_back(hidden.astype(BF), perm)

    grad = matmul(output_grad[0], perm)
    terms = [None] * LAYERS
    for layer in reversed(range(LAYERS)):
        grad, attn, expand, shrink = backward_layer(
            grad, params[layer], kept[layer], perm, perm_wide
        )
        terms[layer] = (scatter_grad(attn), scatter_grad(expand), scatter_grad(shrink))
    input_grad = move_back(grad.astype(BF), perm)
    vector_grad = jnp.stack(
        [
            (
                terms[layer][0][:, 4 * width : 4 * width + VECS]
                + terms[layer][0][:, 4 * width + VECS : 4 * width + 2 * VECS]
            ).T
            for layer in range(LAYERS)
        ]
    )
    return (
        hidden_output[None],
        input_grad[None],
        jnp.stack([terms[layer][0][:, : 3 * width] for layer in range(LAYERS)]),
        jnp.stack([terms[layer][0][:, 3 * width : 4 * width] for layer in range(LAYERS)]),
        jnp.stack([terms[layer][1] for layer in range(LAYERS)]),
        jnp.stack([terms[layer][2] for layer in range(LAYERS)]),
        vector_grad,
        root_squares,
    )


ANY = pl.BlockSpec(memory_space=pl.ANY)
VMEM = pl.BlockSpec(memory_space=pltpu.VMEM)
VMEM_BYTES = 56 * 1024 * 1024
HINT = 4
SIDE_HINT = 40
SIDE = ("feed_terms", "attend_terms", "fold", "split", "input_back")


def shape(dims, kind):
    return jax.ShapeDtypeStruct(dims, kind)


def run(kernel, name, outs, placed, streamed=(), scratch=(), flops=0):
    hint = SIDE_HINT if name in SIDE else HINT
    size = sum(
        math.prod(member.shape) * member.dtype.itemsize
        for member in [*outs, *placed, *streamed]
    )
    return pl.pallas_call(
        kernel,
        name=name,
        out_shape=list(outs),
        in_specs=[VMEM] * len(placed) + [ANY] * len(streamed),
        out_specs=[VMEM] * len(outs),
        scratch_shapes=list(scratch),
        compiler_params=pltpu.CompilerParams(vmem_limit_bytes=VMEM_BYTES),
        cost_estimate=pl.CostEstimate(
            flops=int(flops * hint), bytes_accessed=int(size * hint), transcendentals=0
        ),
    )(*placed, *streamed)


def spot_in():
    index = lax.axis_index("seq")
    return index // 2, index % 2


def fetch_left(pieces, target, sems, columns, goal):
    _, core = spot_in()
    _, high = dp_place()
    rows = pieces[0].shape[0]
    copies = []
    for index, piece in enumerate(pieces):
        part = core if index < 2 else 1 - core
        side = high if index % 2 == 0 else 1 - high
        start = pl.multiple_of((part * 2 + side) * rows, 16)
        copy = pltpu.make_async_copy(
            piece.at[:, columns], target.at[pl.ds(start, rows), goal], sems.at[index]
        )
        copy.start()
        copies.append(copy)
    return copies


def fetch_whole(pieces, target, sems, columns, goal):
    _, core = spot_in()
    rows = pieces[0].shape[0]
    copies = []
    for index, piece in enumerate(pieces):
        part = core if index == 0 else 1 - core
        start = pl.multiple_of(part * rows, 16)
        copy = pltpu.make_async_copy(
            piece.at[:, columns], target.at[pl.ds(start, rows), goal], sems.at[index]
        )
        copy.start()
        copies.append(copy)
    return copies


def fetch_right(pieces, target, sems, columns, goal):
    _, core = spot_in()
    bit, _ = dp_place()
    rows = pieces[0].shape[0] // 2
    copies = []
    for index, piece in enumerate(pieces):
        part = core if index < 2 else 1 - core
        side = bit if index % 2 == 0 else 1 - bit
        for row in range(2):
            start = pl.multiple_of((part * 4 + row * 2 + side) * rows, 16)
            copy = pltpu.make_async_copy(
                piece.at[row * rows : (row + 1) * rows, columns],
                target.at[pl.ds(start, rows), goal],
                sems.at[2 * index + row],
            )
            copy.start()
            copies.append(copy)
    return copies


def wait_all(copies):
    for copy in copies:
        copy.wait()


def half_at(ref, part):
    half = ref.shape[1] // 2
    return ref[:, pl.ds(pl.multiple_of(part * half, LANES), half)]


def column_sum(values):
    return jnp.sum(values, 0, keepdims=True)


def fetch_project(pieces, weight, left_sems, right_sems, width):
    first, last = slice(0, 2 * width), slice(2 * width, 3 * width)
    copies = fetch_left(pieces[:4], weight, left_sems, first, first)
    return copies + fetch_right(pieces[4:], weight, right_sems, slice(0, width), last)


def project_kernel(first, chips, source, perm, bias, *rest):
    pieces, low_out, rest = rest[:8], rest[8], rest[9:]
    outs, (weight, stage, left_sems, right_sems) = rest[:chips], rest[chips:]
    chip, _ = spot_in()
    width = perm.shape[0]
    copies = fetch_project(pieces, weight, left_sems, right_sems, width)
    if first:
        low = matmul(source[...], perm[...]).astype(BF)
    else:
        low = source[...].astype(BF)
    low_out[...] = low
    wait_all(copies)
    group = width // chips
    for section in range(3):
        part = matmul(low, weight[:, section * width : (section + 1) * width])
        if section == 0:
            part = (part + bias[0:1]) * 0.125
        if section == 2:
            part = part + bias[1:2]
        part = part.astype(BF)
        for index in range(chips):
            stage[index, :, section * group : (section + 1) * group] = part[
                :, index * group : (index + 1) * group
            ]
    for step in range(chips):
        outs[step][...] = stage[lax.rem(chip + step, chips)]


def project_fast(first, chips, source, perm, bias, pieces):
    rows, width = source.shape
    group = 3 * width // chips
    out = run(
        functools.partial(project_kernel, first, chips),
        "project",
        [shape((rows, width), BF)] + [shape((rows, group), BF)] * chips,
        [source, perm, bias],
        pieces,
        [
            pltpu.VMEM((width, 3 * width), BF),
            pltpu.VMEM((chips, rows, group), BF),
            pltpu.SemaphoreType.DMA((4,)),
            pltpu.SemaphoreType.DMA((8,)),
        ],
        flops=6 * rows * width * width,
    )
    return out[0], out[1:]


def fill_heads(blocks, others, group, queries, keys, values):
    rows = blocks[0].shape[0]
    for index, block in enumerate(blocks):
        cut = slice(index * rows, (index + 1) * rows)
        queries[cut, :] = block[:, :group]
        keys[cut, :] = block[:, group : 2 * group]
        values[cut, :] = block[:, 2 * group :]
    base = len(blocks) * rows
    for index, block in enumerate(others):
        cut = slice(base + index * rows, base + (index + 1) * rows)
        keys[cut, :] = block[:, group : 2 * group]
        values[cut, :] = block[:, 2 * group :]


def chunks_of(total):
    size = min(total, 256)
    return [slice(start, start + size) for start in range(0, total, size)]


def attend_kernel(chips, *refs):
    blocks, others = refs[:chips], refs[chips : 2 * chips]
    mixed, logs = refs[2 * chips : 2 * chips + 2]
    outs = refs[2 * chips + 2 : 3 * chips + 2]
    queries, keys, values = refs[3 * chips + 2 :]
    rows = blocks[0].shape[0]
    group = queries.shape[1]
    fill_heads(blocks, others, group, queries, keys, values)
    for head in range(group // HEAD):
        cut = slice(head * HEAD, (head + 1) * HEAD)
        key_head = keys[:, cut]
        value_head = values[:, cut]
        for part in chunks_of(chips * rows):
            scores = matmul_t(queries[part, cut], key_head)
            top = jnp.max(scores, -1, keepdims=True)
            power = jnp.exp(scores - top)
            total = jnp.sum(power, -1, keepdims=True)
            mixed[part, cut] = matmul(power.astype(BF), value_head) * (1.0 / total)
            logs[part, head : head + 1] = top + jnp.log(total)
    for index in range(chips):
        outs[index][...] = mixed[index * rows : (index + 1) * rows, :].astype(BF)


def attend_fast(chips, blocks, others):
    rows, wide = blocks[0].shape
    group = wide // 3
    span = chips * rows
    out = run(
        functools.partial(attend_kernel, chips),
        "attend",
        [shape((span, group), F32), shape((span, LANES), F32)]
        + [shape((rows, group), BF)] * chips,
        [*blocks, *others],
        (),
        [
            pltpu.VMEM((span, group), BF),
            pltpu.VMEM((2 * span, group), BF),
            pltpu.VMEM((2 * span, group), BF),
        ],
        flops=8 * span * span * group,
    )
    return out[0], out[1], out[2:]


def norm_in(residual):
    center = residual - jnp.mean(residual, -1, keepdims=True)
    spread = jnp.mean(center * center, -1, keepdims=True)
    scale = lax.rsqrt(spread + EPSILON)
    return center * scale, scale


def shrink_cut(index, wide, width):
    count = wide // width
    core, block = index // count, index % count
    half = width // 2
    return (
        slice(core * half, (core + 1) * half),
        slice(block * width, (block + 1) * width),
    )


def fetch_feed(weights, mixer, expand, shrink, sems):
    width, wide = expand.shape
    every, full = slice(0, width), slice(0, wide)
    mixer_copies = fetch_right(weights[:4], mixer, sems[0], slice(width, 2 * width), every)
    if len(weights) == 6:
        return (
            mixer_copies,
            fetch_whole(weights[4:], expand, sems[1], full, full),
            fetch_whole(weights[4:], shrink, sems[2], slice(wide, 2 * wide), full),
        )
    return (
        mixer_copies,
        fetch_left(weights[4:8], expand, sems[1], full, full),
        fetch_right(weights[8:], shrink, sems[2], full, full),
    )


def feed_kernel(chips, many, hidden, low, perm, rows_in, wide_bias, *refs):
    pieces, refs = refs[:chips], refs[chips:]
    weights, refs = refs[:many], refs[many:]
    (out, attended, normed_low, pre_out, act_out, hat_one, scale_one, hat_two, scale_two,
     sent, squares) = refs[:11]
    stage, mixer, expand, shrink, *sems = refs[11:]
    chip, core = spot_in()
    width = perm.shape[0]
    wide = expand.shape[1]
    group = width // chips
    mixer_copies, expand_copies, shrink_copies = fetch_feed(
        weights, mixer, expand, shrink, sems
    )
    for step in range(chips):
        stage[lax.rem(chip + step, chips)] = pieces[step][...]
    moved = matmul(stage[0], perm[:group, :])
    for index in range(1, chips):
        moved += matmul(stage[index], perm[index * group : (index + 1) * group, :])
    moved = moved.astype(BF)
    attended[...] = moved
    wait_all(mixer_copies)
    attn_out = matmul(moved, mixer[...]) + rows_in[2:3]
    start = hidden[...].astype(F32)
    hat, scale = norm_in(start + attn_out)
    hat_one[...] = hat
    scale_one[...] = jnp.broadcast_to(scale, scale_one.shape)
    normed = hat * rows_in[3:4] + rows_in[4:5]
    normed_b = normed.astype(BF)
    normed_low[...] = normed_b
    squares[...] = jnp.zeros_like(squares)
    squares[0:1, :] = column_sum(start * start)
    squares[1:2, :] = column_sum(attn_out * attn_out)
    wait_all(expand_copies)
    wait_all(shrink_copies)
    half = width // 2
    total = None
    for index in range(wide // width):
        cut = slice(index * width, (index + 1) * width)
        pre = matmul(normed_b, expand[:, cut]) + wide_bias[:, cut]
        pre_out[:, cut] = pre
        act = (0.5 * pre * (1.0 + lax.erf(pre * ROOT_HALF))).astype(BF)
        act_out[:, cut] = act
        for side in range(2):
            rows, columns = shrink_cut(2 * index + side, wide, width)
            term = matmul(act[:, side * half : (side + 1) * half], shrink[rows, columns])
            total = term if total is None else total + term
    ffn_out = total + rows_in[9:10]
    squares[2:3, :] = column_sum(ffn_out * ffn_out)
    hat, scale = norm_in(normed + ffn_out)
    hat_two[...] = hat
    scale_two[...] = jnp.broadcast_to(scale, scale_two.shape)
    out[...] = hat * rows_in[10:11] + rows_in[11:12]
    for index, member in enumerate((low, attended, normed_low)):
        sent[:, index * half : (index + 1) * half] = half_at(member, 1 - core)
    sent[:, 3 * half :] = half_at(act_out, 1 - core)


def feed_fast(chips, hidden, low, perm, vectors, wide_bias, pieces, weights):
    rows, width = hidden.shape
    wide = wide_bias.shape[1]
    return run(
        functools.partial(feed_kernel, chips, len(weights)),
        "feed",
        [
            shape((rows, width), F32),
            shape((rows, width), BF),
            shape((rows, width), BF),
            shape((rows, wide), F32),
            shape((rows, wide), BF),
            shape((rows, width), F32),
            shape((rows, LANES), F32),
            shape((rows, width), F32),
            shape((rows, LANES), F32),
            shape((rows, (3 * width + wide) // 2), BF),
            shape((8, width), F32),
        ],
        [hidden, low, perm, vectors, wide_bias, *pieces],
        weights,
        [
            pltpu.VMEM((chips, rows, width // chips), BF),
            pltpu.VMEM((width, width), BF),
            pltpu.VMEM((width, wide), BF),
            pltpu.VMEM((width, wide), BF),
            pltpu.SemaphoreType.DMA((8,)),
            pltpu.SemaphoreType.DMA((4,)),
            pltpu.SemaphoreType.DMA((8,)),
        ],
        flops=4 * rows * width * (wide + width),
    )


def norm_back(grad, hat, scale):
    first = jnp.mean(grad, -1, keepdims=True)
    second = jnp.mean(grad * hat, -1, keepdims=True)
    return (grad - first - hat * second) * scale


def feed_back_kernel(
    first, chips, many, source, perm, perm_wide, vectors, hat_one, scale_one, hat_two, scale_two,
    pre_in, *refs
):
    weights, refs = refs[:many], refs[many:]
    grad_one_out, gave, attn_nat, sums = refs[:4]
    outs = refs[4 : 4 + chips]
    stage, grad_pre, mixer, expand, shrink, *sems = refs[4 + chips :]
    chip, _ = spot_in()
    width = perm.shape[0]
    wide = expand.shape[1]
    group = width // chips
    half = width // 2
    mixer_copies, expand_copies, shrink_copies = fetch_feed(
        weights, mixer, expand, shrink, sems
    )
    grad = matmul(source[...], perm[...]) if first else source[...]
    hat = hat_two[...]
    sums[...] = jnp.zeros_like(sums)
    sums[10:11, :] = column_sum(grad * hat)
    sums[11:12, :] = column_sum(grad)
    grad_two = norm_back(grad * vectors[10:11], hat, scale_two[:, 0:1])
    grad_ffn = grad_two.astype(BF)
    sums[9:10, :] = column_sum(grad_ffn.astype(F32))
    gave[:, :width] = matmul_t(grad_ffn, perm[...]).astype(BF)
    wait_all(shrink_copies)
    wait_all(expand_copies)
    grad_normed = grad_two
    for index in range(wide // width):
        cut = slice(index * width, (index + 1) * width)
        pre = pre_in[:, cut]
        slope = 0.5 * (1.0 + lax.erf(pre * ROOT_HALF)) + pre * (
            jnp.exp(-0.5 * pre * pre) * ROOT_TAU
        )
        sides = []
        for side in range(2):
            rows, columns = shrink_cut(2 * index + side, wide, width)
            sides.append(matmul_t(grad_ffn, shrink[rows, columns]))
        part = (jnp.concatenate(sides, 1) * slope).astype(BF)
        grad_pre[:, cut] = part
        grad_normed += matmul_t(part, expand[:, cut])
    groups = wide // width
    piece = half // groups
    for index in range(groups):
        joined = jnp.concatenate(
            [
                grad_pre[:, spot * half + index * piece : spot * half + (index + 1) * piece]
                for spot in range(2 * groups)
            ],
            1,
        )
        moved = matmul_t(joined, perm_wide[...])
        sums[5 + index : 6 + index, :] = column_sum(moved)
        gave[:, (index + 1) * width : (index + 2) * width] = moved.astype(BF)
    hat = hat_one[...]
    sums[3:4, :] = column_sum(grad_normed * hat)
    sums[4:5, :] = column_sum(grad_normed)
    grad_one = norm_back(grad_normed * vectors[3:4], hat, scale_one[:, 0:1])
    grad_one_out[...] = grad_one
    grad_attn = grad_one.astype(BF)
    sums[2:3, :] = column_sum(grad_attn.astype(F32))
    attn_nat[...] = matmul_t(grad_attn, perm[...]).astype(BF)
    wait_all(mixer_copies)
    grad_mixed = matmul_t(grad_attn, mixer[...]).astype(BF)
    for index in range(chips):
        stage[index] = matmul_t(
            grad_mixed, perm[index * group : (index + 1) * group, :]
        ).astype(BF)
    for step in range(chips):
        outs[step][...] = stage[lax.rem(chip + step, chips)]


def feed_back_fast(first, chips, source, perm, perm_wide, vectors, saved, weights):
    rows, width = source.shape
    wide = saved[-1].shape[1]
    out = run(
        functools.partial(feed_back_kernel, first, chips, len(weights)),
        "feed_back",
        [
            shape((rows, width), F32),
            shape((rows, width + wide), BF),
            shape((rows, width), BF),
            shape((16, width), F32),
        ]
        + [shape((rows, width // chips), BF)] * chips,
        [source, perm, perm_wide, vectors, *saved],
        weights,
        [
            pltpu.VMEM((chips, rows, width // chips), BF),
            pltpu.VMEM((rows, wide), BF),
            pltpu.VMEM((width, width), BF),
            pltpu.VMEM((width, wide), BF),
            pltpu.VMEM((width, wide), BF),
            pltpu.SemaphoreType.DMA((8,)),
            pltpu.SemaphoreType.DMA((4,)),
            pltpu.SemaphoreType.DMA((8,)),
        ],
        flops=4 * rows * width * (wide + 2 * width),
    )
    return out[0], out[1], out[2], out[3], out[4:]


def attend_back_kernel(chips, *refs):
    blocks, refs = refs[:chips], refs[chips:]
    others, refs = refs[:chips], refs[chips:]
    grads, refs = refs[:chips], refs[chips:]
    mixed, logs, grad_q, near, far, queries, keys, values, grad_in, key_sum, value_sum = refs
    rows = blocks[0].shape[0]
    group = queries.shape[1]
    span = chips * rows
    fill_heads(blocks, others, group, queries, keys, values)
    for index in range(chips):
        grad_in[index * rows : (index + 1) * rows, :] = grads[index][...]
    for head in range(group // HEAD):
        cut = slice(head * HEAD, (head + 1) * HEAD)
        key_head = keys[:, cut]
        value_head = values[:, cut]
        for place_in, part in enumerate(chunks_of(span)):
            query = queries[part, cut]
            grad = grad_in[part, cut]
            delta = jnp.sum(grad.astype(F32) * mixed[part, cut], -1, keepdims=True)
            probability = jnp.exp(matmul_t(query, key_head) - logs[part, head : head + 1])
            slope = matmul_t(grad, value_head) - delta
            grad_scores = (probability * slope).astype(BF)
            grad_q[part, cut] = (matmul(grad_scores, key_head) * 0.125).astype(BF)
            key_term = grad_matmul(grad_scores, query)
            value_term = grad_matmul(probability.astype(BF), grad)
            if place_in == 0:
                key_sum[:, cut] = key_term
                value_sum[:, cut] = value_term
            else:
                key_sum[:, cut] += key_term
                value_sum[:, cut] += value_term
    near[:, :group] = key_sum[:span, :]
    near[:, group:] = value_sum[:span, :]
    far[:, :group] = key_sum[span:, :].astype(BF)
    far[:, group:] = value_sum[span:, :].astype(BF)


def attend_back_fast(chips, blocks, others, grads, mixed, logs):
    rows, wide = blocks[0].shape
    group = wide // 3
    span = chips * rows
    return run(
        functools.partial(attend_back_kernel, chips),
        "attend_back",
        [
            shape((span, group), BF),
            shape((span, 2 * group), F32),
            shape((span, 2 * group), BF),
        ],
        [*blocks, *others, *grads, mixed, logs],
        (),
        [
            pltpu.VMEM((span, group), BF),
            pltpu.VMEM((2 * span, group), BF),
            pltpu.VMEM((2 * span, group), BF),
            pltpu.VMEM((span, group), BF),
            pltpu.VMEM((2 * span, group), F32),
            pltpu.VMEM((2 * span, group), F32),
        ],
        flops=20 * span * span * group,
    )


def combine_kernel(grad_q, near, far, *outs):
    rows, wide = outs[0].shape
    group = wide // 3
    for index, out in enumerate(outs):
        cut = slice(index * rows, (index + 1) * rows)
        out[:, :group] = grad_q[cut, :]
        out[:, group:] = (near[cut, :] + far[cut, :].astype(F32)).astype(BF)


def combine_fast(chips, grad_q, near, far):
    span, group = grad_q.shape
    return run(
        combine_kernel,
        "combine",
        [shape((span // chips, 3 * group), BF)] * chips,
        [grad_q, near, far],
    )


def exact_move(values, perm):
    high = values.astype(BF)
    rest = values - high.astype(F32)
    middle = rest.astype(BF)
    low = (rest - middle.astype(F32)).astype(BF)
    return matmul(high, perm) + matmul(middle, perm) + matmul(low, perm)


def collect(chips, stage, pieces, project):
    chip, _ = spot_in()
    width = project.shape[1] // 3
    group = width // chips
    for step in range(chips):
        stage[lax.rem(chip + step, chips)] = pieces[step][...]
    for section in range(3):
        cut = slice(section * group, (section + 1) * group)
        joined = jnp.concatenate([stage[index][:, cut] for index in range(chips)], 1)
        project[:, section * width : (section + 1) * width] = joined


def through_project(grad, project, weight):
    width = grad.shape[1]
    for section in range(3):
        cut = slice(section * width, (section + 1) * width)
        grad += matmul_t(project[:, cut], weight[:, cut])
    return grad


def project_back_kernel(chips, grad_one, perm, sums, *refs):
    pieces, refs = refs[:chips], refs[chips:]
    weights, refs = refs[:8], refs[8:]
    out, project, vector_out, stage, weight, left_sems, right_sems = refs
    copies = fetch_project(weights, weight, left_sems, right_sems, perm.shape[0])
    collect(chips, stage, pieces, project)
    wait_all(copies)
    out[...] = through_project(grad_one[...], project, weight)
    vector_rows(project, sums, perm, vector_out)


def collect_kernel(chips, perm, sums, *refs):
    pieces, refs = refs[:chips], refs[chips:]
    project, vector_out, stage = refs
    collect(chips, stage, pieces, project)
    vector_rows(project, sums, perm, vector_out)


def collect_fast(chips, perm, sums, pieces):
    rows, group = pieces[0].shape
    return run(
        functools.partial(collect_kernel, chips),
        "collect",
        [shape((rows, chips * group), BF), shape(sums.shape, F32)],
        [perm, sums, *pieces],
        (),
        [pltpu.VMEM((chips, rows, group), BF)],
    )


def input_back_kernel(grad_one, perm, project, *refs):
    weights, refs = refs[:8], refs[8:]
    out, weight, left_sems, right_sems = refs
    wait_all(fetch_project(weights, weight, left_sems, right_sems, perm.shape[0]))
    grad = through_project(grad_one[...], project, weight)
    out[...] = matmul_t(grad.astype(BF), perm[...]).astype(BF)


def input_back_fast(grad_one, perm, project, weights):
    rows, width = grad_one.shape
    return run(
        input_back_kernel,
        "input_back",
        [shape((rows, width), BF)],
        [grad_one, perm, project],
        weights,
        [
            pltpu.VMEM((width, 3 * width), BF),
            pltpu.SemaphoreType.DMA((4,)),
            pltpu.SemaphoreType.DMA((8,)),
        ],
        flops=6 * rows * width * width,
    )[0]


def vector_rows(project, sums, perm, vector_out):
    width = perm.shape[0]
    vector_out[...] = sums[...]
    vector_out[0:1, :] = column_sum(project[:, :width].astype(F32))
    vector_out[1:2, :] = column_sum(project[:, 2 * width :].astype(F32))
    moved = exact_move(vector_out[0:8, :], perm[...])
    vector_out[0:2, :] = moved[0:2, :]
    vector_out[5:8, :] = moved[5:8, :]
    moved = exact_move(vector_out[8:16, :], perm[...])
    vector_out[8:9, :] = moved[0:1, :]


def project_back_fast(chips, grad_one, perm, sums, pieces, weights):
    rows, width = grad_one.shape
    return run(
        functools.partial(project_back_kernel, chips),
        "project_back",
        [
            shape((rows, width), F32),
            shape((rows, 3 * width), BF),
            shape((16, width), F32),
        ],
        [grad_one, perm, sums, *pieces],
        weights,
        [
            pltpu.VMEM((chips, rows, 3 * width // chips), BF),
            pltpu.VMEM((width, 3 * width), BF),
            pltpu.SemaphoreType.DMA((4,)),
            pltpu.SemaphoreType.DMA((8,)),
        ],
        flops=6 * rows * width * width,
    )


def feed_terms_kernel(normed, act, gave, theirs, gave_theirs, out):
    _, core = spot_in()
    width = normed.shape[1]
    half = width // 2
    left = jnp.concatenate([half_at(normed, core), theirs[:, 2 * half : 3 * half]], 0)
    count = act.shape[1] // width
    for index in range(count):
        cut = slice(index * width, (index + 1) * width)
        far = slice((index + 1) * width, (index + 2) * width)
        right = jnp.concatenate([gave[:, far], gave_theirs[:, far]], 0)
        out[:, cut] = grad_matmul(left, right).astype(BF)
    left = jnp.concatenate([half_at(act, core), theirs[:, 3 * half :]], 0)
    right = jnp.concatenate([gave[:, :width], gave_theirs[:, :width]], 0)
    for index in range(count):
        cut = slice(index * half, (index + 1) * half)
        spot = slice((count + index) * width, (count + index + 1) * width)
        out[:, spot] = grad_matmul(left[:, cut], right).astype(BF)


def feed_terms_fast(normed, act, gave, theirs, gave_theirs):
    rows, width = normed.shape
    wide = act.shape[1]
    return run(
        feed_terms_kernel,
        "feed_terms",
        [shape((width // 2, 2 * wide), BF)],
        [normed, act, gave, theirs, gave_theirs],
        flops=4 * rows * width * wide,
    )[0]


def attend_terms_kernel(
    low, attended, project, attn_nat, vector, theirs, project_theirs, attn_theirs,
    vector_theirs, left_keep, left_sent, right_keep, right_sent
):
    _, core = spot_in()
    bit, high = dp_place()
    width = low.shape[1]
    half = width // 2
    block = half // 4

    def put_left(columns, value):
        value = value.astype(BF)
        for side in range(2):
            first = value[2 * side * block : (2 * side + 1) * block]
            second = value[(2 * side + 1) * block : (2 * side + 2) * block]
            rows = slice(side * block, (side + 1) * block)
            left_keep[rows, columns] = jnp.where(bit == 0, first, second)
            left_sent[rows, columns] = jnp.where(bit == 0, second, first)

    def put_right(columns, value):
        value = value.astype(BF)
        first, second = value[: 2 * block], value[2 * block :]
        right_keep[:, columns] = jnp.where(high == 0, first, second)
        right_sent[:, columns] = jnp.where(high == 0, second, first)

    left = jnp.concatenate([half_at(low, core), theirs[:, :half]], 0)
    for index in range(3):
        cut = slice(index * width, (index + 1) * width)
        right = jnp.concatenate([project[:, cut], project_theirs[:, cut]], 0)
        if index < 2:
            put_left(cut, grad_matmul(left, right))
        else:
            put_right(slice(0, width), grad_matmul(left, right))
    left = jnp.concatenate([half_at(attended, core), theirs[:, half : 2 * half]], 0)
    right = jnp.concatenate([attn_nat[...], attn_theirs[...]], 0)
    put_right(slice(width, 2 * width), grad_matmul(left, right))
    rows = half_at(vector, core) + half_at(vector_theirs, core)
    upper = rows.astype(BF)
    rest = (rows - upper.astype(F32)).astype(BF)
    count = rows.shape[0]
    line = lax.broadcasted_iota(jnp.int32, (count, LANES), 0)
    lane = lax.broadcasted_iota(jnp.int32, (count, LANES), 1)
    extra = grad_matmul(upper, (lane == line).astype(BF))
    extra += grad_matmul(rest, (lane == line + count).astype(BF))
    put_right(slice(2 * width, 2 * width + LANES), extra)


def attend_terms_fast(*args):
    rows, width = args[0].shape
    return run(
        attend_terms_kernel,
        "attend_terms",
        [shape((width // 4, 2 * width), BF)] * 2
        + [shape((width // 4, 2 * width + LANES), BF)] * 2,
        list(args),
        flops=16 * rows * width * width // 2,
    )


def after(array, *others):
    return lax.optimization_barrier((array, *others))[0]


def chips_parts(array):
    return [array] + [chip_shift(array, step) for step in range(1, chips_of())]


def chips_gather(array):
    return lax.all_gather(
        array, "seq", axis=0, tiled=True, axis_index_groups=core_groups()
    )


def chips_join(parts):
    chips = chips_of()
    chip, _ = place()
    return jnp.concatenate(
        [
            lax.select_n(chip, *[parts[(spot - index) % chips] for spot in range(chips)])
            for index in range(chips)
        ],
        0,
    )


def dp_swap(array, bit):
    size = lax.axis_size("dp")
    return lax.ppermute(array, "dp", [(i, i ^ bit) for i in range(size)])


def dp_place():
    spot = lax.axis_index("dp")
    return spot % 2, spot // 2


def join_pair(bit, own, other):
    return jnp.where(
        bit == 0, jnp.concatenate([own, other], 0), jnp.concatenate([other, own], 0)
    )


def square_first(part, cut):
    left, right = part[:, :cut], part[:, cut:]
    return left, dp_swap(left, 1), right, dp_swap(right, 2)


def square_second(left, left_far, right, right_far):
    bit, high = dp_place()
    left_far, right_far = lax.optimization_barrier((left_far, right_far))
    left = join_pair(bit, left, left_far)
    right = join_pair(high, right, right_far)
    return left, dp_swap(left, 2), right, dp_swap(right, 1)


def square_pieces(left, left_far, right, right_far):
    near = [core_swap(left), core_swap(right)]
    left_far, right_far = lax.optimization_barrier((left_far, right_far))
    return [
        left, left_far, near[0], core_swap(left_far),
        right, right_far, near[1], core_swap(right_far),
    ]


def vectors_kernel(groups, perm, perm_wide, *refs):
    pieces, refs = refs[:4], refs[4:]
    moved_out, plain_out, wide_out, stage, sems = refs
    width = perm.shape[0]
    start = pieces[0].shape[1] - LANES
    wait_all(
        fetch_right(pieces, stage, sems, slice(start, start + LANES), slice(0, LANES))
    )
    columns = stage[...]
    line = lax.broadcasted_iota(jnp.int32, (width, width), 0)
    spot = lax.broadcasted_iota(jnp.int32, (width, width), 1)
    moved_out[...] = grad_matmul(columns, (line == spot).astype(BF))
    plain = lax.dot_general(
        columns, perm[...], (((0,), (1,)), ((), ())), preferred_element_type=F32
    )
    plain_out[...] = plain
    wide = matmul(plain.astype(BF), perm_wide[...])
    piece = width // (2 * groups)
    for layer in range(LAYERS):
        for index in range(groups):
            row = layer * VECS + 5 + index
            for part in range(2 * groups):
                goal = part * groups * piece + index * piece
                wide_out[layer : layer + 1, goal : goal + piece] = wide[
                    row : row + 1, part * piece : (part + 1) * piece
                ]


def vectors_fast(groups, perm, perm_wide, pieces):
    width = perm.shape[0]
    return run(
        functools.partial(vectors_kernel, groups),
        "vectors",
        [shape((LANES, width), F32)] * 2 + [shape((8, groups * width), F32)],
        [perm, perm_wide],
        pieces,
        [pltpu.VMEM((width, LANES), BF), pltpu.SemaphoreType.DMA((8,))],
    )


def fold_kernel(*refs):
    bit, high = dp_place()
    for index, flag in enumerate((high, bit)):
        keep, came, keep_out, sent_out = (refs[index * 2], refs[index * 2 + 1],
                                          refs[4 + index * 2], refs[5 + index * 2])
        rows = keep.shape[0] // 2
        total = keep[...].astype(F32) + came[...].astype(F32)
        keep_out[...] = jnp.where(flag == 0, total[:rows], total[rows:]).astype(BF)
        sent_out[...] = jnp.where(flag == 0, total[rows:], total[:rows]).astype(BF)


def split_kernel(chips, *refs):
    left, left_far, right, right_far = refs[:4]
    own, sends, total = refs[4], refs[5 : 4 + chips], refs[4 + chips]
    chip, _ = spot_in()
    cut = left.shape[1]
    rows = left.shape[0] // chips
    for index in range(chips):
        span = slice(index * rows, (index + 1) * rows)
        total[index, :, :cut] = left[span, :].astype(F32) + left_far[span, :].astype(F32)
        total[index, :, cut:] = right[span, :].astype(F32) + right_far[span, :].astype(F32)
    own[...] = total[chip]
    for step in range(1, chips):
        sends[step - 1][...] = total[lax.rem(chip + step, chips)].astype(BF)


def square_fold(parts):
    left, left_sent, right, right_sent = parts
    rows = left.shape[0] // 2
    kinds = [shape((rows, member.shape[1]), BF) for member in (left, left, right, right)]
    return run(
        fold_kernel, "fold", kinds,
        [left, dp_swap(left_sent, 1), right, dp_swap(right_sent, 2)],
    )


def square_split(parts):
    chips = chips_of()
    left, left_sent, right, right_sent = parts
    share = left.shape[0] // chips
    width = left.shape[1] + right.shape[1]
    return run(
        functools.partial(split_kernel, chips),
        "split",
        [shape((share, width), F32)] + [shape((share, width), BF)] * (chips - 1),
        [left, dp_swap(left_sent, 2), right, dp_swap(right_sent, 1)],
        (),
        [pltpu.VMEM((chips, share, width), F32)],
    )


def square_total(parts):
    total = parts[0]
    for step in range(1, len(parts)):
        total = total + chip_shift(parts[step], step).astype(F32)
    return total


def piece_matrix(width, block, count):
    spot = np.arange(width)
    inner = spot % block
    return one_hot(
        ((spot // block) % 2) * (width // 2)
        + (inner % count) * (width // (2 * count))
        + (spot // (2 * block)) * (block // count)
        + inner // count
    )


def fast_device(
    hidden_input,
    triple_weight,
    mixer_weight,
    expand_weight,
    shrink_weight,
    vector_params,
    output_grad,
):
    _, count, width = hidden_input.shape
    chips = chips_of()
    _, core = place()
    share = triple_weight.shape[1]
    wide_share = shrink_weight.shape[1]
    wide = expand_weight.shape[2]
    groups = wide // width
    perm = swap_matrix(width, share)
    perm_wide = piece_matrix(width, wide_share, groups)
    mixer_moved = move(mixer_weight.reshape(-1, width), perm).reshape(mixer_weight.shape)
    shrink_moved = move(shrink_weight.reshape(-1, width), perm).reshape(shrink_weight.shape)
    pieces = 2 * groups
    expand_moved = (
        move(expand_weight.reshape(-1, width), perm_wide)
        .reshape(LAYERS * share, groups, pieces, width // pieces)
        .transpose(0, 2, 1, 3)
        .reshape(expand_weight.shape)
    )
    shrink_moved = shrink_moved.reshape(LAYERS, share, groups * width)
    vector_columns = vector_params.reshape(LAYERS * VECS, share).T
    vector_columns = jnp.pad(vector_columns, ((0, 0), (0, LANES - LAYERS * VECS)))

    feed_parts = [
        jnp.concatenate([expand_moved[layer], shrink_moved[layer]], 1) for layer in range(LAYERS)
    ]
    attn_one = jnp.concatenate([triple_weight[1], mixer_moved[1]], 1)
    parts = chips_parts(jnp.concatenate([triple_weight[0], mixer_moved[0], vector_columns], 1))
    parts[-1] = after(parts[-1], feed_parts[0])
    attn_zero = chips_join(parts)
    attn_zero = square_pieces(*square_second(*square_first(attn_zero, 2 * width)))
    feed_zero = chips_gather(feed_parts[0])
    attn_one = chips_parts(after(attn_one, attn_zero[0], attn_zero[4]))
    feed_zero = square_first(after(feed_zero, *attn_zero), wide)
    moved_rows, plain_rows, wide_rows = vectors_fast(groups, perm, perm_wide, attn_zero[4:])
    rows_of = []
    for layer in range(LAYERS):
        cut = slice(layer * VECS, (layer + 1) * VECS)
        rows_of.append(
            (moved_rows[cut], plain_rows[cut], wide_rows[layer : layer + 1])
        )

    def project(layer, hidden, pieces):
        low, blocks = project_fast(layer == 0, chips, hidden, perm, rows_of[layer][1], pieces)
        blocks = [blocks[0]] + [chip_shift(blocks[step], step) for step in range(1, chips)]
        return low, blocks

    def attend_blocks(blocks):
        others = [core_swap(block) for block in blocks]
        mixed, logs, pieces = attend_fast(chips, blocks, others)
        pieces = [pieces[0]] + [chip_shift(pieces[step], -step) for step in range(1, chips)]
        return (blocks, others, mixed, logs), pieces

    def feed(layer, hidden, low, pieces, weights):
        rows, _, ffn_bias = rows_of[layer]
        (
            hidden, attended, normed, pre_act, act, hat_one, scale_one, hat_two, scale_two,
            sent, squares,
        ) = feed_fast(chips, hidden, low, perm, rows, ffn_bias, pieces, weights)
        return (
            hidden,
            (hat_one, scale_one, hat_two, scale_two, pre_act),
            (low, attended, normed, act, core_swap(sent)),
            jnp.sum(squares[:3], -1),
        )

    low, blocks = project(0, hidden_input[0], attn_zero)
    feed_zero = [after(feed_zero[0], low), *feed_zero[1:]]
    feed_zero = square_second(*feed_zero)
    blocks[0] = after(blocks[0], feed_zero[0], feed_zero[2])
    feed_one = chips_gather(after(feed_parts[1], *blocks))
    attn_one[-1] = after(attn_one[-1], low)
    attn_one = chips_join(attn_one)
    attend_zero, pieces = attend_blocks(blocks)
    attn_one = square_first(after(attn_one, attend_zero[2]), 2 * width)
    attn_one = square_second(*attn_one)
    feed_one = lax.all_gather(
        after(feed_one, attn_one[0], attn_one[2]), "dp", axis=0, tiled=True
    )
    feed_zero = square_pieces(*feed_zero)
    pieces[0] = after(pieces[0], attn_one[0], attn_one[2])
    hidden, feed_saved_zero, acts_zero, squares_zero = feed(
        0, low, low, pieces, attn_zero[4:] + feed_zero
    )
    attn_one = square_pieces(*attn_one)
    low, blocks = project(1, hidden, attn_one)
    attend_one, pieces = attend_blocks(blocks)
    feed_one = after(feed_one, attend_one[2])
    feed_one = [feed_one, core_swap(feed_one)]
    hidden, feed_saved_one, acts_one, squares_one = feed(
        1, hidden, low, pieces, attn_one[4:] + feed_one
    )
    packs = [attn_zero + feed_zero, attn_one + feed_one]
    kept = [(attend_zero, feed_saved_zero, acts_zero), (attend_one, feed_saved_one, acts_one)]
    collected = [squares_zero, squares_one]
    elements = count * width * lax.axis_size("dp") * lax.axis_size("seq")
    hidden_output = move_back(hidden.astype(BF), perm)

    totals = jnp.stack(collected)
    sum_steps = [("seq", 1), ("seq", 2), ("seq", 4), ("dp", 1), ("dp", 2)]
    sum_steps = [step for step in sum_steps if step[1] < lax.axis_size(step[0])]

    def sum_more(totals, token):
        if sum_steps:
            axis, bit = sum_steps.pop(0)
            size = lax.axis_size(axis)
            pairs = [(i, i ^ bit) for i in range(size)]
            totals = totals + lax.ppermute(after(totals, token), axis, pairs)
        return totals

    def scatter_feed(term):
        part = lax.psum_scatter(term, "dp", scatter_dimension=0, tiled=True)
        part = lax.psum_scatter(
            part, "seq", scatter_dimension=0, tiled=True, axis_index_groups=core_groups()
        )
        return part.astype(F32)

    def back_feed(layer, grad):
        (_, feed_saved, acts), weights = kept[layer], packs[layer]
        grad_one, gave, attn_nat, sums, grads = feed_back_fast(
            layer == LAYERS - 1, chips, grad, perm, perm_wide, rows_of[layer][0], feed_saved,
            weights[4:],
        )
        grads = [grads[0]] + [chip_shift(grads[step], step) for step in range(1, chips)]
        _, _, normed, act, theirs = acts
        feed_term = feed_terms_fast(normed, act, gave, theirs, core_swap(gave))
        return grad_one, attn_nat, sums, grads, feed_term

    def back_attend(layer, grads):
        blocks, others, mixed, logs = kept[layer][0]
        return attend_back_fast(chips, blocks, others, grads, mixed, logs)

    def back_combine(grad_q, near, far):
        pieces = combine_fast(chips, grad_q, near, far)
        return [pieces[0]] + [chip_shift(pieces[step], -step) for step in range(1, chips)]

    def back_project(layer, grad_one, sums, pieces):
        return project_back_fast(chips, grad_one, perm, sums, pieces, packs[layer][:8])

    def back_terms(layer, project_grad, attn_nat, vector, far):
        low, attended, _, _, theirs = kept[layer][2]
        return attend_terms_fast(
            low, attended, project_grad, attn_nat, vector, theirs, *far
        )

    def swap_all(*members):
        return [core_swap(member) for member in members]

    grad_one, attn_nat, sums, grads, feed_term = back_feed(1, output_grad[0])
    totals = sum_more(totals, grad_one)
    feed_sum_one = lax.psum_scatter(feed_term, "dp", scatter_dimension=0, tiled=True)
    grads[0] = after(grads[0], feed_term, totals)
    grad_q, near, far = back_attend(1, grads)
    totals = sum_more(totals, grad_q)
    pieces = back_combine(after(grad_q, totals), near, core_swap(far))
    totals = sum_more(totals, pieces[0])
    pieces[0] = after(pieces[0], totals)
    grad, project_grad, vector = back_project(1, grad_one, sums, pieces)
    far_one = swap_all(project_grad, attn_nat, vector)
    terms_args = (project_grad, attn_nat, vector)

    grad_one, attn_nat, sums, grads, feed_term = back_feed(0, grad)
    attn_terms = back_terms(1, *terms_args, far_one)
    totals = sum_more(totals, grad_one)
    grads[0] = after(grads[0], feed_term, attn_terms[0], totals)
    grad_q, near, far = back_attend(0, grads)
    feed_sum_zero = scatter_feed(feed_term)
    totals = sum_more(totals, grad_q)
    pieces = back_combine(grad_q, near, core_swap(far))
    folded = square_fold(attn_terms)
    pieces[0] = after(pieces[0], folded[0], totals)
    project_grad, vector = collect_fast(chips, perm, sums, pieces)
    far_zero = swap_all(project_grad, attn_nat, vector)
    attn_terms = back_terms(0, project_grad, attn_nat, vector, far_zero)
    input_grad = input_back_fast(
        after(grad_one, attn_terms[0]), perm, project_grad, packs[0][:8]
    )
    split_one = square_split([after(folded[0], attn_terms[0]), *folded[1:]])
    feed_sum_one = after(feed_sum_one, attn_terms[0])
    feed_sum_one = scatter_chips(feed_sum_one)
    attn_terms = [
        attn_terms[0], after(attn_terms[1], split_one[0], input_grad), *attn_terms[2:]
    ]
    folded = square_fold(attn_terms)
    attn_sum_one = square_total(split_one)
    folded = [after(folded[0], attn_sum_one, feed_sum_one), *folded[1:]]
    attn_sum_zero = square_total(square_split(folded))
    terms = [(attn_sum_zero, feed_sum_zero), (attn_sum_one, feed_sum_one)]
    grad = input_grad
    root_squares = jnp.sqrt(totals / elements)
    vector_grad = jnp.stack(
        [
            (
                terms[layer][0][:, 4 * width : 4 * width + VECS]
                + terms[layer][0][:, 4 * width + 16 : 4 * width + 16 + VECS]
            ).T
            for layer in range(LAYERS)
        ]
    )
    return (
        hidden_output[None],
        grad[None],
        jnp.stack([terms[layer][0][:, : 3 * width] for layer in range(LAYERS)]),
        jnp.stack([terms[layer][0][:, 3 * width : 4 * width] for layer in range(LAYERS)]),
        jnp.stack([terms[layer][1][:, :wide] for layer in range(LAYERS)]),
        jnp.stack(
            [terms[layer][1][:, wide:].reshape(wide_share, width) for layer in range(LAYERS)]
        ),
        vector_grad,
        root_squares,
    )


def per_device(*args):
    chips = chips_of()
    if chips in (2, 4) and HEADS % chips == 0 and lax.axis_size("dp") == 4:
        return fast_device(*args)
    return plain_device(*args)


def solution(mesh):
    return jax.shard_map(
        per_device,
        mesh=mesh,
        in_specs=(
            P("dp", "seq", None),
            P(None, ("dp", "seq"), None),
            P(None, ("dp", "seq"), None),
            P(None, ("dp", "seq"), None),
            P(None, ("dp", "seq"), None),
            P(None, None, ("dp", "seq")),
            P("dp", "seq", None),
        ),
        out_specs=(
            P("dp", "seq", None),
            P("dp", "seq", None),
            P(None, ("dp", "seq"), None),
            P(None, ("dp", "seq"), None),
            P(None, ("dp", "seq"), None),
            P(None, ("dp", "seq"), None),
            P(None, None, ("dp", "seq")),
            P(),
        ),
        check_vma=False,
    )
```

```python
import functools
import math

import jax
import jax.numpy as jnp
import numpy as np
from jax import lax
from jax.experimental import pallas as pl
from jax.experimental.pallas import tpu as pltpu
from jax.sharding import PartitionSpec as P

HEADS = 12
HEAD = 64
LAYERS = 2
VECS = 12
LANES = 128

EPSILON = 1e-12
ROOT_HALF = 2.0 ** -0.5
ROOT_TAU = (2.0 * math.pi) ** -0.5

BF = jnp.bfloat16
F32 = jnp.float32


def layer_norm(residual, gain_row, shift_row):
    center = residual - jnp.mean(residual, -1, keepdims=True)
    spread = jnp.mean(center * center, -1, keepdims=True)
    return center * lax.rsqrt(spread + EPSILON) * gain_row + shift_row


def gelu_exact(values):
    return jax.nn.gelu(values, approximate=False)


def matmul(left, right):
    return jnp.dot(left, right, preferred_element_type=F32)


def matmul_t(left, right):
    return lax.dot_general(left, right, (((1,), (1,)), ((), ())), preferred_element_type=F32)


def grad_matmul(left, right):
    return lax.dot_general(left, right, (((0,), (0,)), ((), ())), preferred_element_type=F32)


def chips_of():
    return lax.axis_size("seq") // 2


def core_swap(array):
    size = lax.axis_size("seq")
    return lax.ppermute(array, "seq", [(i, i ^ 1) for i in range(size)])


def chip_shift(array, step):
    size = lax.axis_size("seq")
    chips = size // 2
    pairs = [(i, ((i // 2 + step) % chips) * 2 + i % 2) for i in range(size)]
    return lax.ppermute(array, "seq", pairs)


def core_groups():
    size = lax.axis_size("seq")
    return [list(range(0, size, 2)), list(range(1, size, 2))]


def place():
    spot = lax.axis_index("seq")
    return spot // 2, spot % 2


def gather_chips(array):
    chips = chips_of()
    if chips > 4:
        return lax.all_gather(
            array, "seq", axis=0, tiled=True, axis_index_groups=core_groups()
        )
    chip, _ = place()
    rows = array.shape[0]
    whole = jnp.zeros((chips * rows, array.shape[1]), array.dtype)
    for step in range(chips):
        part = array if step == 0 else chip_shift(array, step)
        whole = lax.dynamic_update_slice(whole, part, (((chip - step) % chips) * rows, 0))
    return whole


def gather_weight(array):
    own = lax.all_gather(gather_chips(array), "dp", axis=0, tiled=True)
    return join_cores(own, core_swap(own), 0)


def join_cores(own, other, axis):
    _, core = place()
    return jnp.where(
        core == 0,
        jnp.concatenate([own, other], axis),
        jnp.concatenate([other, own], axis),
    )


def scatter_chips(array):
    chips = chips_of()
    if chips > 4:
        return lax.psum_scatter(
            array, "seq", scatter_dimension=0, tiled=True, axis_index_groups=core_groups()
        ).astype(F32)
    chip, _ = place()
    rows = array.shape[0] // chips
    total = None
    for step in range(chips):
        part = lax.dynamic_slice(
            array, (((chip + step) % chips) * rows, 0), (rows, array.shape[1])
        )
        if step > 0:
            part = chip_shift(part, step)
        total = part.astype(F32) if total is None else total + part.astype(F32)
    return total


def scatter_grad(array):
    part = lax.psum_scatter(array.astype(BF), "dp", scatter_dimension=0, tiled=True)
    return scatter_chips(part)


def half_of(array, index):
    width = array.shape[1] // 2
    return lax.dynamic_slice(array, (0, index * width), (array.shape[0], width))


def one_hot(goal):
    return jnp.asarray(np.asarray(goal[:, None] == np.arange(goal.size)[None], np.float32), BF)


def swap_matrix(width, block):
    spot = np.arange(width)
    return one_hot(
        ((spot // block) % 2) * (width // 2) + (spot // (2 * block)) * block + spot % block
    )


def move(array, matrix):
    return jnp.dot(array, matrix, preferred_element_type=F32).astype(BF)


def move_back(array, matrix):
    return matmul_t(array, matrix).astype(BF)


def attend(queries, key_rows, value_rows):
    count = queries.shape[1] // HEAD
    outs = []
    logs = []
    for head in range(count):
        cut = slice(head * HEAD, (head + 1) * HEAD)
        scores = matmul_t(queries[:, cut], key_rows[:, cut])
        top = jnp.max(scores, -1, keepdims=True)
        log_total = top + jnp.log(jnp.sum(jnp.exp(scores - top), -1, keepdims=True))
        probability = jnp.exp(scores - log_total).astype(BF)
        outs.append(matmul(probability, value_rows[:, cut]))
        logs.append(log_total)
    return jnp.concatenate(outs, 1), jnp.concatenate(logs, 1)


def attend_back(queries, key_rows, value_rows, logs, mixed, grad_mixed):
    count = queries.shape[1] // HEAD
    grad_q, grad_k, grad_v = [], [], []
    for head in range(count):
        cut = slice(head * HEAD, (head + 1) * HEAD)
        grad_head = grad_mixed[:, cut]
        delta = jnp.sum(grad_head.astype(F32) * mixed[:, cut], -1, keepdims=True)
        probability = jnp.exp(
            matmul_t(queries[:, cut], key_rows[:, cut]) - logs[:, head : head + 1]
        )
        grad_prob = matmul_t(grad_head, value_rows[:, cut])
        grad_scores = (probability * (grad_prob - delta)).astype(BF)
        grad_q.append(matmul(grad_scores, key_rows[:, cut]))
        grad_k.append(grad_matmul(grad_scores, queries[:, cut]))
        grad_v.append(grad_matmul(probability.astype(BF), grad_head))
    return (
        jnp.concatenate(grad_q, 1).astype(BF),
        jnp.concatenate(grad_k + grad_v, 1).astype(BF),
    )


def forward_layer(hidden, params, perm):
    triple, mixer, expand, shrink, vectors, head_bias, ffn_bias = params
    rows, width = hidden.shape
    half = width // 2
    _, core = place()
    low = hidden.astype(BF)
    project = matmul(low, triple)
    queries = ((project[:, :width] + head_bias[0]) * 0.125).astype(BF)
    key_rows = project[:, width : 2 * width].astype(BF)
    value_rows = (project[:, 2 * width :] + head_bias[1]).astype(BF)
    trio = (queries, key_rows, value_rows)
    mine = jnp.concatenate([half_of(member, core) for member in trio], 1)
    sent = jnp.concatenate([half_of(member, 1 - core) for member in trio], 1)
    pair = jnp.concatenate([mine, core_swap(sent)], 0)
    pair_queries = pair[:, :half]
    pair_rest = pair[:, half:]
    chips = chips_of()
    if chips > 4:
        keyed = gather_chips(pair_rest)
    else:
        keyed = jnp.concatenate(
            [pair_rest] + [chip_shift(pair_rest, step) for step in range(1, chips)], 0
        )
    mixed, logs = attend(pair_queries, keyed[:, :half], keyed[:, half:])
    mixed_low = mixed.astype(BF)
    other = core_swap(mixed_low[rows:])
    attended = move(join_cores(mixed_low[:rows], other, 1), perm)
    attn_out = matmul(attended, mixer) + vectors[2]
    residual_one = hidden + attn_out
    normed = layer_norm(residual_one, vectors[3], vectors[4])
    normed_low = normed.astype(BF)
    pre_act = matmul(normed_low, expand) + ffn_bias
    act_low = gelu_exact(pre_act).astype(BF)
    ffn_out = matmul(act_low, shrink) + vectors[9]
    residual_two = normed + ffn_out
    output = layer_norm(residual_two, vectors[10], vectors[11])
    squares = jnp.stack(
        [jnp.sum(hidden * hidden), jnp.sum(attn_out * attn_out), jnp.sum(ffn_out * ffn_out)]
    )
    saved = (
        low, pair_queries, keyed, logs, mixed, attended,
        residual_one, normed_low, pre_act, act_low, residual_two,
    )
    return output, saved, squares


def backward_layer(grad_output, params, saved, perm, perm_wide):
    triple, mixer, expand, shrink, vectors, head_bias, ffn_bias = params
    (
        low, pair_queries, keyed, logs, mixed, attended,
        residual_one, normed_low, pre_act, act_low, residual_two,
    ) = saved
    rows, width = low.shape
    half = width // 2
    chips = chips_of()
    _, core = place()
    acts = jnp.concatenate(
        [half_of(member, 1 - core) for member in (low, attended, normed_low, act_low)], 1
    )
    acts = core_swap(acts)
    low_pair = jnp.concatenate([half_of(low, core), acts[:, :half]], 0)
    attended_pair = jnp.concatenate([half_of(attended, core), acts[:, half : 2 * half]], 0)
    normed_pair = jnp.concatenate([half_of(normed_low, core), acts[:, 2 * half : 3 * half]], 0)
    act_pair = jnp.concatenate([half_of(act_low, core), acts[:, 3 * half :]], 0)

    _, pull_two = jax.vjp(layer_norm, residual_two, vectors[10], vectors[11])
    grad_two, grad_gain_two, grad_shift_two = pull_two(grad_output)
    grad_ffn = grad_two.astype(BF)
    grad_act = matmul_t(grad_ffn, shrink)
    _, pull_gelu = jax.vjp(gelu_exact, pre_act)
    grad_pre = pull_gelu(grad_act)[0].astype(BF)
    grad_normed = grad_two + matmul_t(grad_pre, expand)
    _, pull_one = jax.vjp(layer_norm, residual_one, vectors[3], vectors[4])
    grad_one, grad_gain_one, grad_shift_one = pull_one(grad_normed)
    grad_attn = grad_one.astype(BF)
    grad_attended = move_back(matmul_t(grad_attn, mixer).astype(BF), perm)

    grad_ffn_nat = move_back(grad_ffn, perm)
    grad_attn_nat = move_back(grad_attn, perm)
    quarter = grad_pre.reshape(rows, 2, -1, half).transpose(0, 2, 1, 3).reshape(-1, width)
    grad_pre_nat = move_back(quarter, perm_wide).reshape(rows, -1)
    gave = jnp.concatenate([grad_ffn_nat, grad_pre_nat], 1)
    pair_ffn = jnp.concatenate([gave, core_swap(gave)], 0)
    grad_shrink = grad_matmul(act_pair, pair_ffn[:, :width])
    grad_expand = grad_matmul(normed_pair, pair_ffn[:, width:])

    other = core_swap(half_of(grad_attended, 1 - core))
    pair_grad = jnp.concatenate([half_of(grad_attended, core), other], 0)
    grad_q, grad_kv = attend_back(
        pair_queries, keyed[:, :half], keyed[:, half:], logs, mixed, pair_grad
    )
    span = 2 * rows
    if chips > 4:
        grad_kv = scatter_chips(grad_kv)
    else:
        total = grad_kv[:span].astype(F32)
        for step in range(1, chips):
            total = total + chip_shift(
                grad_kv[step * span : (step + 1) * span], -step
            ).astype(F32)
        grad_kv = total
    mine = jnp.concatenate([grad_q * 0.125, grad_kv.astype(BF)], 1)
    theirs = core_swap(mine)
    theirs = jnp.concatenate([theirs[rows:], theirs[:rows]], 0)
    pair_project = jnp.concatenate(
        [
            join_cores(mine[:, i * half : (i + 1) * half], theirs[:, i * half : (i + 1) * half], 1)
            for i in range(3)
        ],
        1,
    )
    grad_hidden = grad_one + matmul_t(pair_project[:rows], triple)
    grad_triple = grad_matmul(low_pair, pair_project)
    attn_pair = jnp.concatenate([grad_attn_nat, core_swap(grad_attn_nat)], 0)
    grad_mixer = grad_matmul(attended_pair, attn_pair)

    def sums(array):
        return jnp.sum(array.astype(F32), 0)

    bias_rows = jnp.concatenate(
        [
            sums(pair_project[:rows, :width])[None],
            sums(pair_project[:rows, 2 * width :])[None],
            sums(grad_pre_nat).reshape(-1, width),
        ],
        0,
    )
    count = width // (2 * lax.axis_size("dp") * chips)
    bias_rows = (
        bias_rows.reshape(bias_rows.shape[0], -1, 2, count)
        .transpose(0, 2, 1, 3)
        .reshape(bias_rows.shape)
    )
    grad_vector = jnp.concatenate(
        [
            bias_rows[:2],
            sums(grad_attn)[None],
            grad_gain_one[None],
            grad_shift_one[None],
            bias_rows[2:],
            sums(grad_ffn)[None],
            grad_gain_two[None],
            grad_shift_two[None],
        ],
        0,
    )
    grad_vector = half_of(grad_vector, core) + core_swap(half_of(grad_vector, 1 - core))
    high = grad_vector.astype(BF)
    rest = (grad_vector - high.astype(F32)).astype(BF)
    extra = jnp.concatenate([high, rest], 0).T
    extra = jnp.pad(extra, ((0, 0), (0, LANES - extra.shape[1])))
    attn_terms = jnp.concatenate([grad_triple.astype(BF), grad_mixer.astype(BF), extra], 1)
    return grad_hidden, attn_terms, grad_expand.astype(BF), grad_shrink.astype(BF)


def total_of(value):
    for axis in ("seq", "dp"):
        size = lax.axis_size(axis)
        step = 1
        while step < size:
            value = value + lax.ppermute(value, axis, [(i, i ^ step) for i in range(size)])
            step *= 2
    return value


def plain_device(
    hidden_input,
    triple_weight,
    mixer_weight,
    expand_weight,
    shrink_weight,
    vector_params,
    output_grad,
):
    _, count, width = hidden_input.shape
    share = triple_weight.shape[1]
    wide_share = shrink_weight.shape[1]
    wide = expand_weight.shape[2]
    groups = wide // width
    perm = swap_matrix(width, share)
    perm_wide = swap_matrix(width, wide_share)

    mixer_moved = move(mixer_weight.reshape(-1, width), perm).reshape(mixer_weight.shape)
    shrink_moved = move(shrink_weight.reshape(-1, width), perm).reshape(shrink_weight.shape)
    expand_moved = move(expand_weight.reshape(-1, width), perm_wide)
    expand_moved = (
        expand_moved.reshape(LAYERS * share, groups, 2, width // 2)
        .transpose(0, 2, 1, 3)
        .reshape(expand_weight.shape)
    )
    vector_columns = vector_params.reshape(LAYERS * VECS, share).T
    vector_columns = jnp.pad(vector_columns, ((0, 0), (0, LANES - LAYERS * VECS)))
    packs = []
    for layer in range(LAYERS):
        attn = [triple_weight[layer], mixer_moved[layer]]
        if layer == 0:
            attn.append(vector_columns)
        packs.append(
            (
                gather_weight(jnp.concatenate(attn, 1)),
                gather_weight(expand_moved[layer]),
                gather_weight(shrink_moved[layer]),
            )
        )
    vectors = packs[0][0][:, 4 * width : 4 * width + LAYERS * VECS].T
    natural = move_back(vectors, perm)
    params = []
    for layer in range(LAYERS):
        rows = vectors[layer * VECS : (layer + 1) * VECS].astype(F32)
        plain = natural[layer * VECS : (layer + 1) * VECS]
        ffn_bias = (
            move(plain[5 : 5 + groups], perm_wide)
            .reshape(groups, 2, width // 2)
            .transpose(1, 0, 2)
            .reshape(1, wide)
        ).astype(F32)
        attn, expand, shrink = packs[layer]
        params.append(
            (
                attn[:, : 3 * width],
                attn[:, 3 * width : 4 * width],
                expand,
                shrink,
                rows,
                plain[:2].astype(F32),
                ffn_bias,
            )
        )

    hidden = matmul(hidden_input[0], perm)
    kept = []
    collected = []
    for layer in range(LAYERS):
        hidden, saved, squares = forward_layer(hidden, params[layer], perm)
        kept.append(saved)
        collected.append(squares)
    elements = count * width * lax.axis_size("dp") * lax.axis_size("seq")
    root_squares = jnp.sqrt(total_of(jnp.stack(collected)) / elements)
    hidden_output = move_back(hidden.astype(BF), perm)

    grad = matmul(output_grad[0], perm)
    terms = [None] * LAYERS
    for layer in reversed(range(LAYERS)):
        grad, attn, expand, shrink = backward_layer(
            grad, params[layer], kept[layer], perm, perm_wide
        )
        terms[layer] = (scatter_grad(attn), scatter_grad(expand), scatter_grad(shrink))
    input_grad = move_back(grad.astype(BF), perm)
    vector_grad = jnp.stack(
        [
            (
                terms[layer][0][:, 4 * width : 4 * width + VECS]
                + terms[layer][0][:, 4 * width + VECS : 4 * width + 2 * VECS]
            ).T
            for layer in range(LAYERS)
        ]
    )
    return (
        hidden_output[None],
        input_grad[None],
        jnp.stack([terms[layer][0][:, : 3 * width] for layer in range(LAYERS)]),
        jnp.stack([terms[layer][0][:, 3 * width : 4 * width] for layer in range(LAYERS)]),
        jnp.stack([terms[layer][1] for layer in range(LAYERS)]),
        jnp.stack([terms[layer][2] for layer in range(LAYERS)]),
        vector_grad,
        root_squares,
    )


ANY = pl.BlockSpec(memory_space=pl.ANY)
VMEM = pl.BlockSpec(memory_space=pltpu.VMEM)
VMEM_BYTES = 56 * 1024 * 1024
HINT = 4
SIDE_HINT = 40
SIDE = ("feed_terms", "attend_terms", "slice_terms", "fold", "split", "input_back")


def shape(dims, kind):
    return jax.ShapeDtypeStruct(dims, kind)


def run(kernel, name, outs, placed, streamed=(), scratch=(), flops=0):
    hint = SIDE_HINT if name in SIDE else HINT
    size = sum(
        math.prod(member.shape) * member.dtype.itemsize
        for member in [*outs, *placed, *streamed]
    )
    return pl.pallas_call(
        kernel,
        name=name,
        out_shape=list(outs),
        in_specs=[VMEM] * len(placed) + [ANY] * len(streamed),
        out_specs=[VMEM] * len(outs),
        scratch_shapes=list(scratch),
        compiler_params=pltpu.CompilerParams(vmem_limit_bytes=VMEM_BYTES),
        cost_estimate=pl.CostEstimate(
            flops=int(flops * hint), bytes_accessed=int(size * hint), transcendentals=0
        ),
    )(*placed, *streamed)


def spot_in():
    index = lax.axis_index("seq")
    return index // 2, index % 2


def fetch_left(pieces, target, sems, columns, goal):
    _, core = spot_in()
    _, high = dp_place()
    rows = pieces[0].shape[0]
    copies = []
    for index, piece in enumerate(pieces):
        part = core if index < 2 else 1 - core
        side = high if index % 2 == 0 else 1 - high
        start = pl.multiple_of((part * 2 + side) * rows, 16)
        copy = pltpu.make_async_copy(
            piece.at[:, columns], target.at[pl.ds(start, rows), goal], sems.at[index]
        )
        copy.start()
        copies.append(copy)
    return copies


def fetch_whole(pieces, target, sems, columns, goal):
    _, core = spot_in()
    rows = pieces[0].shape[0]
    copies = []
    for index, piece in enumerate(pieces):
        part = core if index == 0 else 1 - core
        start = pl.multiple_of(part * rows, 16)
        copy = pltpu.make_async_copy(
            piece.at[:, columns], target.at[pl.ds(start, rows), goal], sems.at[index]
        )
        copy.start()
        copies.append(copy)
    return copies


def fetch_right(pieces, target, sems, columns, goal):
    _, core = spot_in()
    bit, _ = dp_place()
    rows = pieces[0].shape[0] // 2
    copies = []
    for index, piece in enumerate(pieces):
        part = core if index < 2 else 1 - core
        side = bit if index % 2 == 0 else 1 - bit
        for row in range(2):
            start = pl.multiple_of((part * 4 + row * 2 + side) * rows, 16)
            copy = pltpu.make_async_copy(
                piece.at[row * rows : (row + 1) * rows, columns],
                target.at[pl.ds(start, rows), goal],
                sems.at[2 * index + row],
            )
            copy.start()
            copies.append(copy)
    return copies


def wait_all(copies):
    for copy in copies:
        copy.wait()


def half_at(ref, part):
    half = ref.shape[1] // 2
    return ref[:, pl.ds(pl.multiple_of(part * half, LANES), half)]


def column_sum(values):
    return jnp.sum(values, 0, keepdims=True)


def fetch_project(layer, pieces, weight, left_sems, right_sems, width):
    if len(pieces) == 2:
        every = slice(0, 3 * width)
        return fetch_whole(pieces, weight, left_sems, every, every)
    first, last = slice(0, 2 * width), slice(2 * width, 3 * width)
    copies = fetch_left(pieces[:4], weight, left_sems, first, first)
    return copies + fetch_right(pieces[4:], weight, right_sems, slice(0, width), last)


def plain_rows(columns, perm):
    return lax.dot_general(
        columns, perm, (((0,), (1,)), ((), ())), preferred_element_type=F32
    )


def project_kernel(layer, chips, many, source, perm, bias, *rest):
    pieces, low_out, rest = rest[:many], rest[many], rest[many + 1 :]
    outs, (weight, stage, columns, *sems) = rest[:chips], rest[chips:]
    left_sems, right_sems, column_sems = sems
    chip, _ = spot_in()
    width = perm.shape[0]
    copies = fetch_project(layer, pieces, weight, left_sems, right_sems, width)
    if layer == 0:
        start = pieces[4].shape[1] - LANES
        column_copies = fetch_right(
            pieces[4:], columns, column_sems, slice(start, start + LANES), slice(0, LANES)
        )
        low = matmul(source[...], perm[...]).astype(BF)
        wait_all(column_copies)
        bias = plain_rows(columns[...], perm[...])
    else:
        low = source[...].astype(BF)
    low_out[...] = low
    wait_all(copies)
    group = width // chips
    for section in range(3):
        part = matmul(low, weight[:, section * width : (section + 1) * width])
        if section == 0:
            part = (part + bias[0:1]) * 0.125
        if section == 2:
            part = part + bias[1:2]
        part = part.astype(BF)
        for index in range(chips):
            stage[index, :, section * group : (section + 1) * group] = part[
                :, index * group : (index + 1) * group
            ]
    for step in range(chips):
        outs[step][...] = stage[lax.rem(chip + step, chips)]


def project_fast(layer, chips, source, perm, bias, pieces):
    rows, width = source.shape
    group = 3 * width // chips
    out = run(
        functools.partial(project_kernel, layer, chips, len(pieces)),
        "project",
        [shape((rows, width), BF)] + [shape((rows, group), BF)] * chips,
        [source, perm, bias],
        pieces,
        [
            pltpu.VMEM((width, 3 * width), BF),
            pltpu.VMEM((chips, rows, group), BF),
            pltpu.VMEM((width, LANES), BF),
            pltpu.SemaphoreType.DMA((4,)),
            pltpu.SemaphoreType.DMA((8,)),
            pltpu.SemaphoreType.DMA((8,)),
        ],
        flops=6 * rows * width * width,
    )
    return out[0], out[1:]


def fill_heads(blocks, others, group, queries, keys, values):
    rows = blocks[0].shape[0]
    for index, block in enumerate(blocks):
        cut = slice(index * rows, (index + 1) * rows)
        queries[cut, :] = block[:, :group]
        keys[cut, :] = block[:, group : 2 * group]
        values[cut, :] = block[:, 2 * group :]
    base = len(blocks) * rows
    for index, block in enumerate(others):
        cut = slice(base + index * rows, base + (index + 1) * rows)
        keys[cut, :] = block[:, group : 2 * group]
        values[cut, :] = block[:, 2 * group :]


def chunks_of(total):
    size = min(total, 256)
    return [slice(start, start + size) for start in range(0, total, size)]


def attend_kernel(chips, *refs):
    blocks, others = refs[:chips], refs[chips : 2 * chips]
    mixed, logs = refs[2 * chips : 2 * chips + 2]
    outs = refs[2 * chips + 2 : 3 * chips + 2]
    queries, keys, values = refs[3 * chips + 2 :]
    rows = blocks[0].shape[0]
    group = queries.shape[1]
    fill_heads(blocks, others, group, queries, keys, values)
    for head in range(group // HEAD):
        cut = slice(head * HEAD, (head + 1) * HEAD)
        key_head = keys[:, cut]
        value_head = values[:, cut]
        for part in chunks_of(chips * rows):
            scores = matmul_t(queries[part, cut], key_head)
            top = jnp.max(scores, -1, keepdims=True)
            power = jnp.exp(scores - top)
            total = jnp.sum(power, -1, keepdims=True)
            mixed[part, cut] = matmul(power.astype(BF), value_head) * (1.0 / total)
            logs[part, head : head + 1] = top + jnp.log(total)
    for index in range(chips):
        outs[index][...] = mixed[index * rows : (index + 1) * rows, :].astype(BF)


def attend_fast(chips, blocks, others):
    rows, wide = blocks[0].shape
    group = wide // 3
    span = chips * rows
    out = run(
        functools.partial(attend_kernel, chips),
        "attend",
        [shape((span, group), F32), shape((span, LANES), F32)]
        + [shape((rows, group), BF)] * chips,
        [*blocks, *others],
        (),
        [
            pltpu.VMEM((span, group), BF),
            pltpu.VMEM((2 * span, group), BF),
            pltpu.VMEM((2 * span, group), BF),
        ],
        flops=8 * span * span * group,
    )
    return out[0], out[1], out[2:]


def norm_in(residual):
    center = residual - jnp.mean(residual, -1, keepdims=True)
    spread = jnp.mean(center * center, -1, keepdims=True)
    scale = lax.rsqrt(spread + EPSILON)
    return center * scale, scale


def shrink_cut(index, wide, width):
    count = wide // width
    core, block = index // count, index % count
    half = width // 2
    return (
        slice(core * half, (core + 1) * half),
        slice(block * width, (block + 1) * width),
    )


def fetch_feed(weights, mixer, expand, shrink, sems):
    width, wide = expand.shape
    every, full = slice(0, width), slice(0, wide)
    return (
        fetch_right(weights[:4], mixer, sems[0], slice(width, 2 * width), every),
        fetch_whole(weights[4:], expand, sems[1], full, full),
        fetch_whole(weights[4:], shrink, sems[2], slice(wide, 2 * wide), full),
    )


def feed_kernel(layer, chips, many, hidden, low, perm, rows_in, wide_bias, *refs):
    pieces, refs = refs[:chips], refs[chips:]
    weights, refs = refs[:many], refs[many:]
    (out, attended, normed_low, pre_out, act_out, hat_one, scale_one, hat_two, scale_two,
     sent, squares) = refs[:11]
    stage, mixer, expand, shrink, *sems = refs[11:]
    chip, core = spot_in()
    width = perm.shape[0]
    wide = expand.shape[1]
    group = width // chips
    mixer_copies, expand_copies, shrink_copies = fetch_feed(
        weights, mixer, expand, shrink, sems
    )
    for step in range(chips):
        stage[lax.rem(chip + step, chips)] = pieces[step][...]
    moved = matmul(stage[0], perm[:group, :])
    for index in range(1, chips):
        moved += matmul(stage[index], perm[index * group : (index + 1) * group, :])
    moved = moved.astype(BF)
    attended[...] = moved
    wait_all(mixer_copies)
    attn_out = matmul(moved, mixer[...]) + rows_in[2:3]
    start = hidden[...].astype(F32)
    hat, scale = norm_in(start + attn_out)
    hat_one[...] = hat
    scale_one[...] = jnp.broadcast_to(scale, scale_one.shape)
    normed = hat * rows_in[3:4] + rows_in[4:5]
    normed_b = normed.astype(BF)
    normed_low[...] = normed_b
    squares[...] = jnp.zeros_like(squares)
    squares[0:1, :] = column_sum(start * start)
    squares[1:2, :] = column_sum(attn_out * attn_out)
    wait_all(expand_copies)
    wait_all(shrink_copies)
    half = width // 2
    total = None
    for index in range(wide // width):
        cut = slice(index * width, (index + 1) * width)
        pre = matmul(normed_b, expand[:, cut]) + wide_bias[:, cut]
        pre_out[:, cut] = pre
        act = (0.5 * pre * (1.0 + lax.erf(pre * ROOT_HALF))).astype(BF)
        act_out[:, cut] = act
        for side in range(2):
            rows, columns = shrink_cut(2 * index + side, wide, width)
            term = matmul(act[:, side * half : (side + 1) * half], shrink[rows, columns])
            total = term if total is None else total + term
    ffn_out = total + rows_in[9:10]
    squares[2:3, :] = column_sum(ffn_out * ffn_out)
    hat, scale = norm_in(normed + ffn_out)
    hat_two[...] = hat
    scale_two[...] = jnp.broadcast_to(scale, scale_two.shape)
    out[...] = hat * rows_in[10:11] + rows_in[11:12]
    for index, member in enumerate((low, attended, normed_low)):
        sent[:, index * half : (index + 1) * half] = half_at(member, 1 - core)
    sent[:, 3 * half :] = half_at(act_out, 1 - core)


def feed_fast(layer, chips, hidden, low, perm, vectors, wide_bias, pieces, weights):
    rows, width = hidden.shape
    wide = wide_bias.shape[1]
    return run(
        functools.partial(feed_kernel, layer, chips, len(weights)),
        "feed",
        [
            shape((rows, width), F32),
            shape((rows, width), BF),
            shape((rows, width), BF),
            shape((rows, wide), F32),
            shape((rows, wide), BF),
            shape((rows, width), F32),
            shape((rows, LANES), F32),
            shape((rows, width), F32),
            shape((rows, LANES), F32),
            shape((rows, (3 * width + wide) // 2), BF),
            shape((8, width), F32),
        ],
        [hidden, low, perm, vectors, wide_bias, *pieces],
        weights,
        [
            pltpu.VMEM((chips, rows, width // chips), BF),
            pltpu.VMEM((width, width), BF),
            pltpu.VMEM((width, wide), BF),
            pltpu.VMEM((width, wide), BF),
            pltpu.SemaphoreType.DMA((8,)),
            pltpu.SemaphoreType.DMA((4,)),
            pltpu.SemaphoreType.DMA((8,)),
        ],
        flops=4 * rows * width * (wide + width),
    )


def norm_back(grad, hat, scale):
    first = jnp.mean(grad, -1, keepdims=True)
    second = jnp.mean(grad * hat, -1, keepdims=True)
    return (grad - first - hat * second) * scale


def feed_back_kernel(
    layer, chips, many, source, perm, perm_wide, vectors, hat_one, scale_one, hat_two, scale_two,
    pre_in, *refs
):
    weights, refs = refs[:many], refs[many:]
    grad_one_out, gave, attn_nat, sums = refs[:4]
    outs = refs[4 : 4 + chips]
    stage, grad_pre, mixer, expand, shrink, *sems = refs[4 + chips :]
    chip, _ = spot_in()
    width = perm.shape[0]
    wide = expand.shape[1]
    group = width // chips
    half = width // 2
    mixer_copies, expand_copies, shrink_copies = fetch_feed(
        weights, mixer, expand, shrink, sems
    )
    grad = matmul(source[...], perm[...]) if layer == LAYERS - 1 else source[...]
    hat = hat_two[...]
    sums[...] = jnp.zeros_like(sums)
    sums[10:11, :] = column_sum(grad * hat)
    sums[11:12, :] = column_sum(grad)
    grad_two = norm_back(grad * vectors[10:11], hat, scale_two[:, 0:1])
    grad_ffn = grad_two.astype(BF)
    sums[9:10, :] = column_sum(grad_ffn.astype(F32))
    gave[:, :width] = matmul_t(grad_ffn, perm[...]).astype(BF)
    wait_all(shrink_copies)
    wait_all(expand_copies)
    grad_normed = grad_two
    for index in range(wide // width):
        cut = slice(index * width, (index + 1) * width)
        pre = pre_in[:, cut]
        slope = 0.5 * (1.0 + lax.erf(pre * ROOT_HALF)) + pre * (
            jnp.exp(-0.5 * pre * pre) * ROOT_TAU
        )
        sides = []
        for side in range(2):
            rows, columns = shrink_cut(2 * index + side, wide, width)
            sides.append(matmul_t(grad_ffn, shrink[rows, columns]))
        part = (jnp.concatenate(sides, 1) * slope).astype(BF)
        grad_pre[:, cut] = part
        grad_normed += matmul_t(part, expand[:, cut])
    groups = wide // width
    piece = half // groups
    for index in range(groups):
        joined = jnp.concatenate(
            [
                grad_pre[:, spot * half + index * piece : spot * half + (index + 1) * piece]
                for spot in range(2 * groups)
            ],
            1,
        )
        moved = matmul_t(joined, perm_wide[...])
        sums[5 + index : 6 + index, :] = column_sum(moved)
        gave[:, (index + 1) * width : (index + 2) * width] = moved.astype(BF)
    hat = hat_one[...]
    sums[3:4, :] = column_sum(grad_normed * hat)
    sums[4:5, :] = column_sum(grad_normed)
    grad_one = norm_back(grad_normed * vectors[3:4], hat, scale_one[:, 0:1])
    grad_one_out[...] = grad_one
    grad_attn = grad_one.astype(BF)
    sums[2:3, :] = column_sum(grad_attn.astype(F32))
    attn_nat[...] = matmul_t(grad_attn, perm[...]).astype(BF)
    wait_all(mixer_copies)
    grad_mixed = matmul_t(grad_attn, mixer[...]).astype(BF)
    for index in range(chips):
        stage[index] = matmul_t(
            grad_mixed, perm[index * group : (index + 1) * group, :]
        ).astype(BF)
    for step in range(chips):
        outs[step][...] = stage[lax.rem(chip + step, chips)]


def feed_back_fast(layer, chips, source, perm, perm_wide, vectors, saved, weights):
    rows, width = source.shape
    wide = saved[-1].shape[1]
    out = run(
        functools.partial(feed_back_kernel, layer, chips, len(weights)),
        "feed_back",
        [
            shape((rows, width), F32),
            shape((rows, width + wide), BF),
            shape((rows, width), BF),
            shape((16, width), F32),
        ]
        + [shape((rows, width // chips), BF)] * chips,
        [source, perm, perm_wide, vectors, *saved],
        weights,
        [
            pltpu.VMEM((chips, rows, width // chips), BF),
            pltpu.VMEM((rows, wide), BF),
            pltpu.VMEM((width, width), BF),
            pltpu.VMEM((width, wide), BF),
            pltpu.VMEM((width, wide), BF),
            pltpu.SemaphoreType.DMA((8,)),
            pltpu.SemaphoreType.DMA((4,)),
            pltpu.SemaphoreType.DMA((8,)),
        ],
        flops=4 * rows * width * (wide + 2 * width),
    )
    return out[0], out[1], out[2], out[3], out[4:]


def fetch_rows(pieces, target, sems, start):
    _, core = spot_in()
    rows, width = pieces[0].shape[0], target.shape[1]
    copies = []
    for index, piece in enumerate(pieces):
        part = core if index == 0 else 1 - core
        for block in range(4):
            goal = pl.multiple_of((part * 4 + block) * rows, 16)
            copy = pltpu.make_async_copy(
                piece.at[:, start + block * width : start + (block + 1) * width],
                target.at[pl.ds(goal, rows), :],
                sems.at[4 * index + block],
            )
            copy.start()
            copies.append(copy)
    return copies


def fetch_blocks(pieces, target, sems):
    _, core = spot_in()
    spot = lax.axis_index("dp")
    rows, width = pieces[0].shape[0], target.shape[1]
    copies = []
    for index, piece in enumerate(pieces):
        part = core if index == 0 else 1 - core
        for bits in range(4):
            goal = pl.multiple_of((part * 4 + jnp.bitwise_xor(spot, bits)) * rows, 16)
            copy = pltpu.make_async_copy(
                piece.at[:, bits * width : (bits + 1) * width],
                target.at[pl.ds(goal, rows), :],
                sems.at[4 * index + bits],
            )
            copy.start()
            copies.append(copy)
    return copies


def mix_kernel(chips, hidden, low, perm, rows_in, *refs):
    pieces, refs = refs[:chips], refs[chips:]
    weights, refs = refs[:4], refs[4:]
    attended, normed_out, normed_low, hat_one, scale_one, sent, squares = refs[:7]
    stage, mixer, sems = refs[7:]
    chip, core = spot_in()
    width = perm.shape[0]
    group = width // chips
    half = width // 2
    copies = fetch_right(weights, mixer, sems, slice(width, 2 * width), slice(0, width))
    for step in range(chips):
        stage[lax.rem(chip + step, chips)] = pieces[step][...]
    moved = matmul(stage[0], perm[:group, :])
    for index in range(1, chips):
        moved += matmul(stage[index], perm[index * group : (index + 1) * group, :])
    moved = moved.astype(BF)
    attended[...] = moved
    wait_all(copies)
    attn_out = matmul(moved, mixer[...]) + rows_in[2:3]
    start = hidden[...].astype(F32)
    hat, scale = norm_in(start + attn_out)
    hat_one[...] = hat
    scale_one[...] = jnp.broadcast_to(scale, scale_one.shape)
    normed = hat * rows_in[3:4] + rows_in[4:5]
    normed_out[...] = normed
    normed_low[...] = normed.astype(BF)
    squares[...] = jnp.zeros_like(squares)
    squares[0:1, :] = column_sum(start * start)
    squares[1:2, :] = column_sum(attn_out * attn_out)
    sent[:, :half] = half_at(low, 1 - core)
    sent[:, half:] = half_at(attended, 1 - core)


def mix_fast(chips, hidden, low, perm, vectors, pieces, weights):
    rows, width = hidden.shape
    return run(
        functools.partial(mix_kernel, chips),
        "mix",
        [
            shape((rows, width), BF),
            shape((rows, width), F32),
            shape((rows, width), BF),
            shape((rows, width), F32),
            shape((rows, LANES), F32),
            shape((rows, width), BF),
            shape((8, width), F32),
        ],
        [hidden, low, perm, vectors, *pieces],
        weights,
        [
            pltpu.VMEM((chips, rows, width // chips), BF),
            pltpu.VMEM((width, width), BF),
            pltpu.SemaphoreType.DMA((8,)),
        ],
        flops=4 * rows * width * width,
    )


def slice_row(wide_bias):
    spot = lax.axis_index("dp")
    line = lax.broadcasted_iota(jnp.int32, wide_bias.shape, 0)
    return jnp.sum(jnp.where(line == spot, wide_bias[...], 0.0), 0, keepdims=True)


def slice_feed_kernel(wide_bias, *refs):
    peers = 4
    blocks, weights, refs = refs[:peers], refs[peers : peers + 2], refs[peers + 2 :]
    near, sends, refs = refs[0], refs[1:peers], refs[peers:]
    pre_out, act_out, expand, shrink, expand_sems, shrink_sems = refs
    rows, width = blocks[0].shape
    expand_copies = fetch_blocks(weights, expand, expand_sems)
    shrink_copies = fetch_rows(weights, shrink, shrink_sems, 4 * width)
    bias = slice_row(wide_bias)
    wait_all(expand_copies)
    tokens = jnp.concatenate([block[...] for block in blocks], 0)
    pre = matmul(tokens, expand[...]) + bias
    pre_out[...] = pre
    act = (0.5 * pre * (1.0 + lax.erf(pre * ROOT_HALF))).astype(BF)
    act_out[...] = act
    wait_all(shrink_copies)
    part = matmul(act, shrink[...])
    near[...] = part[:rows]
    for index, out in enumerate(sends):
        out[...] = part[(index + 1) * rows : (index + 2) * rows].astype(BF)


def slice_scratch(width):
    return [
        pltpu.VMEM((width, width), BF),
        pltpu.VMEM((width, width), BF),
        pltpu.SemaphoreType.DMA((8,)),
        pltpu.SemaphoreType.DMA((8,)),
    ]


def slice_feed_fast(wide_bias, blocks, weights):
    rows, width = blocks[0].shape
    out = run(
        slice_feed_kernel,
        "slice_feed",
        [shape((rows, width), F32)]
        + [shape((rows, width), BF)] * 3
        + [shape((4 * rows, width), F32), shape((4 * rows, width), BF)],
        [wide_bias, *blocks],
        weights,
        slice_scratch(width),
        flops=16 * rows * width * width,
    )
    return out[:4], out[4], out[5]


def peer_sum(parts):
    total = parts[0][...]
    for part in parts[1:]:
        total = total + part[...].astype(F32)
    return total


def finish_kernel(normed, rows_in, squares_in, *refs):
    parts, (out, hat_two, scale_two, squares) = refs[:4], refs[4:]
    ffn_out = peer_sum(parts) + rows_in[9:10]
    squares[...] = squares_in[...]
    squares[2:3, :] = column_sum(ffn_out * ffn_out)
    hat, scale = norm_in(normed[...] + ffn_out)
    hat_two[...] = hat
    scale_two[...] = jnp.broadcast_to(scale, scale_two.shape)
    out[...] = hat * rows_in[10:11] + rows_in[11:12]


def finish_fast(normed, vectors, squares, parts):
    rows, width = normed.shape
    return run(
        finish_kernel,
        "finish",
        [
            shape((rows, width), F32),
            shape((rows, width), F32),
            shape((rows, LANES), F32),
            shape(squares.shape, F32),
        ],
        [normed, vectors, squares, *parts],
    )


def finish_back_kernel(first, source, perm, vectors, hat_two, scale_two, grad_out, low_out, sums):
    grad = matmul(source[...], perm[...]) if first else source[...]
    hat = hat_two[...]
    sums[...] = jnp.zeros_like(sums)
    sums[10:11, :] = column_sum(grad * hat)
    sums[11:12, :] = column_sum(grad)
    grad_two = norm_back(grad * vectors[10:11], hat, scale_two[:, 0:1])
    grad_out[...] = grad_two
    low = grad_two.astype(BF)
    low_out[...] = low
    sums[9:10, :] = column_sum(low.astype(F32))


def finish_back_fast(first, source, perm, vectors, hat_two, scale_two):
    rows, width = source.shape
    return run(
        functools.partial(finish_back_kernel, first),
        "finish_back",
        [shape((rows, width), F32), shape((rows, width), BF), shape((16, width), F32)],
        [source, perm, vectors, hat_two, scale_two],
    )


def slice_back_kernel(*refs):
    peers = 4
    blocks, refs = refs[:peers], refs[peers:]
    inputs, refs = refs[:peers], refs[peers:]
    pre_in, act_in, weights, refs = refs[0], refs[1], refs[2:4], refs[4:]
    near, sends, refs = refs[0], refs[1:peers], refs[peers:]
    slope_out, gave, sums, expand, shrink, expand_sems, shrink_sems = refs
    _, core = spot_in()
    rows, width = blocks[0].shape
    half = width // 2
    shrink_copies = fetch_rows(weights, shrink, shrink_sems, 4 * width)
    expand_copies = fetch_blocks(weights, expand, expand_sems)
    for index in range(peers):
        span = slice(index * rows, (index + 1) * rows)
        gave[span, :half] = half_at(inputs[index], 1 - core)
        gave[span, width : 2 * width] = blocks[index][...]
    gave[:, half:width] = half_at(act_in, 1 - core)
    tokens = jnp.concatenate([block[...] for block in blocks], 0)
    pre = pre_in[...]
    slope = 0.5 * (1.0 + lax.erf(pre * ROOT_HALF)) + pre * (
        jnp.exp(-0.5 * pre * pre) * ROOT_TAU
    )
    wait_all(shrink_copies)
    grad_pre = (matmul_t(tokens, shrink[...]) * slope).astype(BF)
    slope_out[...] = grad_pre
    gave[:, 2 * width :] = grad_pre
    sums[...] = jnp.broadcast_to(column_sum(grad_pre.astype(F32)), sums.shape)
    wait_all(expand_copies)
    part = matmul_t(grad_pre, expand[...])
    near[...] = part[:rows]
    for index, out in enumerate(sends):
        out[...] = part[(index + 1) * rows : (index + 2) * rows].astype(BF)


def slice_back_fast(blocks, inputs, pre, act, weights):
    rows, width = blocks[0].shape
    out = run(
        slice_back_kernel,
        "slice_back",
        [shape((rows, width), F32)]
        + [shape((rows, width), BF)] * 3
        + [
            shape((4 * rows, width), BF),
            shape((4 * rows, 3 * width), BF),
            shape((8, width), F32),
        ],
        [*blocks, *inputs, pre, act],
        weights,
        slice_scratch(width),
        flops=16 * rows * width * width,
    )
    return out[:4], out[4], out[5], out[6]


def slice_terms_kernel(peers, perm_rows, perm_units, *refs):
    blocks, inputs, refs = refs[:peers], refs[peers : 2 * peers], refs[2 * peers :]
    act_in, slope, theirs, out = refs
    _, core = spot_in()
    width = slope.shape[1]
    half = width // 2
    left = jnp.concatenate(
        [half_at(member, core) for member in inputs] + [theirs[:, :half]], 0
    )
    left = matmul(left, perm_rows[...]).astype(BF)
    right = jnp.concatenate([slope[...], theirs[:, 2 * width :]], 0)
    out[:, :width] = grad_matmul(left, right).astype(BF)
    left = jnp.concatenate([half_at(act_in, core), theirs[:, half:width]], 0)
    left = matmul(left, perm_units[...]).astype(BF)
    right = jnp.concatenate(
        [block[...] for block in blocks] + [theirs[:, width : 2 * width]], 0
    )
    out[:, width:] = grad_matmul(left, right).astype(BF)


def slice_terms_fast(perm_rows, perm_units, blocks, inputs, act, slope, theirs):
    rows, width = blocks[0].shape
    return run(
        functools.partial(slice_terms_kernel, 4),
        "slice_terms",
        [shape((width // 2, 2 * width), BF)],
        [perm_rows, perm_units, *blocks, *inputs, act, slope, theirs],
        flops=16 * rows * width * width,
    )[0]


def mix_back_kernel(chips, grad_two, perm, vectors, hat_one, scale_one, sums_in, *refs):
    parts, weights, refs = refs[:4], refs[4:8], refs[8:]
    grad_one_out, attn_nat, sums = refs[:3]
    outs = refs[3 : 3 + chips]
    stage, mixer, sems = refs[3 + chips :]
    chip, _ = spot_in()
    width = perm.shape[0]
    group = width // chips
    copies = fetch_right(weights, mixer, sems, slice(width, 2 * width), slice(0, width))
    grad_normed = grad_two[...] + peer_sum(parts)
    hat = hat_one[...]
    sums[...] = sums_in[...]
    sums[3:4, :] = column_sum(grad_normed * hat)
    sums[4:5, :] = column_sum(grad_normed)
    grad_one = norm_back(grad_normed * vectors[3:4], hat, scale_one[:, 0:1])
    grad_one_out[...] = grad_one
    grad_attn = grad_one.astype(BF)
    sums[2:3, :] = column_sum(grad_attn.astype(F32))
    attn_nat[...] = matmul_t(grad_attn, perm[...]).astype(BF)
    wait_all(copies)
    grad_mixed = matmul_t(grad_attn, mixer[...]).astype(BF)
    for index in range(chips):
        stage[index] = matmul_t(
            grad_mixed, perm[index * group : (index + 1) * group, :]
        ).astype(BF)
    for step in range(chips):
        outs[step][...] = stage[lax.rem(chip + step, chips)]


def mix_back_fast(chips, grad_two, perm, vectors, hat_one, scale_one, sums, parts, weights):
    rows, width = grad_two.shape
    out = run(
        functools.partial(mix_back_kernel, chips),
        "mix_back",
        [shape((rows, width), F32), shape((rows, width), BF), shape((16, width), F32)]
        + [shape((rows, width // chips), BF)] * chips,
        [grad_two, perm, vectors, hat_one, scale_one, sums, *parts],
        weights,
        [
            pltpu.VMEM((chips, rows, width // chips), BF),
            pltpu.VMEM((width, width), BF),
            pltpu.SemaphoreType.DMA((8,)),
        ],
        flops=6 * rows * width * width,
    )
    return out[0], out[1], out[2], out[3:]


def attend_back_kernel(chips, *refs):
    blocks, refs = refs[:chips], refs[chips:]
    others, refs = refs[:chips], refs[chips:]
    grads, refs = refs[:chips], refs[chips:]
    mixed, logs, grad_q, near, far, queries, keys, values, grad_in, key_sum, value_sum = refs
    rows = blocks[0].shape[0]
    group = queries.shape[1]
    span = chips * rows
    fill_heads(blocks, others, group, queries, keys, values)
    for index in range(chips):
        grad_in[index * rows : (index + 1) * rows, :] = grads[index][...]
    for head in range(group // HEAD):
        cut = slice(head * HEAD, (head + 1) * HEAD)
        key_head = keys[:, cut]
        value_head = values[:, cut]
        for place_in, part in enumerate(chunks_of(span)):
            query = queries[part, cut]
            grad = grad_in[part, cut]
            delta = jnp.sum(grad.astype(F32) * mixed[part, cut], -1, keepdims=True)
            probability = jnp.exp(matmul_t(query, key_head) - logs[part, head : head + 1])
            slope = matmul_t(grad, value_head) - delta
            grad_scores = (probability * slope).astype(BF)
            grad_q[part, cut] = (matmul(grad_scores, key_head) * 0.125).astype(BF)
            key_term = grad_matmul(grad_scores, query)
            value_term = grad_matmul(probability.astype(BF), grad)
            if place_in == 0:
                key_sum[:, cut] = key_term
                value_sum[:, cut] = value_term
            else:
                key_sum[:, cut] += key_term
                value_sum[:, cut] += value_term
    near[:, :group] = key_sum[:span, :]
    near[:, group:] = value_sum[:span, :]
    far[:, :group] = key_sum[span:, :].astype(BF)
    far[:, group:] = value_sum[span:, :].astype(BF)


def attend_back_fast(chips, blocks, others, grads, mixed, logs):
    rows, wide = blocks[0].shape
    group = wide // 3
    span = chips * rows
    return run(
        functools.partial(attend_back_kernel, chips),
        "attend_back",
        [
            shape((span, group), BF),
            shape((span, 2 * group), F32),
            shape((span, 2 * group), BF),
        ],
        [*blocks, *others, *grads, mixed, logs],
        (),
        [
            pltpu.VMEM((span, group), BF),
            pltpu.VMEM((2 * span, group), BF),
            pltpu.VMEM((2 * span, group), BF),
            pltpu.VMEM((span, group), BF),
            pltpu.VMEM((2 * span, group), F32),
            pltpu.VMEM((2 * span, group), F32),
        ],
        flops=20 * span * span * group,
    )


def combine_kernel(grad_q, near, far, *outs):
    rows, wide = outs[0].shape
    group = wide // 3
    for index, out in enumerate(outs):
        cut = slice(index * rows, (index + 1) * rows)
        out[:, :group] = grad_q[cut, :]
        out[:, group:] = (near[cut, :] + far[cut, :].astype(F32)).astype(BF)


def combine_fast(chips, grad_q, near, far):
    span, group = grad_q.shape
    return run(
        combine_kernel,
        "combine",
        [shape((span // chips, 3 * group), BF)] * chips,
        [grad_q, near, far],
    )


def exact_move(values, perm):
    high = values.astype(BF)
    rest = values - high.astype(F32)
    middle = rest.astype(BF)
    low = (rest - middle.astype(F32)).astype(BF)
    return matmul(high, perm) + matmul(middle, perm) + matmul(low, perm)


def collect(chips, stage, pieces, project):
    chip, _ = spot_in()
    width = project.shape[1] // 3
    group = width // chips
    for step in range(chips):
        stage[lax.rem(chip + step, chips)] = pieces[step][...]
    for section in range(3):
        cut = slice(section * group, (section + 1) * group)
        joined = jnp.concatenate([stage[index][:, cut] for index in range(chips)], 1)
        project[:, section * width : (section + 1) * width] = joined


def through_project(grad, project, weight):
    width = grad.shape[1]
    for section in range(3):
        cut = slice(section * width, (section + 1) * width)
        grad += matmul_t(project[:, cut], weight[:, cut])
    return grad


def project_back_kernel(layer, chips, many, grad_one, perm, sums, *refs):
    pieces, refs = refs[:chips], refs[chips:]
    weights, refs = refs[:many], refs[many:]
    out, project, vector_out, stage, weight, left_sems, right_sems = refs
    copies = fetch_project(layer, weights, weight, left_sems, right_sems, perm.shape[0])
    collect(chips, stage, pieces, project)
    wait_all(copies)
    out[...] = through_project(grad_one[...], project, weight)
    vector_rows(project, sums, perm, vector_out)


def collect_kernel(chips, perm, perm_wide, feed_sums, sums, *refs):
    pieces, refs = refs[:chips], refs[chips:]
    project, vector_out, stage = refs
    collect(chips, stage, pieces, project)
    slice_vector_rows(project, sums, feed_sums, perm, perm_wide, vector_out)


def collect_fast(chips, perm, perm_wide, feed_sums, sums, pieces):
    rows, group = pieces[0].shape
    return run(
        functools.partial(collect_kernel, chips),
        "collect",
        [shape((rows, chips * group), BF), shape(sums.shape, F32)],
        [perm, perm_wide, feed_sums, sums, *pieces],
        (),
        [pltpu.VMEM((chips, rows, group), BF)],
    )


def input_back_kernel(grad_one, perm, project, *refs):
    weights, refs = refs[:8], refs[8:]
    out, weight, left_sems, right_sems = refs
    wait_all(fetch_project(0, weights, weight, left_sems, right_sems, perm.shape[0]))
    grad = through_project(grad_one[...], project, weight)
    out[...] = matmul_t(grad.astype(BF), perm[...]).astype(BF)


def input_back_fast(grad_one, perm, project, weights):
    rows, width = grad_one.shape
    return run(
        input_back_kernel,
        "input_back",
        [shape((rows, width), BF)],
        [grad_one, perm, project],
        weights,
        [
            pltpu.VMEM((width, 3 * width), BF),
            pltpu.SemaphoreType.DMA((4,)),
            pltpu.SemaphoreType.DMA((8,)),
        ],
        flops=6 * rows * width * width,
    )[0]


def exact_back(values, perm):
    high = values.astype(BF)
    rest = values - high.astype(F32)
    middle = rest.astype(BF)
    low = (rest - middle.astype(F32)).astype(BF)
    return matmul_t(high, perm) + matmul_t(middle, perm) + matmul_t(low, perm)


def slice_vector_rows(project, sums, feed_sums, perm, perm_wide, vector_out):
    width = perm.shape[0]
    spot = lax.axis_index("dp")
    vector_out[...] = sums[...]
    line = lax.broadcasted_iota(jnp.int32, (8, width), 0)
    rows = exact_back(feed_sums[...], perm_wide[...])
    first = column_sum(project[:, :width].astype(F32))
    second = column_sum(project[:, 2 * width :].astype(F32))
    rows = jnp.where(line == 0, first, jnp.where(line == 1, second, rows))
    moved = exact_move(rows, perm[...])
    vector_out[0:2, :] = moved[0:2, :]
    wide_line = lax.broadcasted_iota(jnp.int32, (16, width), 0)
    vector_out[...] = jnp.where(wide_line == 5 + spot, moved[2:3, :], vector_out[...])


def vector_rows(project, sums, perm, vector_out):
    width = perm.shape[0]
    vector_out[...] = sums[...]
    vector_out[0:1, :] = column_sum(project[:, :width].astype(F32))
    vector_out[1:2, :] = column_sum(project[:, 2 * width :].astype(F32))
    moved = exact_move(vector_out[0:8, :], perm[...])
    vector_out[0:2, :] = moved[0:2, :]
    vector_out[5:8, :] = moved[5:8, :]
    moved = exact_move(vector_out[8:16, :], perm[...])
    vector_out[8:9, :] = moved[0:1, :]


def project_back_fast(layer, chips, grad_one, perm, sums, pieces, weights):
    rows, width = grad_one.shape
    return run(
        functools.partial(project_back_kernel, layer, chips, len(weights)),
        "project_back",
        [
            shape((rows, width), F32),
            shape((rows, 3 * width), BF),
            shape((16, width), F32),
        ],
        [grad_one, perm, sums, *pieces],
        weights,
        [
            pltpu.VMEM((chips, rows, 3 * width // chips), BF),
            pltpu.VMEM((width, 3 * width), BF),
            pltpu.SemaphoreType.DMA((4,)),
            pltpu.SemaphoreType.DMA((8,)),
        ],
        flops=6 * rows * width * width,
    )


def feed_terms_kernel(normed, act, gave, theirs, gave_theirs, out):
    _, core = spot_in()
    width = normed.shape[1]
    half = width // 2
    left = jnp.concatenate([half_at(normed, core), theirs[:, 2 * half : 3 * half]], 0)
    count = act.shape[1] // width
    for index in range(count):
        cut = slice(index * width, (index + 1) * width)
        far = slice((index + 1) * width, (index + 2) * width)
        right = jnp.concatenate([gave[:, far], gave_theirs[:, far]], 0)
        out[:, cut] = grad_matmul(left, right).astype(BF)
    left = jnp.concatenate([half_at(act, core), theirs[:, 3 * half :]], 0)
    right = jnp.concatenate([gave[:, :width], gave_theirs[:, :width]], 0)
    for index in range(count):
        cut = slice(index * half, (index + 1) * half)
        spot = slice((count + index) * width, (count + index + 1) * width)
        out[:, spot] = grad_matmul(left[:, cut], right).astype(BF)


def feed_terms_fast(normed, act, gave, theirs, gave_theirs):
    rows, width = normed.shape
    wide = act.shape[1]
    return run(
        feed_terms_kernel,
        "feed_terms",
        [shape((width // 2, 2 * wide), BF)],
        [normed, act, gave, theirs, gave_theirs],
        flops=4 * rows * width * wide,
    )[0]


def attend_terms_kernel(
    low, attended, project, attn_nat, vector, theirs, project_theirs, attn_theirs,
    vector_theirs, left_keep, left_sent, right_keep, right_sent
):
    _, core = spot_in()
    bit, high = dp_place()
    width = low.shape[1]
    half = width // 2
    block = half // 4

    def put_left(columns, value):
        value = value.astype(BF)
        for side in range(2):
            first = value[2 * side * block : (2 * side + 1) * block]
            second = value[(2 * side + 1) * block : (2 * side + 2) * block]
            rows = slice(side * block, (side + 1) * block)
            left_keep[rows, columns] = jnp.where(bit == 0, first, second)
            left_sent[rows, columns] = jnp.where(bit == 0, second, first)

    def put_right(columns, value):
        value = value.astype(BF)
        first, second = value[: 2 * block], value[2 * block :]
        right_keep[:, columns] = jnp.where(high == 0, first, second)
        right_sent[:, columns] = jnp.where(high == 0, second, first)

    left = jnp.concatenate([half_at(low, core), theirs[:, :half]], 0)
    for index in range(3):
        cut = slice(index * width, (index + 1) * width)
        right = jnp.concatenate([project[:, cut], project_theirs[:, cut]], 0)
        if index < 2:
            put_left(cut, grad_matmul(left, right))
        else:
            put_right(slice(0, width), grad_matmul(left, right))
    left = jnp.concatenate([half_at(attended, core), theirs[:, half : 2 * half]], 0)
    right = jnp.concatenate([attn_nat[...], attn_theirs[...]], 0)
    put_right(slice(width, 2 * width), grad_matmul(left, right))
    rows = half_at(vector, core) + half_at(vector_theirs, core)
    upper = rows.astype(BF)
    rest = (rows - upper.astype(F32)).astype(BF)
    count = rows.shape[0]
    line = lax.broadcasted_iota(jnp.int32, (count, LANES), 0)
    lane = lax.broadcasted_iota(jnp.int32, (count, LANES), 1)
    extra = grad_matmul(upper, (lane == line).astype(BF))
    extra += grad_matmul(rest, (lane == line + count).astype(BF))
    put_right(slice(2 * width, 2 * width + LANES), extra)


def attend_terms_fast(*args):
    rows, width = args[0].shape
    return run(
        attend_terms_kernel,
        "attend_terms",
        [shape((width // 4, 2 * width), BF)] * 2
        + [shape((width // 4, 2 * width + LANES), BF)] * 2,
        list(args),
        flops=16 * rows * width * width // 2,
    )


def after(array, *others):
    return lax.optimization_barrier((array, *others))[0]


def chips_parts(array):
    return [array] + [chip_shift(array, step) for step in range(1, chips_of())]


def chips_gather(array):
    return lax.all_gather(
        array, "seq", axis=0, tiled=True, axis_index_groups=core_groups()
    )


def chips_scatter(array):
    return lax.psum_scatter(
        array, "seq", scatter_dimension=0, tiled=True, axis_index_groups=core_groups()
    )


def chips_join(parts):
    chips = chips_of()
    chip, _ = place()
    return jnp.concatenate(
        [
            lax.select_n(chip, *[parts[(spot - index) % chips] for spot in range(chips)])
            for index in range(chips)
        ],
        0,
    )


def dp_swap(array, bit):
    size = lax.axis_size("dp")
    return lax.ppermute(array, "dp", [(i, i ^ bit) for i in range(size)])


def dp_place():
    spot = lax.axis_index("dp")
    return spot % 2, spot // 2


def join_pair(bit, own, other):
    return jnp.where(
        bit == 0, jnp.concatenate([own, other], 0), jnp.concatenate([other, own], 0)
    )


def square_first(part, cut):
    left, right = part[:, :cut], part[:, cut:]
    return left, dp_swap(left, 1), right, dp_swap(right, 2)


def square_second(left, left_far, right, right_far):
    bit, high = dp_place()
    left_far, right_far = lax.optimization_barrier((left_far, right_far))
    left = join_pair(bit, left, left_far)
    right = join_pair(high, right, right_far)
    return left, dp_swap(left, 2), right, dp_swap(right, 1)


def square_pieces(left, left_far, right, right_far):
    near = [core_swap(left), core_swap(right)]
    left_far, right_far = lax.optimization_barrier((left_far, right_far))
    return [
        left, left_far, near[0], core_swap(left_far),
        right, right_far, near[1], core_swap(right_far),
    ]


def vectors_kernel(groups, perm, perm_wide, *refs):
    pieces, refs = refs[:4], refs[4:]
    outs, (stage, sems) = refs[:-2], refs[-2:]
    width = perm.shape[0]
    start = pieces[0].shape[1] - LANES
    wait_all(
        fetch_right(pieces, stage, sems, slice(start, start + LANES), slice(0, LANES))
    )
    columns = stage[...]
    line = lax.broadcasted_iota(jnp.int32, (width, width), 0)
    spot = lax.broadcasted_iota(jnp.int32, (width, width), 1)
    moved = grad_matmul(columns, (line == spot).astype(BF))
    plain = plain_rows(columns, perm[...])
    wide = matmul(plain.astype(BF), perm_wide[...])
    piece = width // (2 * groups)
    for layer in range(LAYERS):
        base = layer * VECS
        moved_out, plain_out, wide_out = outs[3 * layer : 3 * layer + 3]
        moved_out[:VECS, :] = moved[base : base + VECS]
        plain_out[:VECS, :] = plain[base : base + VECS]
        if layer == 0:
            wide_out[...] = wide[base + 5 : base + 5 + groups]
            continue
        for index in range(groups):
            row = base + 5 + index
            for part in range(2 * groups):
                goal = part * groups * piece + index * piece
                wide_out[:, goal : goal + piece] = wide[
                    row : row + 1, part * piece : (part + 1) * piece
                ]


def vectors_fast(groups, perm, perm_wide, pieces):
    width = perm.shape[0]
    out = run(
        functools.partial(vectors_kernel, groups),
        "vectors",
        [
            *[shape((16, width), F32)] * 2,
            shape((groups, width), F32),
            *[shape((16, width), F32)] * 2,
            shape((1, groups * width), F32),
        ],
        [perm, perm_wide],
        pieces,
        [pltpu.VMEM((width, LANES), BF), pltpu.SemaphoreType.DMA((8,))],
    )
    return [out[:3], out[3:]]


def fold_kernel(*refs):
    bit, high = dp_place()
    for index, flag in enumerate((high, bit)):
        keep, came, keep_out, sent_out = (refs[index * 2], refs[index * 2 + 1],
                                          refs[4 + index * 2], refs[5 + index * 2])
        rows = keep.shape[0] // 2
        total = keep[...].astype(F32) + came[...].astype(F32)
        keep_out[...] = jnp.where(flag == 0, total[:rows], total[rows:]).astype(BF)
        sent_out[...] = jnp.where(flag == 0, total[rows:], total[:rows]).astype(BF)


def split_kernel(chips, *refs):
    left, left_far, right, right_far = refs[:4]
    own, sends, total = refs[4], refs[5 : 4 + chips], refs[4 + chips]
    chip, _ = spot_in()
    cut = left.shape[1]
    rows = left.shape[0] // chips
    for index in range(chips):
        span = slice(index * rows, (index + 1) * rows)
        total[index, :, :cut] = left[span, :].astype(F32) + left_far[span, :].astype(F32)
        total[index, :, cut:] = right[span, :].astype(F32) + right_far[span, :].astype(F32)
    own[...] = total[chip]
    for step in range(1, chips):
        sends[step - 1][...] = total[lax.rem(chip + step, chips)].astype(BF)


def square_fold(parts):
    left, left_sent, right, right_sent = parts
    rows = left.shape[0] // 2
    kinds = [shape((rows, member.shape[1]), BF) for member in (left, left, right, right)]
    return run(
        fold_kernel, "fold", kinds,
        [left, dp_swap(left_sent, 1), right, dp_swap(right_sent, 2)],
    )


def square_split(parts):
    chips = chips_of()
    left, left_sent, right, right_sent = parts
    share = left.shape[0] // chips
    width = left.shape[1] + right.shape[1]
    return run(
        functools.partial(split_kernel, chips),
        "split",
        [shape((share, width), F32)] + [shape((share, width), BF)] * (chips - 1),
        [left, dp_swap(left_sent, 2), right, dp_swap(right_sent, 1)],
        (),
        [pltpu.VMEM((chips, share, width), F32)],
    )


def square_total(parts):
    total = parts[0]
    for step in range(1, len(parts)):
        total = total + chip_shift(parts[step], step).astype(F32)
    return total


def piece_matrix(width, block, count):
    spot = np.arange(width)
    inner = spot % block
    return one_hot(
        ((spot // block) % 2) * (width // 2)
        + (inner % count) * (width // (2 * count))
        + (spot // (2 * block)) * (block // count)
        + inner // count
    )


def peer_shift(array, bits):
    size = lax.axis_size("dp")
    return lax.ppermute(array, "dp", [(i, i ^ bits) for i in range(size)])


def peer_gather(array):
    return [array] + [peer_shift(array, bits) for bits in range(1, 4)]


def peer_trade(parts):
    return [parts[0]] + [peer_shift(parts[bits], bits) for bits in range(1, 4)]


def units_matrix(width, block, count):
    half = width // 2
    spot = np.arange(half)
    inner = spot % block
    chips = half // (block * count)
    return one_hot(
        (spot // block) % chips * (block * count) + inner * count + spot // (block * chips)
    )


def rows_matrix(width, block):
    half = width // 2
    spot = np.arange(half)
    chips = half // (4 * block)
    return one_hot(
        (spot // block) % chips * (4 * block) + spot // (block * chips) * block + spot % block
    )


def fast_device(
    hidden_input,
    triple_weight,
    mixer_weight,
    expand_weight,
    shrink_weight,
    vector_params,
    output_grad,
):
    _, count, width = hidden_input.shape
    chips = chips_of()
    _, core = place()
    share = triple_weight.shape[1]
    wide_share = shrink_weight.shape[1]
    wide = expand_weight.shape[2]
    groups = wide // width
    perm = swap_matrix(width, share)
    perm_wide = piece_matrix(width, wide_share, groups)
    mixer_moved = move(mixer_weight.reshape(-1, width), perm).reshape(mixer_weight.shape)
    shrink_moved = move(shrink_weight.reshape(-1, width), perm).reshape(shrink_weight.shape)
    pieces = 2 * groups
    spot = lax.axis_index("dp")
    perm_rows = rows_matrix(width, share)
    perm_units = units_matrix(width, share, groups)
    expand_zero = move(expand_weight[0].reshape(-1, width), perm_wide).reshape(share, wide)
    expand_one = (
        move(expand_weight[1].reshape(-1, width), perm_wide)
        .reshape(share, groups, pieces, width // pieces)
        .transpose(0, 2, 1, 3)
        .reshape(share, wide)
    )
    shrink_moved = shrink_moved.reshape(LAYERS, share, groups * width)
    vector_columns = vector_params.reshape(LAYERS * VECS, share).T
    vector_columns = jnp.pad(vector_columns, ((0, 0), (0, LANES - LAYERS * VECS)))

    parts = chips_parts(
        jnp.concatenate([triple_weight[0], mixer_moved[0], vector_columns], 1)
    )
    expand_zero = after(expand_zero, parts[1])
    expand_zero = jnp.concatenate(
        peer_trade(
            [
                lax.dynamic_slice(
                    expand_zero, (0, jnp.bitwise_xor(spot, bits) * width), (share, width)
                )
                for bits in range(4)
            ]
        ),
        1,
    )
    feed_parts = [
        jnp.concatenate([expand_zero, shrink_moved[0]], 1),
        jnp.concatenate([expand_one, shrink_moved[1]], 1),
    ]
    early = jnp.concatenate([feed_parts[0], triple_weight[1], mixer_moved[1]], 1)
    parts[-1] = after(parts[-1], early, feed_parts[1])
    attn = chips_join(parts)
    early = chips_gather(after(early, attn))
    feed_zero, attn_one = early[:, : 2 * wide], early[:, 2 * wide :]
    attn = square_second(*square_first(attn, 2 * width))
    attn = square_pieces(*attn)

    def project(layer, hidden, pieces):
        bias = perm[:8].astype(F32) if layer == 0 else rows_of[layer][1]
        low, blocks = project_fast(layer, chips, hidden, perm, bias, pieces)
        blocks = [blocks[0]] + [chip_shift(blocks[step], step) for step in range(1, chips)]
        return low, blocks

    def attend_blocks(blocks):
        others = [core_swap(block) for block in blocks]
        mixed, logs, pieces = attend_fast(chips, blocks, others)
        pieces = [pieces[0]] + [chip_shift(pieces[step], -step) for step in range(1, chips)]
        return (blocks, others, mixed, logs), pieces

    def feed(layer, hidden, low, pieces, weights):
        rows, _, ffn_bias = rows_of[layer]
        (
            hidden, attended, normed, pre_act, act, hat_one, scale_one, hat_two, scale_two,
            sent, squares,
        ) = feed_fast(layer, chips, hidden, low, perm, rows, ffn_bias, pieces, weights)
        return (
            hidden,
            (hat_one, scale_one, hat_two, scale_two, pre_act),
            (low, attended, normed, act, core_swap(sent)),
            jnp.sum(squares[:3], -1),
        )

    low_zero, blocks = project(0, hidden_input[0], attn)
    feed_zero = after(feed_zero, *blocks)
    attn_one = square_second(*square_first(after(attn_one, *blocks), 2 * width))
    feed_one = chips_gather(after(feed_parts[1], *blocks))
    blocks[0] = after(blocks[0], attn_one[0], attn_one[2])
    attend_zero, pieces = attend_blocks(blocks)
    attn_one = [
        attn_one[0], after(attn_one[1], attend_zero[2]),
        attn_one[2], after(attn_one[3], attend_zero[2]),
    ]
    vector_pieces = [after(attn[4], attend_zero[2], attn_one[1], attn_one[3]), *attn[5:]]
    rows_of = vectors_fast(groups, perm, perm_wide, vector_pieces)
    attn_one = square_pieces(*attn_one)
    slice_pieces = [feed_zero, core_swap(feed_zero)]
    pieces[0] = after(pieces[0], slice_pieces[1], *attn_one)

    attended, normed, normed_low, hat, scale, sent, squares = mix_fast(
        chips, low_zero, low_zero, perm, rows_of[0][0], pieces, attn[4:]
    )
    norms_zero, acts_zero = (hat, scale), (low_zero, attended, None, None, core_swap(sent))
    inputs = peer_gather(normed_low)
    terms, pre, act = slice_feed_fast(rows_of[0][2], inputs, slice_pieces)
    feed_one = lax.all_gather(after(feed_one, normed), "dp", axis=0, tiled=True)
    slice_saved = (inputs, pre, act)
    hidden, hat, scale, squares = finish_fast(normed, rows_of[0][0], squares, peer_trade(terms))
    ends_zero, squares_zero = (hat, scale), jnp.sum(squares[:3], -1)

    low, blocks = project(1, hidden, attn_one)
    attend_one, pieces = attend_blocks(blocks)
    feed_one = after(feed_one, attend_one[2])
    feed_one = [feed_one, core_swap(feed_one)]
    hidden, feed_saved_one, acts_one, squares_one = feed(
        1, hidden, low, pieces, attn_one[4:] + feed_one
    )
    packs = [attn, attn_one + feed_one]
    kept = [(attend_zero, None, acts_zero), (attend_one, feed_saved_one, acts_one)]
    collected = [squares_zero, squares_one]
    elements = count * width * lax.axis_size("dp") * lax.axis_size("seq")
    hidden_output = move_back(hidden.astype(BF), perm)

    totals = jnp.stack(collected)
    sum_steps = [("seq", 1), ("seq", 2), ("seq", 4), ("dp", 1), ("dp", 2)]
    sum_steps = [step for step in sum_steps if step[1] < lax.axis_size(step[0])]

    def sum_more(totals, token):
        if sum_steps:
            axis, bit = sum_steps.pop(0)
            size = lax.axis_size(axis)
            pairs = [(i, i ^ bit) for i in range(size)]
            totals = totals + lax.ppermute(after(totals, token), axis, pairs)
        return totals

    def scatter_feed(term):
        part = lax.psum_scatter(term, "dp", scatter_dimension=0, tiled=True)
        part = lax.psum_scatter(
            part, "seq", scatter_dimension=0, tiled=True, axis_index_groups=core_groups()
        )
        return part.astype(F32)

    def back_feed(layer, grad):
        (_, feed_saved, acts), weights = kept[layer], packs[layer]
        grad_one, gave, attn_nat, sums, grads = feed_back_fast(
            layer, chips, grad, perm, perm_wide, rows_of[layer][0], feed_saved,
            weights[4:],
        )
        grads = [grads[0]] + [chip_shift(grads[step], step) for step in range(1, chips)]
        _, _, normed, act, theirs = acts
        feed_term = feed_terms_fast(normed, act, gave, theirs, core_swap(gave))
        return grad_one, attn_nat, sums, grads, feed_term

    def back_attend(layer, grads):
        blocks, others, mixed, logs = kept[layer][0]
        return attend_back_fast(chips, blocks, others, grads, mixed, logs)

    def back_combine(grad_q, near, far):
        pieces = combine_fast(chips, grad_q, near, far)
        return [pieces[0]] + [chip_shift(pieces[step], -step) for step in range(1, chips)]

    def back_project(layer, grad_one, sums, pieces):
        return project_back_fast(layer, chips, grad_one, perm, sums, pieces, packs[layer][:8])

    def back_terms(layer, project_grad, attn_nat, vector, far):
        low, attended, _, _, theirs = kept[layer][2]
        return attend_terms_fast(
            low, attended, project_grad, attn_nat, vector, theirs, *far
        )

    def swap_all(*members):
        return [core_swap(member) for member in members]

    grad_one, attn_nat, sums, grads, feed_term = back_feed(1, output_grad[0])
    totals = sum_more(totals, grad_one)
    feed_sum_one = lax.psum_scatter(feed_term, "dp", scatter_dimension=0, tiled=True)
    grads[0] = after(grads[0], feed_term, totals, hidden_output)
    grad_q, near, far = back_attend(1, grads)
    totals = sum_more(totals, grad_q)
    pieces = back_combine(after(grad_q, totals), near, core_swap(far))
    totals = sum_more(totals, pieces[0])
    pieces[0] = after(pieces[0], totals)
    grad, project_grad, vector = back_project(1, grad_one, sums, pieces)
    far_one = swap_all(project_grad, attn_nat, vector)
    terms_args = (project_grad, attn_nat, vector)

    attn_terms = back_terms(1, *terms_args, far_one)
    rows = rows_of[0][0]
    totals = sum_more(totals, grad)
    grad_two, grad_low, sums = finish_back_fast(False, grad, perm, rows, *ends_zero)
    blocks = peer_gather(grad_low)
    blocks[2] = after(blocks[2], totals)
    blocks[1] = after(blocks[1], feed_sum_one, attn_terms[0])
    feed_sum_one = chips_scatter(feed_sum_one).astype(F32)
    inputs, pre, act = slice_saved
    terms, slope, gave, feed_sums = slice_back_fast(blocks, inputs, pre, act, slice_pieces)
    totals = sum_more(totals, slope)
    terms = peer_trade(terms)
    terms[0] = after(terms[0], totals)
    grad_one, attn_nat, sums, grads = mix_back_fast(
        chips, grad_two, perm, rows, *norms_zero, sums, terms, attn[4:]
    )
    grads = [grads[0]] + [chip_shift(grads[step], step) for step in range(1, chips)]
    attn_terms = [
        attn_terms[0], after(attn_terms[1], grad_one), attn_terms[2], after(attn_terms[3], grad_one)
    ]
    grads[0] = after(grads[0], feed_sum_one)
    grad_q, near, far = back_attend(0, grads)
    feed_term = slice_terms_fast(
        perm_rows, perm_units, blocks, inputs, act, after(slope, grad_q), core_swap(gave)
    )
    feed_sum_zero = chips_scatter(feed_term)
    attn_terms[0] = after(attn_terms[0], grad_q)
    folded = square_fold(attn_terms)
    pieces = back_combine(after(grad_q, folded[0]), near, core_swap(far))
    split_one = square_split(folded)
    pieces[0] = after(pieces[0], split_one[0], feed_term)
    project_grad, vector = collect_fast(chips, perm, perm_wide, feed_sums, sums, pieces)
    far_zero = swap_all(project_grad, attn_nat, vector)
    attn_terms = list(back_terms(0, project_grad, attn_nat, vector, far_zero))
    folded = square_fold(attn_terms)
    input_grad = input_back_fast(after(grad_one, folded[0]), perm, project_grad, attn)
    split_one = [after(split_one[0], folded[0]), *split_one[1:]]
    attn_sum_one = square_total(split_one)
    feed_sum_zero = after(feed_sum_zero, folded[0])
    expand_sums = peer_trade(
        [
            lax.dynamic_slice(
                feed_sum_zero, (jnp.bitwise_xor(spot, bits) * share, 0), (share, width)
            )
            for bits in range(4)
        ]
    )
    expand_zero = jnp.concatenate(
        [
            matmul_t(
                lax.select_n(spot, *[expand_sums[index ^ other] for other in range(4)]), perm_wide
            )
            for index in range(groups)
        ],
        1,
    )
    shrink_zero = matmul_t(feed_sum_zero[:, width:], perm)
    folded = [after(folded[0], input_grad, *expand_sums, shrink_zero), *folded[1:]]
    attn_sum_zero = square_total(square_split(folded))
    terms = [(attn_sum_zero, None), (attn_sum_one, None)]
    expand_grads = [expand_zero, feed_sum_one[:, :wide]]
    shrink_grads = [shrink_zero, feed_sum_one[:, wide:].reshape(wide_share, width)]
    grad = input_grad
    root_squares = jnp.sqrt(totals / elements)
    vector_grad = jnp.stack(
        [
            (
                terms[layer][0][:, 4 * width : 4 * width + VECS]
                + terms[layer][0][:, 4 * width + 16 : 4 * width + 16 + VECS]
            ).T
            for layer in range(LAYERS)
        ]
    )
    return (
        hidden_output[None],
        grad[None],
        jnp.stack([terms[layer][0][:, : 3 * width] for layer in range(LAYERS)]),
        jnp.stack([terms[layer][0][:, 3 * width : 4 * width] for layer in range(LAYERS)]),
        jnp.stack(expand_grads),
        jnp.stack(shrink_grads),
        vector_grad,
        root_squares,
    )


def per_device(*args):
    chips = chips_of()
    if chips in (2, 4) and HEADS % chips == 0 and lax.axis_size("dp") == 4:
        return fast_device(*args)
    return plain_device(*args)


def solution(mesh):
    return jax.shard_map(
        per_device,
        mesh=mesh,
        in_specs=(
            P("dp", "seq", None),
            P(None, ("dp", "seq"), None),
            P(None, ("dp", "seq"), None),
            P(None, ("dp", "seq"), None),
            P(None, ("dp", "seq"), None),
            P(None, None, ("dp", "seq")),
            P("dp", "seq", None),
        ),
        out_specs=(
            P("dp", "seq", None),
            P("dp", "seq", None),
            P(None, ("dp", "seq"), None),
            P(None, ("dp", "seq"), None),
            P(None, ("dp", "seq"), None),
            P(None, ("dp", "seq"), None),
            P(None, None, ("dp", "seq")),
            P(),
        ),
        check_vma=False,
    )
```

```python
import functools
import math

import jax
import jax.numpy as jnp
import numpy as np
from jax import lax
from jax.experimental import pallas as pl
from jax.experimental.pallas import tpu as pltpu
from jax.sharding import PartitionSpec as P

HEADS = 12
HEAD = 64
LAYERS = 2
VECS = 12
LANES = 128

EPSILON = 1e-12
ROOT_HALF = 2.0 ** -0.5
ROOT_TAU = (2.0 * math.pi) ** -0.5

BF = jnp.bfloat16
F32 = jnp.float32


def layer_norm(residual, gain_row, shift_row):
    center = residual - jnp.mean(residual, -1, keepdims=True)
    spread = jnp.mean(center * center, -1, keepdims=True)
    return center * lax.rsqrt(spread + EPSILON) * gain_row + shift_row


def gelu_exact(values):
    return jax.nn.gelu(values, approximate=False)


def matmul(left, right):
    return jnp.dot(left, right, preferred_element_type=F32)


def matmul_t(left, right):
    return lax.dot_general(left, right, (((1,), (1,)), ((), ())), preferred_element_type=F32)


def grad_matmul(left, right):
    return lax.dot_general(left, right, (((0,), (0,)), ((), ())), preferred_element_type=F32)


def chips_of():
    return lax.axis_size("seq") // 2


def core_swap(array):
    size = lax.axis_size("seq")
    return lax.ppermute(array, "seq", [(i, i ^ 1) for i in range(size)])


def chip_shift(array, step):
    size = lax.axis_size("seq")
    chips = size // 2
    pairs = [(i, ((i // 2 + step) % chips) * 2 + i % 2) for i in range(size)]
    return lax.ppermute(array, "seq", pairs)


def core_groups():
    size = lax.axis_size("seq")
    return [list(range(0, size, 2)), list(range(1, size, 2))]


def place():
    spot = lax.axis_index("seq")
    return spot // 2, spot % 2


def gather_chips(array):
    chips = chips_of()
    if chips > 4:
        return lax.all_gather(
            array, "seq", axis=0, tiled=True, axis_index_groups=core_groups()
        )
    chip, _ = place()
    rows = array.shape[0]
    whole = jnp.zeros((chips * rows, array.shape[1]), array.dtype)
    for step in range(chips):
        part = array if step == 0 else chip_shift(array, step)
        whole = lax.dynamic_update_slice(whole, part, (((chip - step) % chips) * rows, 0))
    return whole


def gather_weight(array):
    own = lax.all_gather(gather_chips(array), "dp", axis=0, tiled=True)
    return join_cores(own, core_swap(own), 0)


def join_cores(own, other, axis):
    _, core = place()
    return jnp.where(
        core == 0,
        jnp.concatenate([own, other], axis),
        jnp.concatenate([other, own], axis),
    )


def scatter_chips(array):
    chips = chips_of()
    if chips > 4:
        return lax.psum_scatter(
            array, "seq", scatter_dimension=0, tiled=True, axis_index_groups=core_groups()
        ).astype(F32)
    chip, _ = place()
    rows = array.shape[0] // chips
    total = None
    for step in range(chips):
        part = lax.dynamic_slice(
            array, (((chip + step) % chips) * rows, 0), (rows, array.shape[1])
        )
        if step > 0:
            part = chip_shift(part, step)
        total = part.astype(F32) if total is None else total + part.astype(F32)
    return total


def scatter_grad(array):
    part = lax.psum_scatter(array.astype(BF), "dp", scatter_dimension=0, tiled=True)
    return scatter_chips(part)


def half_of(array, index):
    width = array.shape[1] // 2
    return lax.dynamic_slice(array, (0, index * width), (array.shape[0], width))


def one_hot(goal):
    return jnp.asarray(np.asarray(goal[:, None] == np.arange(goal.size)[None], np.float32), BF)


def swap_matrix(width, block):
    spot = np.arange(width)
    return one_hot(
        ((spot // block) % 2) * (width // 2) + (spot // (2 * block)) * block + spot % block
    )


def move(array, matrix):
    return jnp.dot(array, matrix, preferred_element_type=F32).astype(BF)


def move_back(array, matrix):
    return matmul_t(array, matrix).astype(BF)


def attend(queries, key_rows, value_rows):
    count = queries.shape[1] // HEAD
    outs = []
    logs = []
    for head in range(count):
        cut = slice(head * HEAD, (head + 1) * HEAD)
        scores = matmul_t(queries[:, cut], key_rows[:, cut])
        top = jnp.max(scores, -1, keepdims=True)
        log_total = top + jnp.log(jnp.sum(jnp.exp(scores - top), -1, keepdims=True))
        probability = jnp.exp(scores - log_total).astype(BF)
        outs.append(matmul(probability, value_rows[:, cut]))
        logs.append(log_total)
    return jnp.concatenate(outs, 1), jnp.concatenate(logs, 1)


def attend_back(queries, key_rows, value_rows, logs, mixed, grad_mixed):
    count = queries.shape[1] // HEAD
    grad_q, grad_k, grad_v = [], [], []
    for head in range(count):
        cut = slice(head * HEAD, (head + 1) * HEAD)
        grad_head = grad_mixed[:, cut]
        delta = jnp.sum(grad_head.astype(F32) * mixed[:, cut], -1, keepdims=True)
        probability = jnp.exp(
            matmul_t(queries[:, cut], key_rows[:, cut]) - logs[:, head : head + 1]
        )
        grad_prob = matmul_t(grad_head, value_rows[:, cut])
        grad_scores = (probability * (grad_prob - delta)).astype(BF)
        grad_q.append(matmul(grad_scores, key_rows[:, cut]))
        grad_k.append(grad_matmul(grad_scores, queries[:, cut]))
        grad_v.append(grad_matmul(probability.astype(BF), grad_head))
    return (
        jnp.concatenate(grad_q, 1).astype(BF),
        jnp.concatenate(grad_k + grad_v, 1).astype(BF),
    )


def forward_layer(hidden, params, perm):
    triple, mixer, expand, shrink, vectors, head_bias, ffn_bias = params
    rows, width = hidden.shape
    half = width // 2
    _, core = place()
    low = hidden.astype(BF)
    project = matmul(low, triple)
    queries = ((project[:, :width] + head_bias[0]) * 0.125).astype(BF)
    key_rows = project[:, width : 2 * width].astype(BF)
    value_rows = (project[:, 2 * width :] + head_bias[1]).astype(BF)
    trio = (queries, key_rows, value_rows)
    mine = jnp.concatenate([half_of(member, core) for member in trio], 1)
    sent = jnp.concatenate([half_of(member, 1 - core) for member in trio], 1)
    pair = jnp.concatenate([mine, core_swap(sent)], 0)
    pair_queries = pair[:, :half]
    pair_rest = pair[:, half:]
    chips = chips_of()
    if chips > 4:
        keyed = gather_chips(pair_rest)
    else:
        keyed = jnp.concatenate(
            [pair_rest] + [chip_shift(pair_rest, step) for step in range(1, chips)], 0
        )
    mixed, logs = attend(pair_queries, keyed[:, :half], keyed[:, half:])
    mixed_low = mixed.astype(BF)
    other = core_swap(mixed_low[rows:])
    attended = move(join_cores(mixed_low[:rows], other, 1), perm)
    attn_out = matmul(attended, mixer) + vectors[2]
    residual_one = hidden + attn_out
    normed = layer_norm(residual_one, vectors[3], vectors[4])
    normed_low = normed.astype(BF)
    pre_act = matmul(normed_low, expand) + ffn_bias
    act_low = gelu_exact(pre_act).astype(BF)
    ffn_out = matmul(act_low, shrink) + vectors[9]
    residual_two = normed + ffn_out
    output = layer_norm(residual_two, vectors[10], vectors[11])
    squares = jnp.stack(
        [jnp.sum(hidden * hidden), jnp.sum(attn_out * attn_out), jnp.sum(ffn_out * ffn_out)]
    )
    saved = (
        low, pair_queries, keyed, logs, mixed, attended,
        residual_one, normed_low, pre_act, act_low, residual_two,
    )
    return output, saved, squares


def backward_layer(grad_output, params, saved, perm, perm_wide):
    triple, mixer, expand, shrink, vectors, head_bias, ffn_bias = params
    (
        low, pair_queries, keyed, logs, mixed, attended,
        residual_one, normed_low, pre_act, act_low, residual_two,
    ) = saved
    rows, width = low.shape
    half = width // 2
    chips = chips_of()
    _, core = place()
    acts = jnp.concatenate(
        [half_of(member, 1 - core) for member in (low, attended, normed_low, act_low)], 1
    )
    acts = core_swap(acts)
    low_pair = jnp.concatenate([half_of(low, core), acts[:, :half]], 0)
    attended_pair = jnp.concatenate([half_of(attended, core), acts[:, half : 2 * half]], 0)
    normed_pair = jnp.concatenate([half_of(normed_low, core), acts[:, 2 * half : 3 * half]], 0)
    act_pair = jnp.concatenate([half_of(act_low, core), acts[:, 3 * half :]], 0)

    _, pull_two = jax.vjp(layer_norm, residual_two, vectors[10], vectors[11])
    grad_two, grad_gain_two, grad_shift_two = pull_two(grad_output)
    grad_ffn = grad_two.astype(BF)
    grad_act = matmul_t(grad_ffn, shrink)
    _, pull_gelu = jax.vjp(gelu_exact, pre_act)
    grad_pre = pull_gelu(grad_act)[0].astype(BF)
    grad_normed = grad_two + matmul_t(grad_pre, expand)
    _, pull_one = jax.vjp(layer_norm, residual_one, vectors[3], vectors[4])
    grad_one, grad_gain_one, grad_shift_one = pull_one(grad_normed)
    grad_attn = grad_one.astype(BF)
    grad_attended = move_back(matmul_t(grad_attn, mixer).astype(BF), perm)

    grad_ffn_nat = move_back(grad_ffn, perm)
    grad_attn_nat = move_back(grad_attn, perm)
    quarter = grad_pre.reshape(rows, 2, -1, half).transpose(0, 2, 1, 3).reshape(-1, width)
    grad_pre_nat = move_back(quarter, perm_wide).reshape(rows, -1)
    gave = jnp.concatenate([grad_ffn_nat, grad_pre_nat], 1)
    pair_ffn = jnp.concatenate([gave, core_swap(gave)], 0)
    grad_shrink = grad_matmul(act_pair, pair_ffn[:, :width])
    grad_expand = grad_matmul(normed_pair, pair_ffn[:, width:])

    other = core_swap(half_of(grad_attended, 1 - core))
    pair_grad = jnp.concatenate([half_of(grad_attended, core), other], 0)
    grad_q, grad_kv = attend_back(
        pair_queries, keyed[:, :half], keyed[:, half:], logs, mixed, pair_grad
    )
    span = 2 * rows
    if chips > 4:
        grad_kv = scatter_chips(grad_kv)
    else:
        total = grad_kv[:span].astype(F32)
        for step in range(1, chips):
            total = total + chip_shift(
                grad_kv[step * span : (step + 1) * span], -step
            ).astype(F32)
        grad_kv = total
    mine = jnp.concatenate([grad_q * 0.125, grad_kv.astype(BF)], 1)
    theirs = core_swap(mine)
    theirs = jnp.concatenate([theirs[rows:], theirs[:rows]], 0)
    pair_project = jnp.concatenate(
        [
            join_cores(mine[:, i * half : (i + 1) * half], theirs[:, i * half : (i + 1) * half], 1)
            for i in range(3)
        ],
        1,
    )
    grad_hidden = grad_one + matmul_t(pair_project[:rows], triple)
    grad_triple = grad_matmul(low_pair, pair_project)
    attn_pair = jnp.concatenate([grad_attn_nat, core_swap(grad_attn_nat)], 0)
    grad_mixer = grad_matmul(attended_pair, attn_pair)

    def sums(array):
        return jnp.sum(array.astype(F32), 0)

    bias_rows = jnp.concatenate(
        [
            sums(pair_project[:rows, :width])[None],
            sums(pair_project[:rows, 2 * width :])[None],
            sums(grad_pre_nat).reshape(-1, width),
        ],
        0,
    )
    count = width // (2 * lax.axis_size("dp") * chips)
    bias_rows = (
        bias_rows.reshape(bias_rows.shape[0], -1, 2, count)
        .transpose(0, 2, 1, 3)
        .reshape(bias_rows.shape)
    )
    grad_vector = jnp.concatenate(
        [
            bias_rows[:2],
            sums(grad_attn)[None],
            grad_gain_one[None],
            grad_shift_one[None],
            bias_rows[2:],
            sums(grad_ffn)[None],
            grad_gain_two[None],
            grad_shift_two[None],
        ],
        0,
    )
    grad_vector = half_of(grad_vector, core) + core_swap(half_of(grad_vector, 1 - core))
    high = grad_vector.astype(BF)
    rest = (grad_vector - high.astype(F32)).astype(BF)
    extra = jnp.concatenate([high, rest], 0).T
    extra = jnp.pad(extra, ((0, 0), (0, LANES - extra.shape[1])))
    attn_terms = jnp.concatenate([grad_triple.astype(BF), grad_mixer.astype(BF), extra], 1)
    return grad_hidden, attn_terms, grad_expand.astype(BF), grad_shrink.astype(BF)


def total_of(value):
    for axis in ("seq", "dp"):
        size = lax.axis_size(axis)
        step = 1
        while step < size:
            value = value + lax.ppermute(value, axis, [(i, i ^ step) for i in range(size)])
            step *= 2
    return value


def plain_device(
    hidden_input,
    triple_weight,
    mixer_weight,
    expand_weight,
    shrink_weight,
    vector_params,
    output_grad,
):
    _, count, width = hidden_input.shape
    share = triple_weight.shape[1]
    wide_share = shrink_weight.shape[1]
    wide = expand_weight.shape[2]
    groups = wide // width
    perm = swap_matrix(width, share)
    perm_wide = swap_matrix(width, wide_share)

    mixer_moved = move(mixer_weight.reshape(-1, width), perm).reshape(mixer_weight.shape)
    shrink_moved = move(shrink_weight.reshape(-1, width), perm).reshape(shrink_weight.shape)
    expand_moved = move(expand_weight.reshape(-1, width), perm_wide)
    expand_moved = (
        expand_moved.reshape(LAYERS * share, groups, 2, width // 2)
        .transpose(0, 2, 1, 3)
        .reshape(expand_weight.shape)
    )
    vector_columns = vector_params.reshape(LAYERS * VECS, share).T
    vector_columns = jnp.pad(vector_columns, ((0, 0), (0, LANES - LAYERS * VECS)))
    packs = []
    for layer in range(LAYERS):
        attn = [triple_weight[layer], mixer_moved[layer]]
        if layer == 0:
            attn.append(vector_columns)
        packs.append(
            (
                gather_weight(jnp.concatenate(attn, 1)),
                gather_weight(expand_moved[layer]),
                gather_weight(shrink_moved[layer]),
            )
        )
    vectors = packs[0][0][:, 4 * width : 4 * width + LAYERS * VECS].T
    natural = move_back(vectors, perm)
    params = []
    for layer in range(LAYERS):
        rows = vectors[layer * VECS : (layer + 1) * VECS].astype(F32)
        plain = natural[layer * VECS : (layer + 1) * VECS]
        ffn_bias = (
            move(plain[5 : 5 + groups], perm_wide)
            .reshape(groups, 2, width // 2)
            .transpose(1, 0, 2)
            .reshape(1, wide)
        ).astype(F32)
        attn, expand, shrink = packs[layer]
        params.append(
            (
                attn[:, : 3 * width],
                attn[:, 3 * width : 4 * width],
                expand,
                shrink,
                rows,
                plain[:2].astype(F32),
                ffn_bias,
            )
        )

    hidden = matmul(hidden_input[0], perm)
    kept = []
    collected = []
    for layer in range(LAYERS):
        hidden, saved, squares = forward_layer(hidden, params[layer], perm)
        kept.append(saved)
        collected.append(squares)
    elements = count * width * lax.axis_size("dp") * lax.axis_size("seq")
    root_squares = jnp.sqrt(total_of(jnp.stack(collected)) / elements)
    hidden_output = move_back(hidden.astype(BF), perm)

    grad = matmul(output_grad[0], perm)
    terms = [None] * LAYERS
    for layer in reversed(range(LAYERS)):
        grad, attn, expand, shrink = backward_layer(
            grad, params[layer], kept[layer], perm, perm_wide
        )
        terms[layer] = (scatter_grad(attn), scatter_grad(expand), scatter_grad(shrink))
    input_grad = move_back(grad.astype(BF), perm)
    vector_grad = jnp.stack(
        [
            (
                terms[layer][0][:, 4 * width : 4 * width + VECS]
                + terms[layer][0][:, 4 * width + VECS : 4 * width + 2 * VECS]
            ).T
            for layer in range(LAYERS)
        ]
    )
    return (
        hidden_output[None],
        input_grad[None],
        jnp.stack([terms[layer][0][:, : 3 * width] for layer in range(LAYERS)]),
        jnp.stack([terms[layer][0][:, 3 * width : 4 * width] for layer in range(LAYERS)]),
        jnp.stack([terms[layer][1] for layer in range(LAYERS)]),
        jnp.stack([terms[layer][2] for layer in range(LAYERS)]),
        vector_grad,
        root_squares,
    )


ANY = pl.BlockSpec(memory_space=pl.ANY)
VMEM = pl.BlockSpec(memory_space=pltpu.VMEM)
VMEM_BYTES = 56 * 1024 * 1024
HINT = 2
SIDE_HINT = 40
SIDE = ("feed_terms", "attend_terms", "slice_terms", "fold", "split", "input_back")


def shape(dims, kind):
    return jax.ShapeDtypeStruct(dims, kind)


def run(kernel, name, outs, placed, streamed=(), scratch=(), flops=0):
    hint = SIDE_HINT if name in SIDE else HINT
    size = sum(
        math.prod(member.shape) * member.dtype.itemsize
        for member in [*outs, *placed, *streamed]
    )
    return pl.pallas_call(
        kernel,
        name=name,
        out_shape=list(outs),
        in_specs=[VMEM] * len(placed) + [ANY] * len(streamed),
        out_specs=[VMEM] * len(outs),
        scratch_shapes=list(scratch),
        compiler_params=pltpu.CompilerParams(vmem_limit_bytes=VMEM_BYTES),
        cost_estimate=pl.CostEstimate(
            flops=int(flops * hint), bytes_accessed=int(size * hint), transcendentals=0
        ),
    )(*placed, *streamed)


def spot_in():
    index = lax.axis_index("seq")
    return index // 2, index % 2


def fetch_left(pieces, target, sems, columns, goal):
    _, core = spot_in()
    _, high = dp_place()
    rows = pieces[0].shape[0]
    copies = []
    for index, piece in enumerate(pieces):
        part = core if index < 2 else 1 - core
        side = high if index % 2 == 0 else 1 - high
        start = pl.multiple_of((part * 2 + side) * rows, 16)
        copy = pltpu.make_async_copy(
            piece.at[:, columns], target.at[pl.ds(start, rows), goal], sems.at[index]
        )
        copy.start()
        copies.append(copy)
    return copies


def fetch_whole(pieces, target, sems, columns, goal):
    _, core = spot_in()
    rows = pieces[0].shape[0]
    copies = []
    for index, piece in enumerate(pieces):
        part = core if index == 0 else 1 - core
        start = pl.multiple_of(part * rows, 16)
        copy = pltpu.make_async_copy(
            piece.at[:, columns], target.at[pl.ds(start, rows), goal], sems.at[index]
        )
        copy.start()
        copies.append(copy)
    return copies


def fetch_right(pieces, target, sems, columns, goal):
    _, core = spot_in()
    bit, _ = dp_place()
    rows = pieces[0].shape[0] // 2
    copies = []
    for index, piece in enumerate(pieces):
        part = core if index < 2 else 1 - core
        side = bit if index % 2 == 0 else 1 - bit
        for row in range(2):
            start = pl.multiple_of((part * 4 + row * 2 + side) * rows, 16)
            copy = pltpu.make_async_copy(
                piece.at[row * rows : (row + 1) * rows, columns],
                target.at[pl.ds(start, rows), goal],
                sems.at[2 * index + row],
            )
            copy.start()
            copies.append(copy)
    return copies


def wait_all(copies):
    for copy in copies:
        copy.wait()


def half_at(ref, part):
    half = ref.shape[1] // 2
    return ref[:, pl.ds(pl.multiple_of(part * half, LANES), half)]


def column_sum(values):
    return jnp.sum(values, 0, keepdims=True)


def fetch_project(layer, pieces, weight, left_sems, right_sems, width):
    if len(pieces) == 2:
        every = slice(0, 3 * width)
        return fetch_whole(pieces, weight, left_sems, every, every)
    first, last = slice(0, 2 * width), slice(2 * width, 3 * width)
    copies = fetch_left(pieces[:4], weight, left_sems, first, first)
    return copies + fetch_right(pieces[4:], weight, right_sems, slice(0, width), last)


def plain_rows(columns, perm):
    return lax.dot_general(
        columns, perm, (((0,), (1,)), ((), ())), preferred_element_type=F32
    )


def project_kernel(layer, chips, many, source, perm, bias, *rest):
    pieces, low_out, rest = rest[:many], rest[many], rest[many + 1 :]
    outs, (weight, stage, columns, *sems) = rest[:chips], rest[chips:]
    left_sems, right_sems, column_sems = sems
    chip, _ = spot_in()
    width = perm.shape[0]
    copies = fetch_project(layer, pieces, weight, left_sems, right_sems, width)
    if layer == 0:
        start = pieces[4].shape[1] - LANES
        column_copies = fetch_right(
            pieces[4:], columns, column_sems, slice(start, start + LANES), slice(0, LANES)
        )
        low = matmul(source[...], perm[...]).astype(BF)
        wait_all(column_copies)
        bias = plain_rows(columns[...], perm[...])
    else:
        low = source[...].astype(BF)
    low_out[...] = low
    wait_all(copies)
    group = width // chips
    for section in range(3):
        part = matmul(low, weight[:, section * width : (section + 1) * width])
        if section == 0:
            part = (part + bias[0:1]) * 0.125
        if section == 2:
            part = part + bias[1:2]
        part = part.astype(BF)
        for index in range(chips):
            stage[index, :, section * group : (section + 1) * group] = part[
                :, index * group : (index + 1) * group
            ]
    for step in range(chips):
        outs[step][...] = stage[lax.rem(chip + step, chips)]


def project_fast(layer, chips, source, perm, bias, pieces):
    rows, width = source.shape
    group = 3 * width // chips
    out = run(
        functools.partial(project_kernel, layer, chips, len(pieces)),
        "project",
        [shape((rows, width), BF)] + [shape((rows, group), BF)] * chips,
        [source, perm, bias],
        pieces,
        [
            pltpu.VMEM((width, 3 * width), BF),
            pltpu.VMEM((chips, rows, group), BF),
            pltpu.VMEM((width, LANES), BF),
            pltpu.SemaphoreType.DMA((4,)),
            pltpu.SemaphoreType.DMA((8,)),
            pltpu.SemaphoreType.DMA((8,)),
        ],
        flops=6 * rows * width * width,
    )
    return out[0], out[1:]


def fill_heads(blocks, others, group, queries, keys, values):
    rows = blocks[0].shape[0]
    for index, block in enumerate(blocks):
        cut = slice(index * rows, (index + 1) * rows)
        queries[cut, :] = block[:, :group]
        keys[cut, :] = block[:, group : 2 * group]
        values[cut, :] = block[:, 2 * group :]
    base = len(blocks) * rows
    for index, block in enumerate(others):
        cut = slice(base + index * rows, base + (index + 1) * rows)
        keys[cut, :] = block[:, group : 2 * group]
        values[cut, :] = block[:, 2 * group :]


def chunks_of(total):
    size = min(total, 256)
    return [slice(start, start + size) for start in range(0, total, size)]


def attend_kernel(chips, *refs):
    blocks, others = refs[:chips], refs[chips : 2 * chips]
    mixed, logs = refs[2 * chips : 2 * chips + 2]
    outs = refs[2 * chips + 2 : 3 * chips + 2]
    queries, keys, values = refs[3 * chips + 2 :]
    rows = blocks[0].shape[0]
    group = queries.shape[1]
    fill_heads(blocks, others, group, queries, keys, values)
    for head in range(group // HEAD):
        cut = slice(head * HEAD, (head + 1) * HEAD)
        key_head = keys[:, cut]
        value_head = values[:, cut]
        for part in chunks_of(chips * rows):
            scores = matmul_t(queries[part, cut], key_head)
            top = jnp.max(scores, -1, keepdims=True)
            power = jnp.exp(scores - top)
            total = jnp.sum(power, -1, keepdims=True)
            mixed[part, cut] = matmul(power.astype(BF), value_head) * (1.0 / total)
            logs[part, head : head + 1] = top + jnp.log(total)
    for index in range(chips):
        outs[index][...] = mixed[index * rows : (index + 1) * rows, :].astype(BF)


def attend_fast(chips, blocks, others):
    rows, wide = blocks[0].shape
    group = wide // 3
    span = chips * rows
    out = run(
        functools.partial(attend_kernel, chips),
        "attend",
        [shape((span, group), F32), shape((span, LANES), F32)]
        + [shape((rows, group), BF)] * chips,
        [*blocks, *others],
        (),
        [
            pltpu.VMEM((span, group), BF),
            pltpu.VMEM((2 * span, group), BF),
            pltpu.VMEM((2 * span, group), BF),
        ],
        flops=8 * span * span * group,
    )
    return out[0], out[1], out[2:]


def norm_in(residual):
    center = residual - jnp.mean(residual, -1, keepdims=True)
    spread = jnp.mean(center * center, -1, keepdims=True)
    scale = lax.rsqrt(spread + EPSILON)
    return center * scale, scale


def shrink_cut(index, wide, width):
    count = wide // width
    core, block = index // count, index % count
    half = width // 2
    return (
        slice(core * half, (core + 1) * half),
        slice(block * width, (block + 1) * width),
    )


def fetch_feed(weights, mixer, expand, shrink, sems):
    width, wide = expand.shape
    every, full = slice(0, width), slice(0, wide)
    return (
        fetch_right(weights[:4], mixer, sems[0], slice(width, 2 * width), every),
        fetch_whole(weights[4:], expand, sems[1], full, full),
        fetch_whole(weights[4:], shrink, sems[2], slice(wide, 2 * wide), full),
    )


def feed_kernel(layer, chips, many, hidden, low, perm, rows_in, wide_bias, *refs):
    pieces, refs = refs[:chips], refs[chips:]
    weights, refs = refs[:many], refs[many:]
    (out, attended, normed_low, pre_out, act_out, hat_one, scale_one, hat_two, scale_two,
     sent, squares) = refs[:11]
    stage, mixer, expand, shrink, *sems = refs[11:]
    chip, core = spot_in()
    width = perm.shape[0]
    wide = expand.shape[1]
    group = width // chips
    mixer_copies, expand_copies, shrink_copies = fetch_feed(
        weights, mixer, expand, shrink, sems
    )
    for step in range(chips):
        stage[lax.rem(chip + step, chips)] = pieces[step][...]
    moved = matmul(stage[0], perm[:group, :])
    for index in range(1, chips):
        moved += matmul(stage[index], perm[index * group : (index + 1) * group, :])
    moved = moved.astype(BF)
    attended[...] = moved
    wait_all(mixer_copies)
    attn_out = matmul(moved, mixer[...]) + rows_in[2:3]
    start = hidden[...].astype(F32)
    hat, scale = norm_in(start + attn_out)
    hat_one[...] = hat
    scale_one[...] = jnp.broadcast_to(scale, scale_one.shape)
    normed = hat * rows_in[3:4] + rows_in[4:5]
    normed_b = normed.astype(BF)
    normed_low[...] = normed_b
    squares[...] = jnp.zeros_like(squares)
    squares[0:1, :] = column_sum(start * start)
    squares[1:2, :] = column_sum(attn_out * attn_out)
    wait_all(expand_copies)
    wait_all(shrink_copies)
    half = width // 2
    total = None
    for index in range(wide // width):
        cut = slice(index * width, (index + 1) * width)
        pre = matmul(normed_b, expand[:, cut]) + wide_bias[:, cut]
        pre_out[:, cut] = pre
        act = (0.5 * pre * (1.0 + lax.erf(pre * ROOT_HALF))).astype(BF)
        act_out[:, cut] = act
        for side in range(2):
            rows, columns = shrink_cut(2 * index + side, wide, width)
            term = matmul(act[:, side * half : (side + 1) * half], shrink[rows, columns])
            total = term if total is None else total + term
    ffn_out = total + rows_in[9:10]
    squares[2:3, :] = column_sum(ffn_out * ffn_out)
    hat, scale = norm_in(normed + ffn_out)
    hat_two[...] = hat
    scale_two[...] = jnp.broadcast_to(scale, scale_two.shape)
    out[...] = hat * rows_in[10:11] + rows_in[11:12]
    for index, member in enumerate((low, attended, normed_low)):
        sent[:, index * half : (index + 1) * half] = half_at(member, 1 - core)
    sent[:, 3 * half :] = half_at(act_out, 1 - core)


def feed_fast(layer, chips, hidden, low, perm, vectors, wide_bias, pieces, weights):
    rows, width = hidden.shape
    wide = wide_bias.shape[1]
    return run(
        functools.partial(feed_kernel, layer, chips, len(weights)),
        "feed",
        [
            shape((rows, width), F32),
            shape((rows, width), BF),
            shape((rows, width), BF),
            shape((rows, wide), F32),
            shape((rows, wide), BF),
            shape((rows, width), F32),
            shape((rows, LANES), F32),
            shape((rows, width), F32),
            shape((rows, LANES), F32),
            shape((rows, (3 * width + wide) // 2), BF),
            shape((8, width), F32),
        ],
        [hidden, low, perm, vectors, wide_bias, *pieces],
        weights,
        [
            pltpu.VMEM((chips, rows, width // chips), BF),
            pltpu.VMEM((width, width), BF),
            pltpu.VMEM((width, wide), BF),
            pltpu.VMEM((width, wide), BF),
            pltpu.SemaphoreType.DMA((8,)),
            pltpu.SemaphoreType.DMA((4,)),
            pltpu.SemaphoreType.DMA((8,)),
        ],
        flops=4 * rows * width * (wide + width),
    )


def norm_back(grad, hat, scale):
    first = jnp.mean(grad, -1, keepdims=True)
    second = jnp.mean(grad * hat, -1, keepdims=True)
    return (grad - first - hat * second) * scale


def feed_back_kernel(
    layer, chips, many, source, perm, perm_wide, vectors, hat_one, scale_one, hat_two, scale_two,
    pre_in, *refs
):
    weights, refs = refs[:many], refs[many:]
    grad_one_out, gave, attn_nat, sums = refs[:4]
    outs = refs[4 : 4 + chips]
    stage, grad_pre, mixer, expand, shrink, *sems = refs[4 + chips :]
    chip, _ = spot_in()
    width = perm.shape[0]
    wide = expand.shape[1]
    group = width // chips
    half = width // 2
    mixer_copies, expand_copies, shrink_copies = fetch_feed(
        weights, mixer, expand, shrink, sems
    )
    grad = matmul(source[...], perm[...]) if layer == LAYERS - 1 else source[...]
    hat = hat_two[...]
    sums[...] = jnp.zeros_like(sums)
    sums[10:11, :] = column_sum(grad * hat)
    sums[11:12, :] = column_sum(grad)
    grad_two = norm_back(grad * vectors[10:11], hat, scale_two[:, 0:1])
    grad_ffn = grad_two.astype(BF)
    sums[9:10, :] = column_sum(grad_ffn.astype(F32))
    gave[:, :width] = matmul_t(grad_ffn, perm[...]).astype(BF)
    wait_all(shrink_copies)
    wait_all(expand_copies)
    grad_normed = grad_two
    for index in range(wide // width):
        cut = slice(index * width, (index + 1) * width)
        pre = pre_in[:, cut]
        slope = 0.5 * (1.0 + lax.erf(pre * ROOT_HALF)) + pre * (
            jnp.exp(-0.5 * pre * pre) * ROOT_TAU
        )
        sides = []
        for side in range(2):
            rows, columns = shrink_cut(2 * index + side, wide, width)
            sides.append(matmul_t(grad_ffn, shrink[rows, columns]))
        part = (jnp.concatenate(sides, 1) * slope).astype(BF)
        grad_pre[:, cut] = part
        grad_normed += matmul_t(part, expand[:, cut])
    groups = wide // width
    piece = half // groups
    for index in range(groups):
        joined = jnp.concatenate(
            [
                grad_pre[:, spot * half + index * piece : spot * half + (index + 1) * piece]
                for spot in range(2 * groups)
            ],
            1,
        )
        moved = matmul_t(joined, perm_wide[...])
        sums[5 + index : 6 + index, :] = column_sum(moved)
        gave[:, (index + 1) * width : (index + 2) * width] = moved.astype(BF)
    hat = hat_one[...]
    sums[3:4, :] = column_sum(grad_normed * hat)
    sums[4:5, :] = column_sum(grad_normed)
    grad_one = norm_back(grad_normed * vectors[3:4], hat, scale_one[:, 0:1])
    grad_one_out[...] = grad_one
    grad_attn = grad_one.astype(BF)
    sums[2:3, :] = column_sum(grad_attn.astype(F32))
    attn_nat[...] = matmul_t(grad_attn, perm[...]).astype(BF)
    wait_all(mixer_copies)
    grad_mixed = matmul_t(grad_attn, mixer[...]).astype(BF)
    for index in range(chips):
        stage[index] = matmul_t(
            grad_mixed, perm[index * group : (index + 1) * group, :]
        ).astype(BF)
    for step in range(chips):
        outs[step][...] = stage[lax.rem(chip + step, chips)]


def feed_back_fast(layer, chips, source, perm, perm_wide, vectors, saved, weights):
    rows, width = source.shape
    wide = saved[-1].shape[1]
    out = run(
        functools.partial(feed_back_kernel, layer, chips, len(weights)),
        "feed_back",
        [
            shape((rows, width), F32),
            shape((rows, width + wide), BF),
            shape((rows, width), BF),
            shape((16, width), F32),
        ]
        + [shape((rows, width // chips), BF)] * chips,
        [source, perm, perm_wide, vectors, *saved],
        weights,
        [
            pltpu.VMEM((chips, rows, width // chips), BF),
            pltpu.VMEM((rows, wide), BF),
            pltpu.VMEM((width, width), BF),
            pltpu.VMEM((width, wide), BF),
            pltpu.VMEM((width, wide), BF),
            pltpu.SemaphoreType.DMA((8,)),
            pltpu.SemaphoreType.DMA((4,)),
            pltpu.SemaphoreType.DMA((8,)),
        ],
        flops=4 * rows * width * (wide + 2 * width),
    )
    return out[0], out[1], out[2], out[3], out[4:]


def fetch_rows(pieces, target, sems, start):
    _, core = spot_in()
    rows, width = pieces[0].shape[0], target.shape[1]
    copies = []
    for index, piece in enumerate(pieces):
        part = core if index == 0 else 1 - core
        for block in range(4):
            goal = pl.multiple_of((part * 4 + block) * rows, 16)
            copy = pltpu.make_async_copy(
                piece.at[:, start + block * width : start + (block + 1) * width],
                target.at[pl.ds(goal, rows), :],
                sems.at[4 * index + block],
            )
            copy.start()
            copies.append(copy)
    return copies


def fetch_blocks(pieces, target, sems):
    _, core = spot_in()
    spot = lax.axis_index("dp")
    rows, width = pieces[0].shape[0], target.shape[1]
    copies = []
    for index, piece in enumerate(pieces):
        part = core if index == 0 else 1 - core
        for bits in range(4):
            goal = pl.multiple_of((part * 4 + jnp.bitwise_xor(spot, bits)) * rows, 16)
            copy = pltpu.make_async_copy(
                piece.at[:, bits * width : (bits + 1) * width],
                target.at[pl.ds(goal, rows), :],
                sems.at[4 * index + bits],
            )
            copy.start()
            copies.append(copy)
    return copies


def mix_kernel(chips, hidden, low, perm, rows_in, *refs):
    pieces, refs = refs[:chips], refs[chips:]
    weights, refs = refs[:4], refs[4:]
    attended, normed_out, normed_low, hat_one, scale_one, sent, squares = refs[:7]
    stage, mixer, sems = refs[7:]
    chip, core = spot_in()
    width = perm.shape[0]
    group = width // chips
    half = width // 2
    copies = fetch_right(weights, mixer, sems, slice(width, 2 * width), slice(0, width))
    for step in range(chips):
        stage[lax.rem(chip + step, chips)] = pieces[step][...]
    moved = matmul(stage[0], perm[:group, :])
    for index in range(1, chips):
        moved += matmul(stage[index], perm[index * group : (index + 1) * group, :])
    moved = moved.astype(BF)
    attended[...] = moved
    wait_all(copies)
    attn_out = matmul(moved, mixer[...]) + rows_in[2:3]
    start = hidden[...].astype(F32)
    hat, scale = norm_in(start + attn_out)
    hat_one[...] = hat
    scale_one[...] = jnp.broadcast_to(scale, scale_one.shape)
    normed = hat * rows_in[3:4] + rows_in[4:5]
    normed_out[...] = normed
    normed_low[...] = normed.astype(BF)
    squares[...] = jnp.zeros_like(squares)
    squares[0:1, :] = column_sum(start * start)
    squares[1:2, :] = column_sum(attn_out * attn_out)
    sent[:, :half] = half_at(low, 1 - core)
    sent[:, half:] = half_at(attended, 1 - core)


def mix_fast(chips, hidden, low, perm, vectors, pieces, weights):
    rows, width = hidden.shape
    return run(
        functools.partial(mix_kernel, chips),
        "mix",
        [
            shape((rows, width), BF),
            shape((rows, width), F32),
            shape((rows, width), BF),
            shape((rows, width), F32),
            shape((rows, LANES), F32),
            shape((rows, width), BF),
            shape((8, width), F32),
        ],
        [hidden, low, perm, vectors, *pieces],
        weights,
        [
            pltpu.VMEM((chips, rows, width // chips), BF),
            pltpu.VMEM((width, width), BF),
            pltpu.SemaphoreType.DMA((8,)),
        ],
        flops=4 * rows * width * width,
    )


def slice_row(wide_bias):
    spot = lax.axis_index("dp")
    line = lax.broadcasted_iota(jnp.int32, wide_bias.shape, 0)
    return jnp.sum(jnp.where(line == spot, wide_bias[...], 0.0), 0, keepdims=True)


def slice_feed_kernel(wide_bias, *refs):
    peers = 4
    blocks, weights, refs = refs[:peers], refs[peers : peers + 2], refs[peers + 2 :]
    near, sends, refs = refs[0], refs[1:peers], refs[peers:]
    pre_out, act_out, expand, shrink, expand_sems, shrink_sems = refs
    rows, width = blocks[0].shape
    expand_copies = fetch_blocks(weights, expand, expand_sems)
    shrink_copies = fetch_rows(weights, shrink, shrink_sems, 4 * width)
    bias = slice_row(wide_bias)
    wait_all(expand_copies)
    tokens = jnp.concatenate([block[...] for block in blocks], 0)
    pre = matmul(tokens, expand[...]) + bias
    pre_out[...] = pre
    act = (0.5 * pre * (1.0 + lax.erf(pre * ROOT_HALF))).astype(BF)
    act_out[...] = act
    wait_all(shrink_copies)
    part = matmul(act, shrink[...])
    near[...] = part[:rows]
    for index, out in enumerate(sends):
        out[...] = part[(index + 1) * rows : (index + 2) * rows].astype(BF)


def slice_scratch(width):
    return [
        pltpu.VMEM((width, width), BF),
        pltpu.VMEM((width, width), BF),
        pltpu.SemaphoreType.DMA((8,)),
        pltpu.SemaphoreType.DMA((8,)),
    ]


def slice_feed_fast(wide_bias, blocks, weights):
    rows, width = blocks[0].shape
    out = run(
        slice_feed_kernel,
        "slice_feed",
        [shape((rows, width), F32)]
        + [shape((rows, width), BF)] * 3
        + [shape((4 * rows, width), F32), shape((4 * rows, width), BF)],
        [wide_bias, *blocks],
        weights,
        slice_scratch(width),
        flops=16 * rows * width * width,
    )
    return out[:4], out[4], out[5]


def peer_sum(parts):
    total = parts[0][...]
    for part in parts[1:]:
        total = total + part[...].astype(F32)
    return total


def finish_kernel(normed, rows_in, squares_in, *refs):
    parts, (out, hat_two, scale_two, squares) = refs[:4], refs[4:]
    ffn_out = peer_sum(parts) + rows_in[9:10]
    squares[...] = squares_in[...]
    squares[2:3, :] = column_sum(ffn_out * ffn_out)
    hat, scale = norm_in(normed[...] + ffn_out)
    hat_two[...] = hat
    scale_two[...] = jnp.broadcast_to(scale, scale_two.shape)
    out[...] = hat * rows_in[10:11] + rows_in[11:12]


def finish_fast(normed, vectors, squares, parts):
    rows, width = normed.shape
    return run(
        finish_kernel,
        "finish",
        [
            shape((rows, width), F32),
            shape((rows, width), F32),
            shape((rows, LANES), F32),
            shape(squares.shape, F32),
        ],
        [normed, vectors, squares, *parts],
    )


def finish_back_kernel(first, source, perm, vectors, hat_two, scale_two, grad_out, low_out, sums):
    grad = matmul(source[...], perm[...]) if first else source[...]
    hat = hat_two[...]
    sums[...] = jnp.zeros_like(sums)
    sums[10:11, :] = column_sum(grad * hat)
    sums[11:12, :] = column_sum(grad)
    grad_two = norm_back(grad * vectors[10:11], hat, scale_two[:, 0:1])
    grad_out[...] = grad_two
    low = grad_two.astype(BF)
    low_out[...] = low
    sums[9:10, :] = column_sum(low.astype(F32))


def finish_back_fast(first, source, perm, vectors, hat_two, scale_two):
    rows, width = source.shape
    return run(
        functools.partial(finish_back_kernel, first),
        "finish_back",
        [shape((rows, width), F32), shape((rows, width), BF), shape((16, width), F32)],
        [source, perm, vectors, hat_two, scale_two],
    )


def slice_back_kernel(*refs):
    peers = 4
    blocks, refs = refs[:peers], refs[peers:]
    inputs, refs = refs[:peers], refs[peers:]
    pre_in, act_in, weights, refs = refs[0], refs[1], refs[2:4], refs[4:]
    near, sends, refs = refs[0], refs[1:peers], refs[peers:]
    slope_out, gave, sums, expand, shrink, expand_sems, shrink_sems = refs
    _, core = spot_in()
    rows, width = blocks[0].shape
    half = width // 2
    shrink_copies = fetch_rows(weights, shrink, shrink_sems, 4 * width)
    expand_copies = fetch_blocks(weights, expand, expand_sems)
    for index in range(peers):
        span = slice(index * rows, (index + 1) * rows)
        gave[span, :half] = half_at(inputs[index], 1 - core)
        gave[span, width : 2 * width] = blocks[index][...]
    gave[:, half:width] = half_at(act_in, 1 - core)
    tokens = jnp.concatenate([block[...] for block in blocks], 0)
    pre = pre_in[...]
    slope = 0.5 * (1.0 + lax.erf(pre * ROOT_HALF)) + pre * (
        jnp.exp(-0.5 * pre * pre) * ROOT_TAU
    )
    wait_all(shrink_copies)
    grad_pre = (matmul_t(tokens, shrink[...]) * slope).astype(BF)
    slope_out[...] = grad_pre
    gave[:, 2 * width :] = grad_pre
    sums[...] = jnp.broadcast_to(column_sum(grad_pre.astype(F32)), sums.shape)
    wait_all(expand_copies)
    part = matmul_t(grad_pre, expand[...])
    near[...] = part[:rows]
    for index, out in enumerate(sends):
        out[...] = part[(index + 1) * rows : (index + 2) * rows].astype(BF)


def slice_back_fast(blocks, inputs, pre, act, weights):
    rows, width = blocks[0].shape
    out = run(
        slice_back_kernel,
        "slice_back",
        [shape((rows, width), F32)]
        + [shape((rows, width), BF)] * 3
        + [
            shape((4 * rows, width), BF),
            shape((4 * rows, 3 * width), BF),
            shape((8, width), F32),
        ],
        [*blocks, *inputs, pre, act],
        weights,
        slice_scratch(width),
        flops=16 * rows * width * width,
    )
    return out[:4], out[4], out[5], out[6]


def slice_terms_kernel(peers, perm_rows, perm_units, *refs):
    blocks, inputs, refs = refs[:peers], refs[peers : 2 * peers], refs[2 * peers :]
    act_in, slope, theirs, out = refs
    _, core = spot_in()
    width = slope.shape[1]
    half = width // 2
    left = jnp.concatenate(
        [half_at(member, core) for member in inputs] + [theirs[:, :half]], 0
    )
    left = matmul(left, perm_rows[...]).astype(BF)
    right = jnp.concatenate([slope[...], theirs[:, 2 * width :]], 0)
    out[:, :width] = grad_matmul(left, right).astype(BF)
    left = jnp.concatenate([half_at(act_in, core), theirs[:, half:width]], 0)
    left = matmul(left, perm_units[...]).astype(BF)
    right = jnp.concatenate(
        [block[...] for block in blocks] + [theirs[:, width : 2 * width]], 0
    )
    out[:, width:] = grad_matmul(left, right).astype(BF)


def slice_terms_fast(perm_rows, perm_units, blocks, inputs, act, slope, theirs):
    rows, width = blocks[0].shape
    return run(
        functools.partial(slice_terms_kernel, 4),
        "slice_terms",
        [shape((width // 2, 2 * width), BF)],
        [perm_rows, perm_units, *blocks, *inputs, act, slope, theirs],
        flops=16 * rows * width * width,
    )[0]


def mix_back_kernel(chips, grad_two, perm, vectors, hat_one, scale_one, sums_in, *refs):
    parts, weights, refs = refs[:4], refs[4:8], refs[8:]
    grad_one_out, attn_nat, sums = refs[:3]
    outs = refs[3 : 3 + chips]
    stage, mixer, sems = refs[3 + chips :]
    chip, _ = spot_in()
    width = perm.shape[0]
    group = width // chips
    copies = fetch_right(weights, mixer, sems, slice(width, 2 * width), slice(0, width))
    grad_normed = grad_two[...] + peer_sum(parts)
    hat = hat_one[...]
    sums[...] = sums_in[...]
    sums[3:4, :] = column_sum(grad_normed * hat)
    sums[4:5, :] = column_sum(grad_normed)
    grad_one = norm_back(grad_normed * vectors[3:4], hat, scale_one[:, 0:1])
    grad_one_out[...] = grad_one
    grad_attn = grad_one.astype(BF)
    sums[2:3, :] = column_sum(grad_attn.astype(F32))
    attn_nat[...] = matmul_t(grad_attn, perm[...]).astype(BF)
    wait_all(copies)
    grad_mixed = matmul_t(grad_attn, mixer[...]).astype(BF)
    for index in range(chips):
        stage[index] = matmul_t(
            grad_mixed, perm[index * group : (index + 1) * group, :]
        ).astype(BF)
    for step in range(chips):
        outs[step][...] = stage[lax.rem(chip + step, chips)]


def mix_back_fast(chips, grad_two, perm, vectors, hat_one, scale_one, sums, parts, weights):
    rows, width = grad_two.shape
    out = run(
        functools.partial(mix_back_kernel, chips),
        "mix_back",
        [shape((rows, width), F32), shape((rows, width), BF), shape((16, width), F32)]
        + [shape((rows, width // chips), BF)] * chips,
        [grad_two, perm, vectors, hat_one, scale_one, sums, *parts],
        weights,
        [
            pltpu.VMEM((chips, rows, width // chips), BF),
            pltpu.VMEM((width, width), BF),
            pltpu.SemaphoreType.DMA((8,)),
        ],
        flops=6 * rows * width * width,
    )
    return out[0], out[1], out[2], out[3:]


def attend_back_kernel(chips, *refs):
    blocks, refs = refs[:chips], refs[chips:]
    others, refs = refs[:chips], refs[chips:]
    grads, refs = refs[:chips], refs[chips:]
    mixed, logs, grad_q, near, far, queries, keys, values, grad_in, key_sum, value_sum = refs
    rows = blocks[0].shape[0]
    group = queries.shape[1]
    span = chips * rows
    fill_heads(blocks, others, group, queries, keys, values)
    for index in range(chips):
        grad_in[index * rows : (index + 1) * rows, :] = grads[index][...]
    for head in range(group // HEAD):
        cut = slice(head * HEAD, (head + 1) * HEAD)
        key_head = keys[:, cut]
        value_head = values[:, cut]
        for place_in, part in enumerate(chunks_of(span)):
            query = queries[part, cut]
            grad = grad_in[part, cut]
            delta = jnp.sum(grad.astype(F32) * mixed[part, cut], -1, keepdims=True)
            probability = jnp.exp(matmul_t(query, key_head) - logs[part, head : head + 1])
            slope = matmul_t(grad, value_head) - delta
            grad_scores = (probability * slope).astype(BF)
            grad_q[part, cut] = (matmul(grad_scores, key_head) * 0.125).astype(BF)
            key_term = grad_matmul(grad_scores, query)
            value_term = grad_matmul(probability.astype(BF), grad)
            if place_in == 0:
                key_sum[:, cut] = key_term
                value_sum[:, cut] = value_term
            else:
                key_sum[:, cut] += key_term
                value_sum[:, cut] += value_term
    near[:, :group] = key_sum[:span, :]
    near[:, group:] = value_sum[:span, :]
    far[:, :group] = key_sum[span:, :].astype(BF)
    far[:, group:] = value_sum[span:, :].astype(BF)


def attend_back_fast(chips, blocks, others, grads, mixed, logs):
    rows, wide = blocks[0].shape
    group = wide // 3
    span = chips * rows
    return run(
        functools.partial(attend_back_kernel, chips),
        "attend_back",
        [
            shape((span, group), BF),
            shape((span, 2 * group), F32),
            shape((span, 2 * group), BF),
        ],
        [*blocks, *others, *grads, mixed, logs],
        (),
        [
            pltpu.VMEM((span, group), BF),
            pltpu.VMEM((2 * span, group), BF),
            pltpu.VMEM((2 * span, group), BF),
            pltpu.VMEM((span, group), BF),
            pltpu.VMEM((2 * span, group), F32),
            pltpu.VMEM((2 * span, group), F32),
        ],
        flops=20 * span * span * group,
    )


def combine_kernel(grad_q, near, far, *outs):
    rows, wide = outs[0].shape
    group = wide // 3
    for index, out in enumerate(outs):
        cut = slice(index * rows, (index + 1) * rows)
        out[:, :group] = grad_q[cut, :]
        out[:, group:] = (near[cut, :] + far[cut, :].astype(F32)).astype(BF)


def combine_fast(chips, grad_q, near, far):
    span, group = grad_q.shape
    return run(
        combine_kernel,
        "combine",
        [shape((span // chips, 3 * group), BF)] * chips,
        [grad_q, near, far],
    )


def exact_move(values, perm):
    high = values.astype(BF)
    rest = values - high.astype(F32)
    middle = rest.astype(BF)
    low = (rest - middle.astype(F32)).astype(BF)
    return matmul(high, perm) + matmul(middle, perm) + matmul(low, perm)


def collect(chips, stage, pieces, project):
    chip, _ = spot_in()
    width = project.shape[1] // 3
    group = width // chips
    for step in range(chips):
        stage[lax.rem(chip + step, chips)] = pieces[step][...]
    for section in range(3):
        cut = slice(section * group, (section + 1) * group)
        joined = jnp.concatenate([stage[index][:, cut] for index in range(chips)], 1)
        project[:, section * width : (section + 1) * width] = joined


def through_project(grad, project, weight):
    width = grad.shape[1]
    for section in range(3):
        cut = slice(section * width, (section + 1) * width)
        grad += matmul_t(project[:, cut], weight[:, cut])
    return grad


def project_back_kernel(layer, chips, many, grad_one, perm, sums, *refs):
    pieces, refs = refs[:chips], refs[chips:]
    weights, refs = refs[:many], refs[many:]
    out, project, vector_out, stage, weight, left_sems, right_sems = refs
    copies = fetch_project(layer, weights, weight, left_sems, right_sems, perm.shape[0])
    collect(chips, stage, pieces, project)
    wait_all(copies)
    out[...] = through_project(grad_one[...], project, weight)
    vector_rows(project, sums, perm, vector_out)


def collect_kernel(chips, perm, perm_wide, feed_sums, sums, *refs):
    pieces, refs = refs[:chips], refs[chips:]
    project, vector_out, stage = refs
    collect(chips, stage, pieces, project)
    slice_vector_rows(project, sums, feed_sums, perm, perm_wide, vector_out)


def collect_fast(chips, perm, perm_wide, feed_sums, sums, pieces):
    rows, group = pieces[0].shape
    return run(
        functools.partial(collect_kernel, chips),
        "collect",
        [shape((rows, chips * group), BF), shape(sums.shape, F32)],
        [perm, perm_wide, feed_sums, sums, *pieces],
        (),
        [pltpu.VMEM((chips, rows, group), BF)],
    )


def input_back_kernel(grad_one, perm, project, *refs):
    weights, refs = refs[:8], refs[8:]
    out, weight, left_sems, right_sems = refs
    wait_all(fetch_project(0, weights, weight, left_sems, right_sems, perm.shape[0]))
    grad = through_project(grad_one[...], project, weight)
    out[...] = matmul_t(grad.astype(BF), perm[...]).astype(BF)


def input_back_fast(grad_one, perm, project, weights):
    rows, width = grad_one.shape
    return run(
        input_back_kernel,
        "input_back",
        [shape((rows, width), BF)],
        [grad_one, perm, project],
        weights,
        [
            pltpu.VMEM((width, 3 * width), BF),
            pltpu.SemaphoreType.DMA((4,)),
            pltpu.SemaphoreType.DMA((8,)),
        ],
        flops=6 * rows * width * width,
    )[0]


def exact_back(values, perm):
    high = values.astype(BF)
    rest = values - high.astype(F32)
    middle = rest.astype(BF)
    low = (rest - middle.astype(F32)).astype(BF)
    return matmul_t(high, perm) + matmul_t(middle, perm) + matmul_t(low, perm)


def slice_vector_rows(project, sums, feed_sums, perm, perm_wide, vector_out):
    width = perm.shape[0]
    spot = lax.axis_index("dp")
    vector_out[...] = sums[...]
    line = lax.broadcasted_iota(jnp.int32, (8, width), 0)
    rows = exact_back(feed_sums[...], perm_wide[...])
    first = column_sum(project[:, :width].astype(F32))
    second = column_sum(project[:, 2 * width :].astype(F32))
    rows = jnp.where(line == 0, first, jnp.where(line == 1, second, rows))
    moved = exact_move(rows, perm[...])
    vector_out[0:2, :] = moved[0:2, :]
    wide_line = lax.broadcasted_iota(jnp.int32, (16, width), 0)
    vector_out[...] = jnp.where(wide_line == 5 + spot, moved[2:3, :], vector_out[...])


def vector_rows(project, sums, perm, vector_out):
    width = perm.shape[0]
    vector_out[...] = sums[...]
    vector_out[0:1, :] = column_sum(project[:, :width].astype(F32))
    vector_out[1:2, :] = column_sum(project[:, 2 * width :].astype(F32))
    moved = exact_move(vector_out[0:8, :], perm[...])
    vector_out[0:2, :] = moved[0:2, :]
    vector_out[5:8, :] = moved[5:8, :]
    moved = exact_move(vector_out[8:16, :], perm[...])
    vector_out[8:9, :] = moved[0:1, :]


def project_back_fast(layer, chips, grad_one, perm, sums, pieces, weights):
    rows, width = grad_one.shape
    return run(
        functools.partial(project_back_kernel, layer, chips, len(weights)),
        "project_back",
        [
            shape((rows, width), F32),
            shape((rows, 3 * width), BF),
            shape((16, width), F32),
        ],
        [grad_one, perm, sums, *pieces],
        weights,
        [
            pltpu.VMEM((chips, rows, 3 * width // chips), BF),
            pltpu.VMEM((width, 3 * width), BF),
            pltpu.SemaphoreType.DMA((4,)),
            pltpu.SemaphoreType.DMA((8,)),
        ],
        flops=6 * rows * width * width,
    )


def feed_terms_kernel(normed, act, gave, theirs, gave_theirs, out):
    _, core = spot_in()
    width = normed.shape[1]
    half = width // 2
    left = jnp.concatenate([half_at(normed, core), theirs[:, 2 * half : 3 * half]], 0)
    count = act.shape[1] // width
    for index in range(count):
        cut = slice(index * width, (index + 1) * width)
        far = slice((index + 1) * width, (index + 2) * width)
        right = jnp.concatenate([gave[:, far], gave_theirs[:, far]], 0)
        out[:, cut] = grad_matmul(left, right).astype(BF)
    left = jnp.concatenate([half_at(act, core), theirs[:, 3 * half :]], 0)
    right = jnp.concatenate([gave[:, :width], gave_theirs[:, :width]], 0)
    for index in range(count):
        cut = slice(index * half, (index + 1) * half)
        spot = slice((count + index) * width, (count + index + 1) * width)
        out[:, spot] = grad_matmul(left[:, cut], right).astype(BF)


def feed_terms_fast(normed, act, gave, theirs, gave_theirs):
    rows, width = normed.shape
    wide = act.shape[1]
    return run(
        feed_terms_kernel,
        "feed_terms",
        [shape((width // 2, 2 * wide), BF)],
        [normed, act, gave, theirs, gave_theirs],
        flops=4 * rows * width * wide,
    )[0]


def attend_terms_kernel(
    low, attended, project, attn_nat, vector, theirs, project_theirs, attn_theirs,
    vector_theirs, left_keep, left_sent, right_keep, right_sent
):
    _, core = spot_in()
    bit, high = dp_place()
    width = low.shape[1]
    half = width // 2
    block = half // 4

    def put_left(columns, value):
        value = value.astype(BF)
        for side in range(2):
            first = value[2 * side * block : (2 * side + 1) * block]
            second = value[(2 * side + 1) * block : (2 * side + 2) * block]
            rows = slice(side * block, (side + 1) * block)
            left_keep[rows, columns] = jnp.where(bit == 0, first, second)
            left_sent[rows, columns] = jnp.where(bit == 0, second, first)

    def put_right(columns, value):
        value = value.astype(BF)
        first, second = value[: 2 * block], value[2 * block :]
        right_keep[:, columns] = jnp.where(high == 0, first, second)
        right_sent[:, columns] = jnp.where(high == 0, second, first)

    left = jnp.concatenate([half_at(low, core), theirs[:, :half]], 0)
    for index in range(3):
        cut = slice(index * width, (index + 1) * width)
        right = jnp.concatenate([project[:, cut], project_theirs[:, cut]], 0)
        if index < 2:
            put_left(cut, grad_matmul(left, right))
        else:
            put_right(slice(0, width), grad_matmul(left, right))
    left = jnp.concatenate([half_at(attended, core), theirs[:, half : 2 * half]], 0)
    right = jnp.concatenate([attn_nat[...], attn_theirs[...]], 0)
    put_right(slice(width, 2 * width), grad_matmul(left, right))
    rows = half_at(vector, core) + half_at(vector_theirs, core)
    upper = rows.astype(BF)
    rest = (rows - upper.astype(F32)).astype(BF)
    count = rows.shape[0]
    line = lax.broadcasted_iota(jnp.int32, (count, LANES), 0)
    lane = lax.broadcasted_iota(jnp.int32, (count, LANES), 1)
    extra = grad_matmul(upper, (lane == line).astype(BF))
    extra += grad_matmul(rest, (lane == line + count).astype(BF))
    put_right(slice(2 * width, 2 * width + LANES), extra)


def attend_terms_fast(*args):
    rows, width = args[0].shape
    return run(
        attend_terms_kernel,
        "attend_terms",
        [shape((width // 4, 2 * width), BF)] * 2
        + [shape((width // 4, 2 * width + LANES), BF)] * 2,
        list(args),
        flops=16 * rows * width * width // 2,
    )


def after(array, *others):
    return lax.optimization_barrier((array, *others))[0]


def chips_parts(array):
    return [array] + [chip_shift(array, step) for step in range(1, chips_of())]


def chips_gather(array):
    return lax.all_gather(
        array, "seq", axis=0, tiled=True, axis_index_groups=core_groups()
    )


def chips_scatter(array):
    return lax.psum_scatter(
        array, "seq", scatter_dimension=0, tiled=True, axis_index_groups=core_groups()
    )


def chips_join(parts):
    chips = chips_of()
    chip, _ = place()
    return jnp.concatenate(
        [
            lax.select_n(chip, *[parts[(spot - index) % chips] for spot in range(chips)])
            for index in range(chips)
        ],
        0,
    )


def dp_swap(array, bit):
    size = lax.axis_size("dp")
    return lax.ppermute(array, "dp", [(i, i ^ bit) for i in range(size)])


def dp_place():
    spot = lax.axis_index("dp")
    return spot % 2, spot // 2


def join_pair(bit, own, other):
    return jnp.where(
        bit == 0, jnp.concatenate([own, other], 0), jnp.concatenate([other, own], 0)
    )


def square_first(part, cut):
    left, right = part[:, :cut], part[:, cut:]
    return left, dp_swap(left, 1), right, dp_swap(right, 2)


def square_second(left, left_far, right, right_far):
    bit, high = dp_place()
    left_far, right_far = lax.optimization_barrier((left_far, right_far))
    left = join_pair(bit, left, left_far)
    right = join_pair(high, right, right_far)
    return left, dp_swap(left, 2), right, dp_swap(right, 1)


def square_pieces(left, left_far, right, right_far):
    near = [core_swap(left), core_swap(right)]
    left_far, right_far = lax.optimization_barrier((left_far, right_far))
    return [
        left, left_far, near[0], core_swap(left_far),
        right, right_far, near[1], core_swap(right_far),
    ]


def vectors_kernel(groups, perm, perm_wide, *refs):
    pieces, refs = refs[:4], refs[4:]
    outs, (stage, sems) = refs[:-2], refs[-2:]
    width = perm.shape[0]
    start = pieces[0].shape[1] - LANES
    wait_all(
        fetch_right(pieces, stage, sems, slice(start, start + LANES), slice(0, LANES))
    )
    columns = stage[...]
    line = lax.broadcasted_iota(jnp.int32, (width, width), 0)
    spot = lax.broadcasted_iota(jnp.int32, (width, width), 1)
    moved = grad_matmul(columns, (line == spot).astype(BF))
    plain = plain_rows(columns, perm[...])
    wide = matmul(plain.astype(BF), perm_wide[...])
    piece = width // (2 * groups)
    for layer in range(LAYERS):
        base = layer * VECS
        moved_out, plain_out, wide_out = outs[3 * layer : 3 * layer + 3]
        moved_out[:VECS, :] = moved[base : base + VECS]
        plain_out[:VECS, :] = plain[base : base + VECS]
        if layer == 0:
            wide_out[...] = wide[base + 5 : base + 5 + groups]
            continue
        for index in range(groups):
            row = base + 5 + index
            for part in range(2 * groups):
                goal = part * groups * piece + index * piece
                wide_out[:, goal : goal + piece] = wide[
                    row : row + 1, part * piece : (part + 1) * piece
                ]


def vectors_fast(groups, perm, perm_wide, pieces):
    width = perm.shape[0]
    out = run(
        functools.partial(vectors_kernel, groups),
        "vectors",
        [
            *[shape((16, width), F32)] * 2,
            shape((groups, width), F32),
            *[shape((16, width), F32)] * 2,
            shape((1, groups * width), F32),
        ],
        [perm, perm_wide],
        pieces,
        [pltpu.VMEM((width, LANES), BF), pltpu.SemaphoreType.DMA((8,))],
    )
    return [out[:3], out[3:]]


def fold_kernel(*refs):
    bit, high = dp_place()
    for index, flag in enumerate((high, bit)):
        keep, came, keep_out, sent_out = (refs[index * 2], refs[index * 2 + 1],
                                          refs[4 + index * 2], refs[5 + index * 2])
        rows = keep.shape[0] // 2
        total = keep[...].astype(F32) + came[...].astype(F32)
        keep_out[...] = jnp.where(flag == 0, total[:rows], total[rows:]).astype(BF)
        sent_out[...] = jnp.where(flag == 0, total[rows:], total[:rows]).astype(BF)


def split_kernel(chips, *refs):
    left, left_far, right, right_far = refs[:4]
    own, sends, total = refs[4], refs[5 : 4 + chips], refs[4 + chips]
    chip, _ = spot_in()
    cut = left.shape[1]
    rows = left.shape[0] // chips
    for index in range(chips):
        span = slice(index * rows, (index + 1) * rows)
        total[index, :, :cut] = left[span, :].astype(F32) + left_far[span, :].astype(F32)
        total[index, :, cut:] = right[span, :].astype(F32) + right_far[span, :].astype(F32)
    own[...] = total[chip]
    for step in range(1, chips):
        sends[step - 1][...] = total[lax.rem(chip + step, chips)].astype(BF)


def square_fold(parts):
    left, left_sent, right, right_sent = parts
    rows = left.shape[0] // 2
    kinds = [shape((rows, member.shape[1]), BF) for member in (left, left, right, right)]
    return run(
        fold_kernel, "fold", kinds,
        [left, dp_swap(left_sent, 1), right, dp_swap(right_sent, 2)],
    )


def square_split(parts):
    chips = chips_of()
    left, left_sent, right, right_sent = parts
    share = left.shape[0] // chips
    width = left.shape[1] + right.shape[1]
    return run(
        functools.partial(split_kernel, chips),
        "split",
        [shape((share, width), F32)] + [shape((share, width), BF)] * (chips - 1),
        [left, dp_swap(left_sent, 2), right, dp_swap(right_sent, 1)],
        (),
        [pltpu.VMEM((chips, share, width), F32)],
    )


def square_total(parts):
    total = parts[0]
    for step in range(1, len(parts)):
        total = total + chip_shift(parts[step], step).astype(F32)
    return total


def piece_matrix(width, block, count):
    spot = np.arange(width)
    inner = spot % block
    return one_hot(
        ((spot // block) % 2) * (width // 2)
        + (inner % count) * (width // (2 * count))
        + (spot // (2 * block)) * (block // count)
        + inner // count
    )


def peer_shift(array, bits):
    size = lax.axis_size("dp")
    return lax.ppermute(array, "dp", [(i, i ^ bits) for i in range(size)])


def peer_gather(array):
    return [array] + [peer_shift(array, bits) for bits in range(1, 4)]


def peer_trade(parts):
    return [parts[0]] + [peer_shift(parts[bits], bits) for bits in range(1, 4)]


def units_matrix(width, block, count):
    half = width // 2
    spot = np.arange(half)
    inner = spot % block
    chips = half // (block * count)
    return one_hot(
        (spot // block) % chips * (block * count) + inner * count + spot // (block * chips)
    )


def rows_matrix(width, block):
    half = width // 2
    spot = np.arange(half)
    chips = half // (4 * block)
    return one_hot(
        (spot // block) % chips * (4 * block) + spot // (block * chips) * block + spot % block
    )


def fast_device(
    hidden_input,
    triple_weight,
    mixer_weight,
    expand_weight,
    shrink_weight,
    vector_params,
    output_grad,
):
    _, count, width = hidden_input.shape
    chips = chips_of()
    _, core = place()
    share = triple_weight.shape[1]
    wide_share = shrink_weight.shape[1]
    wide = expand_weight.shape[2]
    groups = wide // width
    perm = swap_matrix(width, share)
    perm_wide = piece_matrix(width, wide_share, groups)
    mixer_moved = move(mixer_weight.reshape(-1, width), perm).reshape(mixer_weight.shape)
    shrink_moved = move(shrink_weight.reshape(-1, width), perm).reshape(shrink_weight.shape)
    pieces = 2 * groups
    spot = lax.axis_index("dp")
    perm_rows = rows_matrix(width, share)
    perm_units = units_matrix(width, share, groups)
    expand_zero = move(expand_weight[0].reshape(-1, width), perm_wide).reshape(share, wide)
    expand_one = (
        move(expand_weight[1].reshape(-1, width), perm_wide)
        .reshape(share, groups, pieces, width // pieces)
        .transpose(0, 2, 1, 3)
        .reshape(share, wide)
    )
    shrink_moved = shrink_moved.reshape(LAYERS, share, groups * width)
    vector_columns = vector_params.reshape(LAYERS * VECS, share).T
    vector_columns = jnp.pad(vector_columns, ((0, 0), (0, LANES - LAYERS * VECS)))

    parts = chips_parts(
        jnp.concatenate([triple_weight[0], mixer_moved[0], vector_columns], 1)
    )
    expand_zero = after(expand_zero, parts[1])
    expand_zero = jnp.concatenate(
        peer_trade(
            [
                lax.dynamic_slice(
                    expand_zero, (0, jnp.bitwise_xor(spot, bits) * width), (share, width)
                )
                for bits in range(4)
            ]
        ),
        1,
    )
    feed_parts = [
        jnp.concatenate([expand_zero, shrink_moved[0]], 1),
        jnp.concatenate([expand_one, shrink_moved[1]], 1),
    ]
    early = jnp.concatenate([feed_parts[0], triple_weight[1], mixer_moved[1]], 1)
    parts[-1] = after(parts[-1], early, feed_parts[1])
    attn = chips_join(parts)
    early = chips_gather(after(early, attn))
    feed_zero, attn_one = early[:, : 2 * wide], early[:, 2 * wide :]
    attn = square_second(*square_first(attn, 2 * width))
    attn = square_pieces(*attn)

    def project(layer, hidden, pieces):
        bias = perm[:8].astype(F32) if layer == 0 else rows_of[layer][1]
        low, blocks = project_fast(layer, chips, hidden, perm, bias, pieces)
        blocks = [blocks[0]] + [chip_shift(blocks[step], step) for step in range(1, chips)]
        return low, blocks

    def attend_blocks(blocks):
        others = [core_swap(block) for block in blocks]
        mixed, logs, pieces = attend_fast(chips, blocks, others)
        pieces = [pieces[0]] + [chip_shift(pieces[step], -step) for step in range(1, chips)]
        return (blocks, others, mixed, logs), pieces

    def feed(layer, hidden, low, pieces, weights):
        rows, _, ffn_bias = rows_of[layer]
        (
            hidden, attended, normed, pre_act, act, hat_one, scale_one, hat_two, scale_two,
            sent, squares,
        ) = feed_fast(layer, chips, hidden, low, perm, rows, ffn_bias, pieces, weights)
        return (
            hidden,
            (hat_one, scale_one, hat_two, scale_two, pre_act),
            (low, attended, normed, act, core_swap(sent)),
            jnp.sum(squares[:3], -1),
        )

    low_zero, blocks = project(0, hidden_input[0], attn)
    feed_zero = after(feed_zero, *blocks)
    attn_one = square_second(*square_first(after(attn_one, *blocks), 2 * width))
    feed_one = chips_gather(after(feed_parts[1], *blocks))
    blocks[0] = after(blocks[0], attn_one[0], attn_one[2])
    attend_zero, pieces = attend_blocks(blocks)
    attn_one = [
        attn_one[0], after(attn_one[1], attend_zero[2]),
        attn_one[2], after(attn_one[3], attend_zero[2]),
    ]
    vector_pieces = [after(attn[4], attend_zero[2], attn_one[1], attn_one[3]), *attn[5:]]
    rows_of = vectors_fast(groups, perm, perm_wide, vector_pieces)
    attn_one = square_pieces(*attn_one)
    slice_pieces = [feed_zero, core_swap(feed_zero)]
    pieces[0] = after(pieces[0], slice_pieces[1], *attn_one)

    attended, normed, normed_low, hat, scale, sent, squares = mix_fast(
        chips, low_zero, low_zero, perm, rows_of[0][0], pieces, attn[4:]
    )
    norms_zero, acts_zero = (hat, scale), (low_zero, attended, None, None, core_swap(sent))
    inputs = peer_gather(normed_low)
    terms, pre, act = slice_feed_fast(rows_of[0][2], inputs, slice_pieces)
    feed_one = lax.all_gather(after(feed_one, normed), "dp", axis=0, tiled=True)
    slice_saved = (inputs, pre, act)
    hidden, hat, scale, squares = finish_fast(normed, rows_of[0][0], squares, peer_trade(terms))
    ends_zero, squares_zero = (hat, scale), jnp.sum(squares[:3], -1)

    low, blocks = project(1, hidden, attn_one)
    attend_one, pieces = attend_blocks(blocks)
    feed_one = after(feed_one, attend_one[2])
    feed_one = [feed_one, core_swap(feed_one)]
    hidden, feed_saved_one, acts_one, squares_one = feed(
        1, hidden, low, pieces, attn_one[4:] + feed_one
    )
    packs = [attn, attn_one + feed_one]
    kept = [(attend_zero, None, acts_zero), (attend_one, feed_saved_one, acts_one)]
    collected = [squares_zero, squares_one]
    elements = count * width * lax.axis_size("dp") * lax.axis_size("seq")
    hidden_output = move_back(hidden.astype(BF), perm)

    totals = jnp.stack(collected)
    sum_steps = [("seq", 1), ("seq", 2), ("seq", 4), ("dp", 1), ("dp", 2)]
    sum_steps = [step for step in sum_steps if step[1] < lax.axis_size(step[0])]

    def sum_more(totals, token):
        if sum_steps:
            axis, bit = sum_steps.pop(0)
            size = lax.axis_size(axis)
            pairs = [(i, i ^ bit) for i in range(size)]
            totals = totals + lax.ppermute(after(totals, token), axis, pairs)
        return totals

    def scatter_feed(term):
        part = lax.psum_scatter(term, "dp", scatter_dimension=0, tiled=True)
        part = lax.psum_scatter(
            part, "seq", scatter_dimension=0, tiled=True, axis_index_groups=core_groups()
        )
        return part.astype(F32)

    def back_feed(layer, grad):
        (_, feed_saved, acts), weights = kept[layer], packs[layer]
        grad_one, gave, attn_nat, sums, grads = feed_back_fast(
            layer, chips, grad, perm, perm_wide, rows_of[layer][0], feed_saved,
            weights[4:],
        )
        grads = [grads[0]] + [chip_shift(grads[step], step) for step in range(1, chips)]
        _, _, normed, act, theirs = acts
        feed_term = feed_terms_fast(normed, act, gave, theirs, core_swap(gave))
        return grad_one, attn_nat, sums, grads, feed_term

    def back_attend(layer, grads):
        blocks, others, mixed, logs = kept[layer][0]
        return attend_back_fast(chips, blocks, others, grads, mixed, logs)

    def back_combine(grad_q, near, far):
        pieces = combine_fast(chips, grad_q, near, far)
        return [pieces[0]] + [chip_shift(pieces[step], -step) for step in range(1, chips)]

    def back_project(layer, grad_one, sums, pieces):
        return project_back_fast(layer, chips, grad_one, perm, sums, pieces, packs[layer][:8])

    def back_terms(layer, project_grad, attn_nat, vector, far):
        low, attended, _, _, theirs = kept[layer][2]
        return attend_terms_fast(
            low, attended, project_grad, attn_nat, vector, theirs, *far
        )

    def swap_all(*members):
        return [core_swap(member) for member in members]

    grad_one, attn_nat, sums, grads, feed_term = back_feed(1, output_grad[0])
    totals = sum_more(totals, grad_one)
    feed_sum_one = lax.psum_scatter(feed_term, "dp", scatter_dimension=0, tiled=True)
    grads[0] = after(grads[0], feed_term, totals, hidden_output)
    grad_q, near, far = back_attend(1, grads)
    totals = sum_more(totals, grad_q)
    pieces = back_combine(after(grad_q, totals), near, core_swap(far))
    totals = sum_more(totals, pieces[0])
    pieces[0] = after(pieces[0], totals)
    grad, project_grad, vector = back_project(1, grad_one, sums, pieces)
    far_one = swap_all(project_grad, attn_nat, vector)
    terms_args = (project_grad, attn_nat, vector)

    attn_terms = back_terms(1, *terms_args, far_one)
    rows = rows_of[0][0]
    totals = sum_more(totals, grad)
    grad_two, grad_low, sums = finish_back_fast(False, grad, perm, rows, *ends_zero)
    blocks = peer_gather(grad_low)
    blocks[2] = after(blocks[2], totals)
    blocks[1] = after(blocks[1], feed_sum_one, attn_terms[0])
    feed_sum_one = chips_scatter(feed_sum_one).astype(F32)
    inputs, pre, act = slice_saved
    terms, slope, gave, feed_sums = slice_back_fast(blocks, inputs, pre, act, slice_pieces)
    totals = sum_more(totals, slope)
    terms = peer_trade(terms)
    terms[0] = after(terms[0], totals)
    grad_one, attn_nat, sums, grads = mix_back_fast(
        chips, grad_two, perm, rows, *norms_zero, sums, terms, attn[4:]
    )
    grads = [grads[0]] + [chip_shift(grads[step], step) for step in range(1, chips)]
    attn_terms = [
        attn_terms[0], after(attn_terms[1], grad_one), attn_terms[2], after(attn_terms[3], grad_one)
    ]
    grads[0] = after(grads[0], feed_sum_one)
    grad_q, near, far = back_attend(0, grads)
    feed_term = slice_terms_fast(
        perm_rows, perm_units, blocks, inputs, act, after(slope, grad_q), core_swap(gave)
    )
    feed_sum_zero = chips_scatter(feed_term)
    attn_terms[0] = after(attn_terms[0], grad_q)
    folded = square_fold(attn_terms)
    pieces = back_combine(after(grad_q, folded[0]), near, core_swap(far))
    split_one = square_split(folded)
    pieces[0] = after(pieces[0], split_one[0], feed_term)
    project_grad, vector = collect_fast(chips, perm, perm_wide, feed_sums, sums, pieces)
    far_zero = swap_all(project_grad, attn_nat, vector)
    attn_terms = list(back_terms(0, project_grad, attn_nat, vector, far_zero))
    folded = square_fold(attn_terms)
    input_grad = input_back_fast(after(grad_one, folded[0]), perm, project_grad, attn)
    split_one = [after(split_one[0], folded[0]), *split_one[1:]]
    attn_sum_one = square_total(split_one)
    feed_sum_zero = after(feed_sum_zero, folded[0])
    expand_sums = peer_trade(
        [
            lax.dynamic_slice(
                feed_sum_zero, (jnp.bitwise_xor(spot, bits) * share, 0), (share, width)
            )
            for bits in range(4)
        ]
    )
    expand_zero = jnp.concatenate(
        [
            matmul_t(
                lax.select_n(spot, *[expand_sums[index ^ other] for other in range(4)]), perm_wide
            )
            for index in range(groups)
        ],
        1,
    )
    shrink_zero = matmul_t(feed_sum_zero[:, width:], perm)
    folded = [after(folded[0], input_grad, *expand_sums, shrink_zero), *folded[1:]]
    attn_sum_zero = square_total(square_split(folded))
    terms = [(attn_sum_zero, None), (attn_sum_one, None)]
    expand_grads = [expand_zero, feed_sum_one[:, :wide]]
    shrink_grads = [shrink_zero, feed_sum_one[:, wide:].reshape(wide_share, width)]
    grad = input_grad
    root_squares = jnp.sqrt(totals / elements)
    vector_grad = jnp.stack(
        [
            (
                terms[layer][0][:, 4 * width : 4 * width + VECS]
                + terms[layer][0][:, 4 * width + 16 : 4 * width + 16 + VECS]
            ).T
            for layer in range(LAYERS)
        ]
    )
    return (
        hidden_output[None],
        grad[None],
        jnp.stack([terms[layer][0][:, : 3 * width] for layer in range(LAYERS)]),
        jnp.stack([terms[layer][0][:, 3 * width : 4 * width] for layer in range(LAYERS)]),
        jnp.stack(expand_grads),
        jnp.stack(shrink_grads),
        vector_grad,
        root_squares,
    )


def per_device(*args):
    chips = chips_of()
    if chips in (2, 4) and HEADS % chips == 0 and lax.axis_size("dp") == 4:
        return fast_device(*args)
    return plain_device(*args)


def solution(mesh):
    return jax.shard_map(
        per_device,
        mesh=mesh,
        in_specs=(
            P("dp", "seq", None),
            P(None, ("dp", "seq"), None),
            P(None, ("dp", "seq"), None),
            P(None, ("dp", "seq"), None),
            P(None, ("dp", "seq"), None),
            P(None, None, ("dp", "seq")),
            P("dp", "seq", None),
        ),
        out_specs=(
            P("dp", "seq", None),
            P("dp", "seq", None),
            P(None, ("dp", "seq"), None),
            P(None, ("dp", "seq"), None),
            P(None, ("dp", "seq"), None),
            P(None, ("dp", "seq"), None),
            P(None, None, ("dp", "seq")),
            P(),
        ),
        check_vma=False,
    )
```

```python
import functools
import math

import jax
import jax.numpy as jnp
import numpy as np
from jax import lax
from jax.experimental import pallas as pl
from jax.experimental.pallas import tpu as pltpu
from jax.sharding import PartitionSpec as P

HEADS = 12
HEAD = 64
LAYERS = 2
VECS = 12
LANES = 128

EPSILON = 1e-12
ROOT_HALF = 2.0 ** -0.5
ROOT_TAU = (2.0 * math.pi) ** -0.5

BF = jnp.bfloat16
F32 = jnp.float32


def layer_norm(residual, gain_row, shift_row):
    center = residual - jnp.mean(residual, -1, keepdims=True)
    spread = jnp.mean(center * center, -1, keepdims=True)
    return center * lax.rsqrt(spread + EPSILON) * gain_row + shift_row


def gelu_exact(values):
    return jax.nn.gelu(values, approximate=False)


def matmul(left, right):
    return jnp.dot(left, right, preferred_element_type=F32)


def matmul_t(left, right):
    return lax.dot_general(left, right, (((1,), (1,)), ((), ())), preferred_element_type=F32)


def grad_matmul(left, right):
    return lax.dot_general(left, right, (((0,), (0,)), ((), ())), preferred_element_type=F32)


def chips_of():
    return lax.axis_size("seq") // 2


def core_swap(array):
    size = lax.axis_size("seq")
    return lax.ppermute(array, "seq", [(i, i ^ 1) for i in range(size)])


def chip_shift(array, step):
    size = lax.axis_size("seq")
    chips = size // 2
    pairs = [(i, ((i // 2 + step) % chips) * 2 + i % 2) for i in range(size)]
    return lax.ppermute(array, "seq", pairs)


def core_groups():
    size = lax.axis_size("seq")
    return [list(range(0, size, 2)), list(range(1, size, 2))]


def place():
    spot = lax.axis_index("seq")
    return spot // 2, spot % 2


def gather_chips(array):
    chips = chips_of()
    if chips > 4:
        return lax.all_gather(
            array, "seq", axis=0, tiled=True, axis_index_groups=core_groups()
        )
    chip, _ = place()
    rows = array.shape[0]
    whole = jnp.zeros((chips * rows, array.shape[1]), array.dtype)
    for step in range(chips):
        part = array if step == 0 else chip_shift(array, step)
        whole = lax.dynamic_update_slice(whole, part, (((chip - step) % chips) * rows, 0))
    return whole


def gather_weight(array):
    own = lax.all_gather(gather_chips(array), "dp", axis=0, tiled=True)
    return join_cores(own, core_swap(own), 0)


def join_cores(own, other, axis):
    _, core = place()
    return jnp.where(
        core == 0,
        jnp.concatenate([own, other], axis),
        jnp.concatenate([other, own], axis),
    )


def scatter_chips(array):
    chips = chips_of()
    if chips > 4:
        return lax.psum_scatter(
            array, "seq", scatter_dimension=0, tiled=True, axis_index_groups=core_groups()
        ).astype(F32)
    chip, _ = place()
    rows = array.shape[0] // chips
    total = None
    for step in range(chips):
        part = lax.dynamic_slice(
            array, (((chip + step) % chips) * rows, 0), (rows, array.shape[1])
        )
        if step > 0:
            part = chip_shift(part, step)
        total = part.astype(F32) if total is None else total + part.astype(F32)
    return total


def scatter_grad(array):
    part = lax.psum_scatter(array.astype(BF), "dp", scatter_dimension=0, tiled=True)
    return scatter_chips(part)


def half_of(array, index):
    width = array.shape[1] // 2
    return lax.dynamic_slice(array, (0, index * width), (array.shape[0], width))


def one_hot(goal):
    return jnp.asarray(np.asarray(goal[:, None] == np.arange(goal.size)[None], np.float32), BF)


def swap_matrix(width, block):
    spot = np.arange(width)
    return one_hot(
        ((spot // block) % 2) * (width // 2) + (spot // (2 * block)) * block + spot % block
    )


def move(array, matrix):
    return jnp.dot(array, matrix, preferred_element_type=F32).astype(BF)


def move_back(array, matrix):
    return matmul_t(array, matrix).astype(BF)


def attend(queries, key_rows, value_rows):
    count = queries.shape[1] // HEAD
    outs = []
    logs = []
    for head in range(count):
        cut = slice(head * HEAD, (head + 1) * HEAD)
        scores = matmul_t(queries[:, cut], key_rows[:, cut])
        top = jnp.max(scores, -1, keepdims=True)
        log_total = top + jnp.log(jnp.sum(jnp.exp(scores - top), -1, keepdims=True))
        probability = jnp.exp(scores - log_total).astype(BF)
        outs.append(matmul(probability, value_rows[:, cut]))
        logs.append(log_total)
    return jnp.concatenate(outs, 1), jnp.concatenate(logs, 1)


def attend_back(queries, key_rows, value_rows, logs, mixed, grad_mixed):
    count = queries.shape[1] // HEAD
    grad_q, grad_k, grad_v = [], [], []
    for head in range(count):
        cut = slice(head * HEAD, (head + 1) * HEAD)
        grad_head = grad_mixed[:, cut]
        delta = jnp.sum(grad_head.astype(F32) * mixed[:, cut], -1, keepdims=True)
        probability = jnp.exp(
            matmul_t(queries[:, cut], key_rows[:, cut]) - logs[:, head : head + 1]
        )
        grad_prob = matmul_t(grad_head, value_rows[:, cut])
        grad_scores = (probability * (grad_prob - delta)).astype(BF)
        grad_q.append(matmul(grad_scores, key_rows[:, cut]))
        grad_k.append(grad_matmul(grad_scores, queries[:, cut]))
        grad_v.append(grad_matmul(probability.astype(BF), grad_head))
    return (
        jnp.concatenate(grad_q, 1).astype(BF),
        jnp.concatenate(grad_k + grad_v, 1).astype(BF),
    )


def forward_layer(hidden, params, perm):
    triple, mixer, expand, shrink, vectors, head_bias, ffn_bias = params
    rows, width = hidden.shape
    half = width // 2
    _, core = place()
    low = hidden.astype(BF)
    project = matmul(low, triple)
    queries = ((project[:, :width] + head_bias[0]) * 0.125).astype(BF)
    key_rows = project[:, width : 2 * width].astype(BF)
    value_rows = (project[:, 2 * width :] + head_bias[1]).astype(BF)
    trio = (queries, key_rows, value_rows)
    mine = jnp.concatenate([half_of(member, core) for member in trio], 1)
    sent = jnp.concatenate([half_of(member, 1 - core) for member in trio], 1)
    pair = jnp.concatenate([mine, core_swap(sent)], 0)
    pair_queries = pair[:, :half]
    pair_rest = pair[:, half:]
    chips = chips_of()
    if chips > 4:
        keyed = gather_chips(pair_rest)
    else:
        keyed = jnp.concatenate(
            [pair_rest] + [chip_shift(pair_rest, step) for step in range(1, chips)], 0
        )
    mixed, logs = attend(pair_queries, keyed[:, :half], keyed[:, half:])
    mixed_low = mixed.astype(BF)
    other = core_swap(mixed_low[rows:])
    attended = move(join_cores(mixed_low[:rows], other, 1), perm)
    attn_out = matmul(attended, mixer) + vectors[2]
    residual_one = hidden + attn_out
    normed = layer_norm(residual_one, vectors[3], vectors[4])
    normed_low = normed.astype(BF)
    pre_act = matmul(normed_low, expand) + ffn_bias
    act_low = gelu_exact(pre_act).astype(BF)
    ffn_out = matmul(act_low, shrink) + vectors[9]
    residual_two = normed + ffn_out
    output = layer_norm(residual_two, vectors[10], vectors[11])
    squares = jnp.stack(
        [jnp.sum(hidden * hidden), jnp.sum(attn_out * attn_out), jnp.sum(ffn_out * ffn_out)]
    )
    saved = (
        low, pair_queries, keyed, logs, mixed, attended,
        residual_one, normed_low, pre_act, act_low, residual_two,
    )
    return output, saved, squares


def backward_layer(grad_output, params, saved, perm, perm_wide):
    triple, mixer, expand, shrink, vectors, head_bias, ffn_bias = params
    (
        low, pair_queries, keyed, logs, mixed, attended,
        residual_one, normed_low, pre_act, act_low, residual_two,
    ) = saved
    rows, width = low.shape
    half = width // 2
    chips = chips_of()
    _, core = place()
    acts = jnp.concatenate(
        [half_of(member, 1 - core) for member in (low, attended, normed_low, act_low)], 1
    )
    acts = core_swap(acts)
    low_pair = jnp.concatenate([half_of(low, core), acts[:, :half]], 0)
    attended_pair = jnp.concatenate([half_of(attended, core), acts[:, half : 2 * half]], 0)
    normed_pair = jnp.concatenate([half_of(normed_low, core), acts[:, 2 * half : 3 * half]], 0)
    act_pair = jnp.concatenate([half_of(act_low, core), acts[:, 3 * half :]], 0)

    _, pull_two = jax.vjp(layer_norm, residual_two, vectors[10], vectors[11])
    grad_two, grad_gain_two, grad_shift_two = pull_two(grad_output)
    grad_ffn = grad_two.astype(BF)
    grad_act = matmul_t(grad_ffn, shrink)
    _, pull_gelu = jax.vjp(gelu_exact, pre_act)
    grad_pre = pull_gelu(grad_act)[0].astype(BF)
    grad_normed = grad_two + matmul_t(grad_pre, expand)
    _, pull_one = jax.vjp(layer_norm, residual_one, vectors[3], vectors[4])
    grad_one, grad_gain_one, grad_shift_one = pull_one(grad_normed)
    grad_attn = grad_one.astype(BF)
    grad_attended = move_back(matmul_t(grad_attn, mixer).astype(BF), perm)

    grad_ffn_nat = move_back(grad_ffn, perm)
    grad_attn_nat = move_back(grad_attn, perm)
    quarter = grad_pre.reshape(rows, 2, -1, half).transpose(0, 2, 1, 3).reshape(-1, width)
    grad_pre_nat = move_back(quarter, perm_wide).reshape(rows, -1)
    gave = jnp.concatenate([grad_ffn_nat, grad_pre_nat], 1)
    pair_ffn = jnp.concatenate([gave, core_swap(gave)], 0)
    grad_shrink = grad_matmul(act_pair, pair_ffn[:, :width])
    grad_expand = grad_matmul(normed_pair, pair_ffn[:, width:])

    other = core_swap(half_of(grad_attended, 1 - core))
    pair_grad = jnp.concatenate([half_of(grad_attended, core), other], 0)
    grad_q, grad_kv = attend_back(
        pair_queries, keyed[:, :half], keyed[:, half:], logs, mixed, pair_grad
    )
    span = 2 * rows
    if chips > 4:
        grad_kv = scatter_chips(grad_kv)
    else:
        total = grad_kv[:span].astype(F32)
        for step in range(1, chips):
            total = total + chip_shift(
                grad_kv[step * span : (step + 1) * span], -step
            ).astype(F32)
        grad_kv = total
    mine = jnp.concatenate([grad_q * 0.125, grad_kv.astype(BF)], 1)
    theirs = core_swap(mine)
    theirs = jnp.concatenate([theirs[rows:], theirs[:rows]], 0)
    pair_project = jnp.concatenate(
        [
            join_cores(mine[:, i * half : (i + 1) * half], theirs[:, i * half : (i + 1) * half], 1)
            for i in range(3)
        ],
        1,
    )
    grad_hidden = grad_one + matmul_t(pair_project[:rows], triple)
    grad_triple = grad_matmul(low_pair, pair_project)
    attn_pair = jnp.concatenate([grad_attn_nat, core_swap(grad_attn_nat)], 0)
    grad_mixer = grad_matmul(attended_pair, attn_pair)

    def sums(array):
        return jnp.sum(array.astype(F32), 0)

    bias_rows = jnp.concatenate(
        [
            sums(pair_project[:rows, :width])[None],
            sums(pair_project[:rows, 2 * width :])[None],
            sums(grad_pre_nat).reshape(-1, width),
        ],
        0,
    )
    count = width // (2 * lax.axis_size("dp") * chips)
    bias_rows = (
        bias_rows.reshape(bias_rows.shape[0], -1, 2, count)
        .transpose(0, 2, 1, 3)
        .reshape(bias_rows.shape)
    )
    grad_vector = jnp.concatenate(
        [
            bias_rows[:2],
            sums(grad_attn)[None],
            grad_gain_one[None],
            grad_shift_one[None],
            bias_rows[2:],
            sums(grad_ffn)[None],
            grad_gain_two[None],
            grad_shift_two[None],
        ],
        0,
    )
    grad_vector = half_of(grad_vector, core) + core_swap(half_of(grad_vector, 1 - core))
    high = grad_vector.astype(BF)
    rest = (grad_vector - high.astype(F32)).astype(BF)
    extra = jnp.concatenate([high, rest], 0).T
    extra = jnp.pad(extra, ((0, 0), (0, LANES - extra.shape[1])))
    attn_terms = jnp.concatenate([grad_triple.astype(BF), grad_mixer.astype(BF), extra], 1)
    return grad_hidden, attn_terms, grad_expand.astype(BF), grad_shrink.astype(BF)


def total_of(value):
    for axis in ("seq", "dp"):
        size = lax.axis_size(axis)
        step = 1
        while step < size:
            value = value + lax.ppermute(value, axis, [(i, i ^ step) for i in range(size)])
            step *= 2
    return value


def plain_device(
    hidden_input,
    triple_weight,
    mixer_weight,
    expand_weight,
    shrink_weight,
    vector_params,
    output_grad,
):
    _, count, width = hidden_input.shape
    share = triple_weight.shape[1]
    wide_share = shrink_weight.shape[1]
    wide = expand_weight.shape[2]
    groups = wide // width
    perm = swap_matrix(width, share)
    perm_wide = swap_matrix(width, wide_share)

    mixer_moved = move(mixer_weight.reshape(-1, width), perm).reshape(mixer_weight.shape)
    shrink_moved = move(shrink_weight.reshape(-1, width), perm).reshape(shrink_weight.shape)
    expand_moved = move(expand_weight.reshape(-1, width), perm_wide)
    expand_moved = (
        expand_moved.reshape(LAYERS * share, groups, 2, width // 2)
        .transpose(0, 2, 1, 3)
        .reshape(expand_weight.shape)
    )
    vector_columns = vector_params.reshape(LAYERS * VECS, share).T
    vector_columns = jnp.pad(vector_columns, ((0, 0), (0, LANES - LAYERS * VECS)))
    packs = []
    for layer in range(LAYERS):
        attn = [triple_weight[layer], mixer_moved[layer]]
        if layer == 0:
            attn.append(vector_columns)
        packs.append(
            (
                gather_weight(jnp.concatenate(attn, 1)),
                gather_weight(expand_moved[layer]),
                gather_weight(shrink_moved[layer]),
            )
        )
    vectors = packs[0][0][:, 4 * width : 4 * width + LAYERS * VECS].T
    natural = move_back(vectors, perm)
    params = []
    for layer in range(LAYERS):
        rows = vectors[layer * VECS : (layer + 1) * VECS].astype(F32)
        plain = natural[layer * VECS : (layer + 1) * VECS]
        ffn_bias = (
            move(plain[5 : 5 + groups], perm_wide)
            .reshape(groups, 2, width // 2)
            .transpose(1, 0, 2)
            .reshape(1, wide)
        ).astype(F32)
        attn, expand, shrink = packs[layer]
        params.append(
            (
                attn[:, : 3 * width],
                attn[:, 3 * width : 4 * width],
                expand,
                shrink,
                rows,
                plain[:2].astype(F32),
                ffn_bias,
            )
        )

    hidden = matmul(hidden_input[0], perm)
    kept = []
    collected = []
    for layer in range(LAYERS):
        hidden, saved, squares = forward_layer(hidden, params[layer], perm)
        kept.append(saved)
        collected.append(squares)
    elements = count * width * lax.axis_size("dp") * lax.axis_size("seq")
    root_squares = jnp.sqrt(total_of(jnp.stack(collected)) / elements)
    hidden_output = move_back(hidden.astype(BF), perm)

    grad = matmul(output_grad[0], perm)
    terms = [None] * LAYERS
    for layer in reversed(range(LAYERS)):
        grad, attn, expand, shrink = backward_layer(
            grad, params[layer], kept[layer], perm, perm_wide
        )
        terms[layer] = (scatter_grad(attn), scatter_grad(expand), scatter_grad(shrink))
    input_grad = move_back(grad.astype(BF), perm)
    vector_grad = jnp.stack(
        [
            (
                terms[layer][0][:, 4 * width : 4 * width + VECS]
                + terms[layer][0][:, 4 * width + VECS : 4 * width + 2 * VECS]
            ).T
            for layer in range(LAYERS)
        ]
    )
    return (
        hidden_output[None],
        input_grad[None],
        jnp.stack([terms[layer][0][:, : 3 * width] for layer in range(LAYERS)]),
        jnp.stack([terms[layer][0][:, 3 * width : 4 * width] for layer in range(LAYERS)]),
        jnp.stack([terms[layer][1] for layer in range(LAYERS)]),
        jnp.stack([terms[layer][2] for layer in range(LAYERS)]),
        vector_grad,
        root_squares,
    )


ANY = pl.BlockSpec(memory_space=pl.ANY)
VMEM = pl.BlockSpec(memory_space=pltpu.VMEM)
VMEM_BYTES = 56 * 1024 * 1024
HINT = 2
SIDE_HINT = 40
SIDE = ("feed_terms", "attend_terms", "slice_terms", "fold", "split", "input_back")


def shape(dims, kind):
    return jax.ShapeDtypeStruct(dims, kind)


def run(kernel, name, outs, placed, streamed=(), scratch=(), flops=0):
    hint = SIDE_HINT if name in SIDE else HINT
    size = sum(
        math.prod(member.shape) * member.dtype.itemsize
        for member in [*outs, *placed, *streamed]
    )
    return pl.pallas_call(
        kernel,
        name=name,
        out_shape=list(outs),
        in_specs=[VMEM] * len(placed) + [ANY] * len(streamed),
        out_specs=[VMEM] * len(outs),
        scratch_shapes=list(scratch),
        compiler_params=pltpu.CompilerParams(vmem_limit_bytes=VMEM_BYTES),
        cost_estimate=pl.CostEstimate(
            flops=int(flops * hint), bytes_accessed=int(size * hint), transcendentals=0
        ),
    )(*placed, *streamed)


def spot_in():
    index = lax.axis_index("seq")
    return index // 2, index % 2


def fetch_left(pieces, target, sems, columns, goal):
    _, core = spot_in()
    _, high = dp_place()
    rows = pieces[0].shape[0]
    copies = []
    for index, piece in enumerate(pieces):
        part = core if index < 2 else 1 - core
        side = high if index % 2 == 0 else 1 - high
        start = pl.multiple_of((part * 2 + side) * rows, 16)
        copy = pltpu.make_async_copy(
            piece.at[:, columns], target.at[pl.ds(start, rows), goal], sems.at[index]
        )
        copy.start()
        copies.append(copy)
    return copies


def fetch_whole(pieces, target, sems, columns, goal):
    _, core = spot_in()
    rows = pieces[0].shape[0]
    copies = []
    for index, piece in enumerate(pieces):
        part = core if index == 0 else 1 - core
        start = pl.multiple_of(part * rows, 16)
        copy = pltpu.make_async_copy(
            piece.at[:, columns], target.at[pl.ds(start, rows), goal], sems.at[index]
        )
        copy.start()
        copies.append(copy)
    return copies


def fetch_right(pieces, target, sems, columns, goal):
    _, core = spot_in()
    bit, _ = dp_place()
    rows = pieces[0].shape[0] // 2
    copies = []
    for index, piece in enumerate(pieces):
        part = core if index < 2 else 1 - core
        side = bit if index % 2 == 0 else 1 - bit
        for row in range(2):
            start = pl.multiple_of((part * 4 + row * 2 + side) * rows, 16)
            copy = pltpu.make_async_copy(
                piece.at[row * rows : (row + 1) * rows, columns],
                target.at[pl.ds(start, rows), goal],
                sems.at[2 * index + row],
            )
            copy.start()
            copies.append(copy)
    return copies


def wait_all(copies):
    for copy in copies:
        copy.wait()


def half_at(ref, part):
    half = ref.shape[1] // 2
    return ref[:, pl.ds(pl.multiple_of(part * half, LANES), half)]


def column_sum(values):
    return jnp.sum(values, 0, keepdims=True)


def fetch_project(layer, pieces, weight, left_sems, right_sems, width):
    if len(pieces) == 2:
        every = slice(0, 3 * width)
        return fetch_whole(pieces, weight, left_sems, every, every)
    first, last = slice(0, 2 * width), slice(2 * width, 3 * width)
    copies = fetch_left(pieces[:4], weight, left_sems, first, first)
    return copies + fetch_right(pieces[4:], weight, right_sems, slice(0, width), last)


def plain_rows(columns, perm):
    return lax.dot_general(
        columns, perm, (((0,), (1,)), ((), ())), preferred_element_type=F32
    )


def project_kernel(layer, chips, many, source, perm, bias, *rest):
    pieces, low_out, rest = rest[:many], rest[many], rest[many + 1 :]
    outs, (weight, stage, columns, *sems) = rest[:chips], rest[chips:]
    left_sems, right_sems, column_sems = sems
    chip, _ = spot_in()
    width = perm.shape[0]
    copies = fetch_project(layer, pieces, weight, left_sems, right_sems, width)
    if layer == 0:
        start = pieces[4].shape[1] - LANES
        column_copies = fetch_right(
            pieces[4:], columns, column_sems, slice(start, start + LANES), slice(0, LANES)
        )
        low = matmul(source[...], perm[...]).astype(BF)
        wait_all(column_copies)
        bias = plain_rows(columns[...], perm[...])
    else:
        low = source[...].astype(BF)
    low_out[...] = low
    wait_all(copies)
    group = width // chips
    for section in range(3):
        part = matmul(low, weight[:, section * width : (section + 1) * width])
        if section == 0:
            part = (part + bias[0:1]) * 0.125
        if section == 2:
            part = part + bias[1:2]
        part = part.astype(BF)
        for index in range(chips):
            stage[index, :, section * group : (section + 1) * group] = part[
                :, index * group : (index + 1) * group
            ]
    for step in range(chips):
        outs[step][...] = stage[lax.rem(chip + step, chips)]


def project_fast(layer, chips, source, perm, bias, pieces):
    rows, width = source.shape
    group = 3 * width // chips
    out = run(
        functools.partial(project_kernel, layer, chips, len(pieces)),
        "project",
        [shape((rows, width), BF)] + [shape((rows, group), BF)] * chips,
        [source, perm, bias],
        pieces,
        [
            pltpu.VMEM((width, 3 * width), BF),
            pltpu.VMEM((chips, rows, group), BF),
            pltpu.VMEM((width, LANES), BF),
            pltpu.SemaphoreType.DMA((4,)),
            pltpu.SemaphoreType.DMA((8,)),
            pltpu.SemaphoreType.DMA((8,)),
        ],
        flops=6 * rows * width * width,
    )
    return out[0], out[1:]


def fill_heads(blocks, others, group, queries, keys, values):
    rows = blocks[0].shape[0]
    for index, block in enumerate(blocks):
        cut = slice(index * rows, (index + 1) * rows)
        queries[cut, :] = block[:, :group]
        keys[cut, :] = block[:, group : 2 * group]
        values[cut, :] = block[:, 2 * group :]
    base = len(blocks) * rows
    for index, block in enumerate(others):
        cut = slice(base + index * rows, base + (index + 1) * rows)
        keys[cut, :] = block[:, group : 2 * group]
        values[cut, :] = block[:, 2 * group :]


def chunks_of(total):
    size = min(total, 256)
    return [slice(start, start + size) for start in range(0, total, size)]


def attend_kernel(chips, *refs):
    blocks, others = refs[:chips], refs[chips : 2 * chips]
    mixed, logs = refs[2 * chips : 2 * chips + 2]
    outs = refs[2 * chips + 2 : 3 * chips + 2]
    queries, keys, values = refs[3 * chips + 2 :]
    rows = blocks[0].shape[0]
    group = queries.shape[1]
    fill_heads(blocks, others, group, queries, keys, values)
    for head in range(group // HEAD):
        cut = slice(head * HEAD, (head + 1) * HEAD)
        key_head = keys[:, cut]
        value_head = values[:, cut]
        for part in chunks_of(chips * rows):
            scores = matmul_t(queries[part, cut], key_head)
            top = jnp.max(scores, -1, keepdims=True)
            power = jnp.exp(scores - top)
            total = jnp.sum(power, -1, keepdims=True)
            mixed[part, cut] = matmul(power.astype(BF), value_head) * (1.0 / total)
            logs[part, head : head + 1] = top + jnp.log(total)
    for index in range(chips):
        outs[index][...] = mixed[index * rows : (index + 1) * rows, :].astype(BF)


def attend_fast(chips, blocks, others):
    rows, wide = blocks[0].shape
    group = wide // 3
    span = chips * rows
    out = run(
        functools.partial(attend_kernel, chips),
        "attend",
        [shape((span, group), F32), shape((span, LANES), F32)]
        + [shape((rows, group), BF)] * chips,
        [*blocks, *others],
        (),
        [
            pltpu.VMEM((span, group), BF),
            pltpu.VMEM((2 * span, group), BF),
            pltpu.VMEM((2 * span, group), BF),
        ],
        flops=8 * span * span * group,
    )
    return out[0], out[1], out[2:]


def norm_in(residual):
    center = residual - jnp.mean(residual, -1, keepdims=True)
    spread = jnp.mean(center * center, -1, keepdims=True)
    scale = lax.rsqrt(spread + EPSILON)
    return center * scale, scale


def shrink_cut(index, wide, width):
    count = wide // width
    core, block = index // count, index % count
    half = width // 2
    return (
        slice(core * half, (core + 1) * half),
        slice(block * width, (block + 1) * width),
    )


def fetch_feed(weights, mixer, expand, shrink, sems):
    width, wide = expand.shape
    every, full = slice(0, width), slice(0, wide)
    return (
        fetch_right(weights[:4], mixer, sems[0], slice(width, 2 * width), every),
        fetch_whole(weights[4:], expand, sems[1], full, full),
        fetch_whole(weights[4:], shrink, sems[2], slice(wide, 2 * wide), full),
    )


def feed_kernel(layer, chips, many, hidden, low, perm, rows_in, wide_bias, *refs):
    pieces, refs = refs[:chips], refs[chips:]
    weights, refs = refs[:many], refs[many:]
    (out, attended, normed_low, pre_out, act_out, hat_one, scale_one, hat_two, scale_two,
     sent, squares) = refs[:11]
    stage, mixer, expand, shrink, *sems = refs[11:]
    chip, core = spot_in()
    width = perm.shape[0]
    wide = expand.shape[1]
    group = width // chips
    mixer_copies, expand_copies, shrink_copies = fetch_feed(
        weights, mixer, expand, shrink, sems
    )
    for step in range(chips):
        stage[lax.rem(chip + step, chips)] = pieces[step][...]
    moved = matmul(stage[0], perm[:group, :])
    for index in range(1, chips):
        moved += matmul(stage[index], perm[index * group : (index + 1) * group, :])
    moved = moved.astype(BF)
    attended[...] = moved
    wait_all(mixer_copies)
    attn_out = matmul(moved, mixer[...]) + rows_in[2:3]
    start = hidden[...].astype(F32)
    hat, scale = norm_in(start + attn_out)
    hat_one[...] = hat
    scale_one[...] = jnp.broadcast_to(scale, scale_one.shape)
    normed = hat * rows_in[3:4] + rows_in[4:5]
    normed_b = normed.astype(BF)
    normed_low[...] = normed_b
    squares[...] = jnp.zeros_like(squares)
    squares[0:1, :] = column_sum(start * start)
    squares[1:2, :] = column_sum(attn_out * attn_out)
    wait_all(expand_copies)
    wait_all(shrink_copies)
    half = width // 2
    total = None
    for index in range(wide // width):
        cut = slice(index * width, (index + 1) * width)
        pre = matmul(normed_b, expand[:, cut]) + wide_bias[:, cut]
        pre_out[:, cut] = pre
        act = (0.5 * pre * (1.0 + lax.erf(pre * ROOT_HALF))).astype(BF)
        act_out[:, cut] = act
        for side in range(2):
            rows, columns = shrink_cut(2 * index + side, wide, width)
            term = matmul(act[:, side * half : (side + 1) * half], shrink[rows, columns])
            total = term if total is None else total + term
    ffn_out = total + rows_in[9:10]
    squares[2:3, :] = column_sum(ffn_out * ffn_out)
    hat, scale = norm_in(normed + ffn_out)
    hat_two[...] = hat
    scale_two[...] = jnp.broadcast_to(scale, scale_two.shape)
    out[...] = hat * rows_in[10:11] + rows_in[11:12]
    for index, member in enumerate((low, attended, normed_low)):
        sent[:, index * half : (index + 1) * half] = half_at(member, 1 - core)
    sent[:, 3 * half :] = half_at(act_out, 1 - core)


def feed_fast(layer, chips, hidden, low, perm, vectors, wide_bias, pieces, weights):
    rows, width = hidden.shape
    wide = wide_bias.shape[1]
    return run(
        functools.partial(feed_kernel, layer, chips, len(weights)),
        "feed",
        [
            shape((rows, width), F32),
            shape((rows, width), BF),
            shape((rows, width), BF),
            shape((rows, wide), F32),
            shape((rows, wide), BF),
            shape((rows, width), F32),
            shape((rows, LANES), F32),
            shape((rows, width), F32),
            shape((rows, LANES), F32),
            shape((rows, (3 * width + wide) // 2), BF),
            shape((8, width), F32),
        ],
        [hidden, low, perm, vectors, wide_bias, *pieces],
        weights,
        [
            pltpu.VMEM((chips, rows, width // chips), BF),
            pltpu.VMEM((width, width), BF),
            pltpu.VMEM((width, wide), BF),
            pltpu.VMEM((width, wide), BF),
            pltpu.SemaphoreType.DMA((8,)),
            pltpu.SemaphoreType.DMA((4,)),
            pltpu.SemaphoreType.DMA((8,)),
        ],
        flops=4 * rows * width * (wide + width),
    )


def norm_back(grad, hat, scale):
    first = jnp.mean(grad, -1, keepdims=True)
    second = jnp.mean(grad * hat, -1, keepdims=True)
    return (grad - first - hat * second) * scale


def feed_back_kernel(
    layer, chips, many, source, perm, perm_wide, vectors, hat_one, scale_one, hat_two, scale_two,
    pre_in, *refs
):
    weights, refs = refs[:many], refs[many:]
    grad_one_out, gave, attn_nat, sums = refs[:4]
    outs = refs[4 : 4 + chips]
    stage, grad_pre, mixer, expand, shrink, *sems = refs[4 + chips :]
    chip, _ = spot_in()
    width = perm.shape[0]
    wide = expand.shape[1]
    group = width // chips
    half = width // 2
    mixer_copies, expand_copies, shrink_copies = fetch_feed(
        weights, mixer, expand, shrink, sems
    )
    grad = matmul(source[...], perm[...]) if layer == LAYERS - 1 else source[...]
    hat = hat_two[...]
    sums[...] = jnp.zeros_like(sums)
    sums[10:11, :] = column_sum(grad * hat)
    sums[11:12, :] = column_sum(grad)
    grad_two = norm_back(grad * vectors[10:11], hat, scale_two[:, 0:1])
    grad_ffn = grad_two.astype(BF)
    sums[9:10, :] = column_sum(grad_ffn.astype(F32))
    gave[:, :width] = matmul_t(grad_ffn, perm[...]).astype(BF)
    wait_all(shrink_copies)
    wait_all(expand_copies)
    grad_normed = grad_two
    for index in range(wide // width):
        cut = slice(index * width, (index + 1) * width)
        pre = pre_in[:, cut]
        slope = 0.5 * (1.0 + lax.erf(pre * ROOT_HALF)) + pre * (
            jnp.exp(-0.5 * pre * pre) * ROOT_TAU
        )
        sides = []
        for side in range(2):
            rows, columns = shrink_cut(2 * index + side, wide, width)
            sides.append(matmul_t(grad_ffn, shrink[rows, columns]))
        part = (jnp.concatenate(sides, 1) * slope).astype(BF)
        grad_pre[:, cut] = part
        grad_normed += matmul_t(part, expand[:, cut])
    groups = wide // width
    piece = half // groups
    for index in range(groups):
        joined = jnp.concatenate(
            [
                grad_pre[:, spot * half + index * piece : spot * half + (index + 1) * piece]
                for spot in range(2 * groups)
            ],
            1,
        )
        moved = matmul_t(joined, perm_wide[...])
        sums[5 + index : 6 + index, :] = column_sum(moved)
        gave[:, (index + 1) * width : (index + 2) * width] = moved.astype(BF)
    hat = hat_one[...]
    sums[3:4, :] = column_sum(grad_normed * hat)
    sums[4:5, :] = column_sum(grad_normed)
    grad_one = norm_back(grad_normed * vectors[3:4], hat, scale_one[:, 0:1])
    grad_one_out[...] = grad_one
    grad_attn = grad_one.astype(BF)
    sums[2:3, :] = column_sum(grad_attn.astype(F32))
    attn_nat[...] = matmul_t(grad_attn, perm[...]).astype(BF)
    wait_all(mixer_copies)
    grad_mixed = matmul_t(grad_attn, mixer[...]).astype(BF)
    for index in range(chips):
        stage[index] = matmul_t(
            grad_mixed, perm[index * group : (index + 1) * group, :]
        ).astype(BF)
    for step in range(chips):
        outs[step][...] = stage[lax.rem(chip + step, chips)]


def feed_back_fast(layer, chips, source, perm, perm_wide, vectors, saved, weights):
    rows, width = source.shape
    wide = saved[-1].shape[1]
    out = run(
        functools.partial(feed_back_kernel, layer, chips, len(weights)),
        "feed_back",
        [
            shape((rows, width), F32),
            shape((rows, width + wide), BF),
            shape((rows, width), BF),
            shape((16, width), F32),
        ]
        + [shape((rows, width // chips), BF)] * chips,
        [source, perm, perm_wide, vectors, *saved],
        weights,
        [
            pltpu.VMEM((chips, rows, width // chips), BF),
            pltpu.VMEM((rows, wide), BF),
            pltpu.VMEM((width, width), BF),
            pltpu.VMEM((width, wide), BF),
            pltpu.VMEM((width, wide), BF),
            pltpu.SemaphoreType.DMA((8,)),
            pltpu.SemaphoreType.DMA((4,)),
            pltpu.SemaphoreType.DMA((8,)),
        ],
        flops=4 * rows * width * (wide + 2 * width),
    )
    return out[0], out[1], out[2], out[3], out[4:]


def fetch_rows(pieces, target, sems, start):
    _, core = spot_in()
    rows, width = pieces[0].shape[0], target.shape[1]
    copies = []
    for index, piece in enumerate(pieces):
        part = core if index == 0 else 1 - core
        for block in range(4):
            goal = pl.multiple_of((part * 4 + block) * rows, 16)
            copy = pltpu.make_async_copy(
                piece.at[:, start + block * width : start + (block + 1) * width],
                target.at[pl.ds(goal, rows), :],
                sems.at[4 * index + block],
            )
            copy.start()
            copies.append(copy)
    return copies


def fetch_blocks(pieces, target, sems):
    _, core = spot_in()
    spot = lax.axis_index("dp")
    rows, width = pieces[0].shape[0], target.shape[1]
    copies = []
    for index, piece in enumerate(pieces):
        part = core if index == 0 else 1 - core
        for bits in range(4):
            goal = pl.multiple_of((part * 4 + jnp.bitwise_xor(spot, bits)) * rows, 16)
            copy = pltpu.make_async_copy(
                piece.at[:, bits * width : (bits + 1) * width],
                target.at[pl.ds(goal, rows), :],
                sems.at[4 * index + bits],
            )
            copy.start()
            copies.append(copy)
    return copies


def mix_kernel(chips, hidden, low, perm, rows_in, *refs):
    pieces, refs = refs[:chips], refs[chips:]
    weights, refs = refs[:4], refs[4:]
    attended, normed_out, normed_low, hat_one, scale_one, sent, squares = refs[:7]
    stage, mixer, sems = refs[7:]
    chip, core = spot_in()
    width = perm.shape[0]
    group = width // chips
    half = width // 2
    copies = fetch_right(weights, mixer, sems, slice(width, 2 * width), slice(0, width))
    for step in range(chips):
        stage[lax.rem(chip + step, chips)] = pieces[step][...]
    moved = matmul(stage[0], perm[:group, :])
    for index in range(1, chips):
        moved += matmul(stage[index], perm[index * group : (index + 1) * group, :])
    moved = moved.astype(BF)
    attended[...] = moved
    wait_all(copies)
    attn_out = matmul(moved, mixer[...]) + rows_in[2:3]
    start = hidden[...].astype(F32)
    hat, scale = norm_in(start + attn_out)
    hat_one[...] = hat
    scale_one[...] = jnp.broadcast_to(scale, scale_one.shape)
    normed = hat * rows_in[3:4] + rows_in[4:5]
    normed_out[...] = normed
    normed_low[...] = normed.astype(BF)
    squares[...] = jnp.zeros_like(squares)
    squares[0:1, :] = column_sum(start * start)
    squares[1:2, :] = column_sum(attn_out * attn_out)
    sent[:, :half] = half_at(low, 1 - core)
    sent[:, half:] = half_at(attended, 1 - core)


def mix_fast(chips, hidden, low, perm, vectors, pieces, weights):
    rows, width = hidden.shape
    return run(
        functools.partial(mix_kernel, chips),
        "mix",
        [
            shape((rows, width), BF),
            shape((rows, width), F32),
            shape((rows, width), BF),
            shape((rows, width), F32),
            shape((rows, LANES), F32),
            shape((rows, width), BF),
            shape((8, width), F32),
        ],
        [hidden, low, perm, vectors, *pieces],
        weights,
        [
            pltpu.VMEM((chips, rows, width // chips), BF),
            pltpu.VMEM((width, width), BF),
            pltpu.SemaphoreType.DMA((8,)),
        ],
        flops=4 * rows * width * width,
    )


def slice_row(wide_bias):
    spot = lax.axis_index("dp")
    line = lax.broadcasted_iota(jnp.int32, wide_bias.shape, 0)
    return jnp.sum(jnp.where(line == spot, wide_bias[...], 0.0), 0, keepdims=True)


def slice_feed_kernel(wide_bias, *refs):
    peers = 4
    blocks, weights, refs = refs[:peers], refs[peers : peers + 2], refs[peers + 2 :]
    near, sends, refs = refs[0], refs[1:peers], refs[peers:]
    pre_out, act_out, expand, shrink, expand_sems, shrink_sems = refs
    rows, width = blocks[0].shape
    expand_copies = fetch_blocks(weights, expand, expand_sems)
    shrink_copies = fetch_rows(weights, shrink, shrink_sems, 4 * width)
    bias = slice_row(wide_bias)
    wait_all(expand_copies)
    tokens = jnp.concatenate([block[...] for block in blocks], 0)
    pre = matmul(tokens, expand[...]) + bias
    pre_out[...] = pre
    act = (0.5 * pre * (1.0 + lax.erf(pre * ROOT_HALF))).astype(BF)
    act_out[...] = act
    wait_all(shrink_copies)
    part = matmul(act, shrink[...])
    near[...] = part[:rows]
    for index, out in enumerate(sends):
        out[...] = part[(index + 1) * rows : (index + 2) * rows].astype(BF)


def slice_scratch(width):
    return [
        pltpu.VMEM((width, width), BF),
        pltpu.VMEM((width, width), BF),
        pltpu.SemaphoreType.DMA((8,)),
        pltpu.SemaphoreType.DMA((8,)),
    ]


def slice_feed_fast(wide_bias, blocks, weights):
    rows, width = blocks[0].shape
    out = run(
        slice_feed_kernel,
        "slice_feed",
        [shape((rows, width), F32)]
        + [shape((rows, width), BF)] * 3
        + [shape((4 * rows, width), F32), shape((4 * rows, width), BF)],
        [wide_bias, *blocks],
        weights,
        slice_scratch(width),
        flops=16 * rows * width * width,
    )
    return out[:4], out[4], out[5]


def peer_sum(parts):
    total = parts[0][...]
    for part in parts[1:]:
        total = total + part[...].astype(F32)
    return total


def finish_kernel(normed, rows_in, squares_in, *refs):
    parts, (out, hat_two, scale_two, squares) = refs[:4], refs[4:]
    ffn_out = peer_sum(parts) + rows_in[9:10]
    squares[...] = squares_in[...]
    squares[2:3, :] = column_sum(ffn_out * ffn_out)
    hat, scale = norm_in(normed[...] + ffn_out)
    hat_two[...] = hat
    scale_two[...] = jnp.broadcast_to(scale, scale_two.shape)
    out[...] = hat * rows_in[10:11] + rows_in[11:12]


def finish_fast(normed, vectors, squares, parts):
    rows, width = normed.shape
    return run(
        finish_kernel,
        "finish",
        [
            shape((rows, width), F32),
            shape((rows, width), F32),
            shape((rows, LANES), F32),
            shape(squares.shape, F32),
        ],
        [normed, vectors, squares, *parts],
    )


def finish_back_kernel(first, source, perm, vectors, hat_two, scale_two, grad_out, low_out, sums):
    grad = matmul(source[...], perm[...]) if first else source[...]
    hat = hat_two[...]
    sums[...] = jnp.zeros_like(sums)
    sums[10:11, :] = column_sum(grad * hat)
    sums[11:12, :] = column_sum(grad)
    grad_two = norm_back(grad * vectors[10:11], hat, scale_two[:, 0:1])
    grad_out[...] = grad_two
    low = grad_two.astype(BF)
    low_out[...] = low
    sums[9:10, :] = column_sum(low.astype(F32))


def finish_back_fast(first, source, perm, vectors, hat_two, scale_two):
    rows, width = source.shape
    return run(
        functools.partial(finish_back_kernel, first),
        "finish_back",
        [shape((rows, width), F32), shape((rows, width), BF), shape((16, width), F32)],
        [source, perm, vectors, hat_two, scale_two],
    )


def slice_back_kernel(*refs):
    peers = 4
    blocks, refs = refs[:peers], refs[peers:]
    inputs, refs = refs[:peers], refs[peers:]
    pre_in, act_in, weights, refs = refs[0], refs[1], refs[2:4], refs[4:]
    near, sends, refs = refs[0], refs[1:peers], refs[peers:]
    slope_out, gave, sums, expand, shrink, expand_sems, shrink_sems = refs
    _, core = spot_in()
    rows, width = blocks[0].shape
    half = width // 2
    shrink_copies = fetch_rows(weights, shrink, shrink_sems, 4 * width)
    expand_copies = fetch_blocks(weights, expand, expand_sems)
    for index in range(peers):
        span = slice(index * rows, (index + 1) * rows)
        gave[span, :half] = half_at(inputs[index], 1 - core)
        gave[span, width : 2 * width] = blocks[index][...]
    gave[:, half:width] = half_at(act_in, 1 - core)
    tokens = jnp.concatenate([block[...] for block in blocks], 0)
    pre = pre_in[...]
    slope = 0.5 * (1.0 + lax.erf(pre * ROOT_HALF)) + pre * (
        jnp.exp(-0.5 * pre * pre) * ROOT_TAU
    )
    wait_all(shrink_copies)
    grad_pre = (matmul_t(tokens, shrink[...]) * slope).astype(BF)
    slope_out[...] = grad_pre
    gave[:, 2 * width :] = grad_pre
    sums[...] = jnp.broadcast_to(column_sum(grad_pre.astype(F32)), sums.shape)
    wait_all(expand_copies)
    part = matmul_t(grad_pre, expand[...])
    near[...] = part[:rows]
    for index, out in enumerate(sends):
        out[...] = part[(index + 1) * rows : (index + 2) * rows].astype(BF)


def slice_back_fast(blocks, inputs, pre, act, weights):
    rows, width = blocks[0].shape
    out = run(
        slice_back_kernel,
        "slice_back",
        [shape((rows, width), F32)]
        + [shape((rows, width), BF)] * 3
        + [
            shape((4 * rows, width), BF),
            shape((4 * rows, 3 * width), BF),
            shape((8, width), F32),
        ],
        [*blocks, *inputs, pre, act],
        weights,
        slice_scratch(width),
        flops=16 * rows * width * width,
    )
    return out[:4], out[4], out[5], out[6]


def slice_terms_kernel(peers, perm_rows, perm_units, *refs):
    blocks, inputs, refs = refs[:peers], refs[peers : 2 * peers], refs[2 * peers :]
    act_in, slope, theirs, out = refs
    _, core = spot_in()
    width = slope.shape[1]
    half = width // 2
    left = jnp.concatenate(
        [half_at(member, core) for member in inputs] + [theirs[:, :half]], 0
    )
    left = matmul(left, perm_rows[...]).astype(BF)
    right = jnp.concatenate([slope[...], theirs[:, 2 * width :]], 0)
    out[:, :width] = grad_matmul(left, right).astype(BF)
    left = jnp.concatenate([half_at(act_in, core), theirs[:, half:width]], 0)
    left = matmul(left, perm_units[...]).astype(BF)
    right = jnp.concatenate(
        [block[...] for block in blocks] + [theirs[:, width : 2 * width]], 0
    )
    out[:, width:] = grad_matmul(left, right).astype(BF)


def slice_terms_fast(perm_rows, perm_units, blocks, inputs, act, slope, theirs):
    rows, width = blocks[0].shape
    return run(
        functools.partial(slice_terms_kernel, 4),
        "slice_terms",
        [shape((width // 2, 2 * width), BF)],
        [perm_rows, perm_units, *blocks, *inputs, act, slope, theirs],
        flops=16 * rows * width * width,
    )[0]


def mix_back_kernel(chips, grad_two, perm, vectors, hat_one, scale_one, sums_in, *refs):
    parts, weights, refs = refs[:4], refs[4:8], refs[8:]
    grad_one_out, attn_nat, sums = refs[:3]
    outs = refs[3 : 3 + chips]
    stage, mixer, sems = refs[3 + chips :]
    chip, _ = spot_in()
    width = perm.shape[0]
    group = width // chips
    copies = fetch_right(weights, mixer, sems, slice(width, 2 * width), slice(0, width))
    grad_normed = grad_two[...] + peer_sum(parts)
    hat = hat_one[...]
    sums[...] = sums_in[...]
    sums[3:4, :] = column_sum(grad_normed * hat)
    sums[4:5, :] = column_sum(grad_normed)
    grad_one = norm_back(grad_normed * vectors[3:4], hat, scale_one[:, 0:1])
    grad_one_out[...] = grad_one
    grad_attn = grad_one.astype(BF)
    sums[2:3, :] = column_sum(grad_attn.astype(F32))
    attn_nat[...] = matmul_t(grad_attn, perm[...]).astype(BF)
    wait_all(copies)
    grad_mixed = matmul_t(grad_attn, mixer[...]).astype(BF)
    for index in range(chips):
        stage[index] = matmul_t(
            grad_mixed, perm[index * group : (index + 1) * group, :]
        ).astype(BF)
    for step in range(chips):
        outs[step][...] = stage[lax.rem(chip + step, chips)]


def mix_back_fast(chips, grad_two, perm, vectors, hat_one, scale_one, sums, parts, weights):
    rows, width = grad_two.shape
    out = run(
        functools.partial(mix_back_kernel, chips),
        "mix_back",
        [shape((rows, width), F32), shape((rows, width), BF), shape((16, width), F32)]
        + [shape((rows, width // chips), BF)] * chips,
        [grad_two, perm, vectors, hat_one, scale_one, sums, *parts],
        weights,
        [
            pltpu.VMEM((chips, rows, width // chips), BF),
            pltpu.VMEM((width, width), BF),
            pltpu.SemaphoreType.DMA((8,)),
        ],
        flops=6 * rows * width * width,
    )
    return out[0], out[1], out[2], out[3:]


def attend_back_kernel(chips, *refs):
    blocks, refs = refs[:chips], refs[chips:]
    others, refs = refs[:chips], refs[chips:]
    grads, refs = refs[:chips], refs[chips:]
    mixed, logs, grad_q, near, far, queries, keys, values, grad_in, key_sum, value_sum = refs
    rows = blocks[0].shape[0]
    group = queries.shape[1]
    span = chips * rows
    fill_heads(blocks, others, group, queries, keys, values)
    for index in range(chips):
        grad_in[index * rows : (index + 1) * rows, :] = grads[index][...]
    for head in range(group // HEAD):
        cut = slice(head * HEAD, (head + 1) * HEAD)
        key_head = keys[:, cut]
        value_head = values[:, cut]
        for place_in, part in enumerate(chunks_of(span)):
            query = queries[part, cut]
            grad = grad_in[part, cut]
            delta = jnp.sum(grad.astype(F32) * mixed[part, cut], -1, keepdims=True)
            probability = jnp.exp(matmul_t(query, key_head) - logs[part, head : head + 1])
            slope = matmul_t(grad, value_head) - delta
            grad_scores = (probability * slope).astype(BF)
            grad_q[part, cut] = (matmul(grad_scores, key_head) * 0.125).astype(BF)
            key_term = grad_matmul(grad_scores, query)
            value_term = grad_matmul(probability.astype(BF), grad)
            if place_in == 0:
                key_sum[:, cut] = key_term
                value_sum[:, cut] = value_term
            else:
                key_sum[:, cut] += key_term
                value_sum[:, cut] += value_term
    near[:, :group] = key_sum[:span, :]
    near[:, group:] = value_sum[:span, :]
    far[:, :group] = key_sum[span:, :].astype(BF)
    far[:, group:] = value_sum[span:, :].astype(BF)


def attend_back_fast(chips, blocks, others, grads, mixed, logs):
    rows, wide = blocks[0].shape
    group = wide // 3
    span = chips * rows
    return run(
        functools.partial(attend_back_kernel, chips),
        "attend_back",
        [
            shape((span, group), BF),
            shape((span, 2 * group), F32),
            shape((span, 2 * group), BF),
        ],
        [*blocks, *others, *grads, mixed, logs],
        (),
        [
            pltpu.VMEM((span, group), BF),
            pltpu.VMEM((2 * span, group), BF),
            pltpu.VMEM((2 * span, group), BF),
            pltpu.VMEM((span, group), BF),
            pltpu.VMEM((2 * span, group), F32),
            pltpu.VMEM((2 * span, group), F32),
        ],
        flops=20 * span * span * group,
    )


def combine_kernel(grad_q, near, far, *outs):
    rows, wide = outs[0].shape
    group = wide // 3
    for index, out in enumerate(outs):
        cut = slice(index * rows, (index + 1) * rows)
        out[:, :group] = grad_q[cut, :]
        out[:, group:] = (near[cut, :] + far[cut, :].astype(F32)).astype(BF)


def combine_fast(chips, grad_q, near, far):
    span, group = grad_q.shape
    return run(
        combine_kernel,
        "combine",
        [shape((span // chips, 3 * group), BF)] * chips,
        [grad_q, near, far],
    )


def exact_move(values, perm):
    high = values.astype(BF)
    rest = values - high.astype(F32)
    middle = rest.astype(BF)
    low = (rest - middle.astype(F32)).astype(BF)
    return matmul(high, perm) + matmul(middle, perm) + matmul(low, perm)


def collect(chips, stage, pieces, project):
    chip, _ = spot_in()
    width = project.shape[1] // 3
    group = width // chips
    for step in range(chips):
        stage[lax.rem(chip + step, chips)] = pieces[step][...]
    for section in range(3):
        cut = slice(section * group, (section + 1) * group)
        joined = jnp.concatenate([stage[index][:, cut] for index in range(chips)], 1)
        project[:, section * width : (section + 1) * width] = joined


def through_project(grad, project, weight):
    width = grad.shape[1]
    for section in range(3):
        cut = slice(section * width, (section + 1) * width)
        grad += matmul_t(project[:, cut], weight[:, cut])
    return grad


def project_back_kernel(layer, chips, many, grad_one, perm, sums, *refs):
    pieces, refs = refs[:chips], refs[chips:]
    weights, refs = refs[:many], refs[many:]
    out, project, vector_out, stage, weight, left_sems, right_sems = refs
    copies = fetch_project(layer, weights, weight, left_sems, right_sems, perm.shape[0])
    collect(chips, stage, pieces, project)
    wait_all(copies)
    out[...] = through_project(grad_one[...], project, weight)
    vector_rows(project, sums, perm, vector_out)


def collect_kernel(chips, perm, perm_wide, feed_sums, sums, *refs):
    pieces, refs = refs[:chips], refs[chips:]
    project, vector_out, stage = refs
    collect(chips, stage, pieces, project)
    slice_vector_rows(project, sums, feed_sums, perm, perm_wide, vector_out)


def collect_fast(chips, perm, perm_wide, feed_sums, sums, pieces):
    rows, group = pieces[0].shape
    return run(
        functools.partial(collect_kernel, chips),
        "collect",
        [shape((rows, chips * group), BF), shape(sums.shape, F32)],
        [perm, perm_wide, feed_sums, sums, *pieces],
        (),
        [pltpu.VMEM((chips, rows, group), BF)],
    )


def input_back_kernel(grad_one, perm, project, *refs):
    weights, refs = refs[:8], refs[8:]
    out, weight, left_sems, right_sems = refs
    wait_all(fetch_project(0, weights, weight, left_sems, right_sems, perm.shape[0]))
    grad = through_project(grad_one[...], project, weight)
    out[...] = matmul_t(grad.astype(BF), perm[...]).astype(BF)


def input_back_fast(grad_one, perm, project, weights):
    rows, width = grad_one.shape
    return run(
        input_back_kernel,
        "input_back",
        [shape((rows, width), BF)],
        [grad_one, perm, project],
        weights,
        [
            pltpu.VMEM((width, 3 * width), BF),
            pltpu.SemaphoreType.DMA((4,)),
            pltpu.SemaphoreType.DMA((8,)),
        ],
        flops=6 * rows * width * width,
    )[0]


def exact_back(values, perm):
    high = values.astype(BF)
    rest = values - high.astype(F32)
    middle = rest.astype(BF)
    low = (rest - middle.astype(F32)).astype(BF)
    return matmul_t(high, perm) + matmul_t(middle, perm) + matmul_t(low, perm)


def slice_vector_rows(project, sums, feed_sums, perm, perm_wide, vector_out):
    width = perm.shape[0]
    spot = lax.axis_index("dp")
    vector_out[...] = sums[...]
    line = lax.broadcasted_iota(jnp.int32, (8, width), 0)
    rows = exact_back(feed_sums[...], perm_wide[...])
    first = column_sum(project[:, :width].astype(F32))
    second = column_sum(project[:, 2 * width :].astype(F32))
    rows = jnp.where(line == 0, first, jnp.where(line == 1, second, rows))
    moved = exact_move(rows, perm[...])
    vector_out[0:2, :] = moved[0:2, :]
    wide_line = lax.broadcasted_iota(jnp.int32, (16, width), 0)
    vector_out[...] = jnp.where(wide_line == 5 + spot, moved[2:3, :], vector_out[...])


def vector_rows(project, sums, perm, vector_out):
    width = perm.shape[0]
    vector_out[...] = sums[...]
    vector_out[0:1, :] = column_sum(project[:, :width].astype(F32))
    vector_out[1:2, :] = column_sum(project[:, 2 * width :].astype(F32))
    moved = exact_move(vector_out[0:8, :], perm[...])
    vector_out[0:2, :] = moved[0:2, :]
    vector_out[5:8, :] = moved[5:8, :]
    moved = exact_move(vector_out[8:16, :], perm[...])
    vector_out[8:9, :] = moved[0:1, :]


def project_back_fast(layer, chips, grad_one, perm, sums, pieces, weights):
    rows, width = grad_one.shape
    return run(
        functools.partial(project_back_kernel, layer, chips, len(weights)),
        "project_back",
        [
            shape((rows, width), F32),
            shape((rows, 3 * width), BF),
            shape((16, width), F32),
        ],
        [grad_one, perm, sums, *pieces],
        weights,
        [
            pltpu.VMEM((chips, rows, 3 * width // chips), BF),
            pltpu.VMEM((width, 3 * width), BF),
            pltpu.SemaphoreType.DMA((4,)),
            pltpu.SemaphoreType.DMA((8,)),
        ],
        flops=6 * rows * width * width,
    )


def feed_terms_kernel(normed, act, gave, theirs, gave_theirs, out):
    _, core = spot_in()
    width = normed.shape[1]
    half = width // 2
    left = jnp.concatenate([half_at(normed, core), theirs[:, 2 * half : 3 * half]], 0)
    count = act.shape[1] // width
    for index in range(count):
        cut = slice(index * width, (index + 1) * width)
        far = slice((index + 1) * width, (index + 2) * width)
        right = jnp.concatenate([gave[:, far], gave_theirs[:, far]], 0)
        out[:, cut] = grad_matmul(left, right).astype(BF)
    left = jnp.concatenate([half_at(act, core), theirs[:, 3 * half :]], 0)
    right = jnp.concatenate([gave[:, :width], gave_theirs[:, :width]], 0)
    for index in range(count):
        cut = slice(index * half, (index + 1) * half)
        spot = slice((count + index) * width, (count + index + 1) * width)
        out[:, spot] = grad_matmul(left[:, cut], right).astype(BF)


def feed_terms_fast(normed, act, gave, theirs, gave_theirs):
    rows, width = normed.shape
    wide = act.shape[1]
    return run(
        feed_terms_kernel,
        "feed_terms",
        [shape((width // 2, 2 * wide), BF)],
        [normed, act, gave, theirs, gave_theirs],
        flops=4 * rows * width * wide,
    )[0]


def attend_terms_kernel(
    low, attended, project, attn_nat, vector, theirs, project_theirs, attn_theirs,
    vector_theirs, left_keep, left_sent, right_keep, right_sent
):
    _, core = spot_in()
    bit, high = dp_place()
    width = low.shape[1]
    half = width // 2
    block = half // 4

    def put_left(columns, value):
        value = value.astype(BF)
        for side in range(2):
            first = value[2 * side * block : (2 * side + 1) * block]
            second = value[(2 * side + 1) * block : (2 * side + 2) * block]
            rows = slice(side * block, (side + 1) * block)
            left_keep[rows, columns] = jnp.where(bit == 0, first, second)
            left_sent[rows, columns] = jnp.where(bit == 0, second, first)

    def put_right(columns, value):
        value = value.astype(BF)
        first, second = value[: 2 * block], value[2 * block :]
        right_keep[:, columns] = jnp.where(high == 0, first, second)
        right_sent[:, columns] = jnp.where(high == 0, second, first)

    left = jnp.concatenate([half_at(low, core), theirs[:, :half]], 0)
    for index in range(3):
        cut = slice(index * width, (index + 1) * width)
        right = jnp.concatenate([project[:, cut], project_theirs[:, cut]], 0)
        if index < 2:
            put_left(cut, grad_matmul(left, right))
        else:
            put_right(slice(0, width), grad_matmul(left, right))
    left = jnp.concatenate([half_at(attended, core), theirs[:, half : 2 * half]], 0)
    right = jnp.concatenate([attn_nat[...], attn_theirs[...]], 0)
    put_right(slice(width, 2 * width), grad_matmul(left, right))
    rows = half_at(vector, core) + half_at(vector_theirs, core)
    upper = rows.astype(BF)
    rest = (rows - upper.astype(F32)).astype(BF)
    count = rows.shape[0]
    line = lax.broadcasted_iota(jnp.int32, (count, LANES), 0)
    lane = lax.broadcasted_iota(jnp.int32, (count, LANES), 1)
    extra = grad_matmul(upper, (lane == line).astype(BF))
    extra += grad_matmul(rest, (lane == line + count).astype(BF))
    put_right(slice(2 * width, 2 * width + LANES), extra)


def attend_terms_fast(*args):
    rows, width = args[0].shape
    return run(
        attend_terms_kernel,
        "attend_terms",
        [shape((width // 4, 2 * width), BF)] * 2
        + [shape((width // 4, 2 * width + LANES), BF)] * 2,
        list(args),
        flops=16 * rows * width * width // 2,
    )


def after(array, *others):
    return lax.optimization_barrier((array, *others))[0]


def chips_parts(array):
    return [array] + [chip_shift(array, step) for step in range(1, chips_of())]


def chips_gather(array):
    return lax.all_gather(
        array, "seq", axis=0, tiled=True, axis_index_groups=core_groups()
    )


def chips_scatter(array):
    return lax.psum_scatter(
        array, "seq", scatter_dimension=0, tiled=True, axis_index_groups=core_groups()
    )


def chips_join(parts):
    chips = chips_of()
    chip, _ = place()
    return jnp.concatenate(
        [
            lax.select_n(chip, *[parts[(spot - index) % chips] for spot in range(chips)])
            for index in range(chips)
        ],
        0,
    )


def dp_swap(array, bit):
    size = lax.axis_size("dp")
    return lax.ppermute(array, "dp", [(i, i ^ bit) for i in range(size)])


def dp_place():
    spot = lax.axis_index("dp")
    return spot % 2, spot // 2


def join_pair(bit, own, other):
    return jnp.where(
        bit == 0, jnp.concatenate([own, other], 0), jnp.concatenate([other, own], 0)
    )


def square_first(part, cut):
    left, right = part[:, :cut], part[:, cut:]
    return left, dp_swap(left, 1), right, dp_swap(right, 2)


def square_second(left, left_far, right, right_far):
    bit, high = dp_place()
    left_far, right_far = lax.optimization_barrier((left_far, right_far))
    left = join_pair(bit, left, left_far)
    right = join_pair(high, right, right_far)
    return left, dp_swap(left, 2), right, dp_swap(right, 1)


def square_pieces(left, left_far, right, right_far):
    near = [core_swap(left), core_swap(right)]
    left_far, right_far = lax.optimization_barrier((left_far, right_far))
    return [
        left, left_far, near[0], core_swap(left_far),
        right, right_far, near[1], core_swap(right_far),
    ]


def vectors_kernel(groups, perm, perm_wide, *refs):
    pieces, refs = refs[:4], refs[4:]
    outs, (stage, sems) = refs[:-2], refs[-2:]
    width = perm.shape[0]
    start = pieces[0].shape[1] - LANES
    wait_all(
        fetch_right(pieces, stage, sems, slice(start, start + LANES), slice(0, LANES))
    )
    columns = stage[...]
    line = lax.broadcasted_iota(jnp.int32, (width, width), 0)
    spot = lax.broadcasted_iota(jnp.int32, (width, width), 1)
    moved = grad_matmul(columns, (line == spot).astype(BF))
    plain = plain_rows(columns, perm[...])
    wide = matmul(plain.astype(BF), perm_wide[...])
    piece = width // (2 * groups)
    for layer in range(LAYERS):
        base = layer * VECS
        moved_out, plain_out, wide_out = outs[3 * layer : 3 * layer + 3]
        moved_out[:VECS, :] = moved[base : base + VECS]
        plain_out[:VECS, :] = plain[base : base + VECS]
        if layer == 0:
            wide_out[...] = wide[base + 5 : base + 5 + groups]
            continue
        for index in range(groups):
            row = base + 5 + index
            for part in range(2 * groups):
                goal = part * groups * piece + index * piece
                wide_out[:, goal : goal + piece] = wide[
                    row : row + 1, part * piece : (part + 1) * piece
                ]


def vectors_fast(groups, perm, perm_wide, pieces):
    width = perm.shape[0]
    out = run(
        functools.partial(vectors_kernel, groups),
        "vectors",
        [
            *[shape((16, width), F32)] * 2,
            shape((groups, width), F32),
            *[shape((16, width), F32)] * 2,
            shape((1, groups * width), F32),
        ],
        [perm, perm_wide],
        pieces,
        [pltpu.VMEM((width, LANES), BF), pltpu.SemaphoreType.DMA((8,))],
    )
    return [out[:3], out[3:]]


def fold_kernel(*refs):
    bit, high = dp_place()
    for index, flag in enumerate((high, bit)):
        keep, came, keep_out, sent_out = (refs[index * 2], refs[index * 2 + 1],
                                          refs[4 + index * 2], refs[5 + index * 2])
        rows = keep.shape[0] // 2
        total = keep[...].astype(F32) + came[...].astype(F32)
        keep_out[...] = jnp.where(flag == 0, total[:rows], total[rows:]).astype(BF)
        sent_out[...] = jnp.where(flag == 0, total[rows:], total[:rows]).astype(BF)


def split_kernel(chips, *refs):
    left, left_far, right, right_far = refs[:4]
    own, sends, total = refs[4], refs[5 : 4 + chips], refs[4 + chips]
    chip, _ = spot_in()
    cut = left.shape[1]
    rows = left.shape[0] // chips
    for index in range(chips):
        span = slice(index * rows, (index + 1) * rows)
        total[index, :, :cut] = left[span, :].astype(F32) + left_far[span, :].astype(F32)
        total[index, :, cut:] = right[span, :].astype(F32) + right_far[span, :].astype(F32)
    own[...] = total[chip]
    for step in range(1, chips):
        sends[step - 1][...] = total[lax.rem(chip + step, chips)].astype(BF)


def square_fold(parts):
    left, left_sent, right, right_sent = parts
    rows = left.shape[0] // 2
    kinds = [shape((rows, member.shape[1]), BF) for member in (left, left, right, right)]
    return run(
        fold_kernel, "fold", kinds,
        [left, dp_swap(left_sent, 1), right, dp_swap(right_sent, 2)],
    )


def square_split(parts):
    chips = chips_of()
    left, left_sent, right, right_sent = parts
    share = left.shape[0] // chips
    width = left.shape[1] + right.shape[1]
    return run(
        functools.partial(split_kernel, chips),
        "split",
        [shape((share, width), F32)] + [shape((share, width), BF)] * (chips - 1),
        [left, dp_swap(left_sent, 2), right, dp_swap(right_sent, 1)],
        (),
        [pltpu.VMEM((chips, share, width), F32)],
    )


def square_total(parts):
    total = parts[0]
    for step in range(1, len(parts)):
        total = total + chip_shift(parts[step], step).astype(F32)
    return total


def piece_matrix(width, block, count):
    spot = np.arange(width)
    inner = spot % block
    return one_hot(
        ((spot // block) % 2) * (width // 2)
        + (inner % count) * (width // (2 * count))
        + (spot // (2 * block)) * (block // count)
        + inner // count
    )


def peer_shift(array, bits):
    size = lax.axis_size("dp")
    return lax.ppermute(array, "dp", [(i, i ^ bits) for i in range(size)])


def peer_gather(array):
    return [array] + [peer_shift(array, bits) for bits in range(1, 4)]


def peer_trade(parts):
    return [parts[0]] + [peer_shift(parts[bits], bits) for bits in range(1, 4)]


def units_matrix(width, block, count):
    half = width // 2
    spot = np.arange(half)
    inner = spot % block
    chips = half // (block * count)
    return one_hot(
        (spot // block) % chips * (block * count) + inner * count + spot // (block * chips)
    )


def rows_matrix(width, block):
    half = width // 2
    spot = np.arange(half)
    chips = half // (4 * block)
    return one_hot(
        (spot // block) % chips * (4 * block) + spot // (block * chips) * block + spot % block
    )


def fast_device(
    hidden_input,
    triple_weight,
    mixer_weight,
    expand_weight,
    shrink_weight,
    vector_params,
    output_grad,
):
    _, count, width = hidden_input.shape
    chips = chips_of()
    _, core = place()
    share = triple_weight.shape[1]
    wide_share = shrink_weight.shape[1]
    wide = expand_weight.shape[2]
    groups = wide // width
    perm = swap_matrix(width, share)
    perm_wide = piece_matrix(width, wide_share, groups)
    mixer_moved = move(mixer_weight.reshape(-1, width), perm).reshape(mixer_weight.shape)
    shrink_moved = move(shrink_weight.reshape(-1, width), perm).reshape(shrink_weight.shape)
    pieces = 2 * groups
    spot = lax.axis_index("dp")
    perm_rows = rows_matrix(width, share)
    perm_units = units_matrix(width, share, groups)
    expand_zero = move(expand_weight[0].reshape(-1, width), perm_wide).reshape(share, wide)
    expand_one = (
        move(expand_weight[1].reshape(-1, width), perm_wide)
        .reshape(share, groups, pieces, width // pieces)
        .transpose(0, 2, 1, 3)
        .reshape(share, wide)
    )
    shrink_moved = shrink_moved.reshape(LAYERS, share, groups * width)
    vector_columns = vector_params.reshape(LAYERS * VECS, share).T
    vector_columns = jnp.pad(vector_columns, ((0, 0), (0, LANES - LAYERS * VECS)))

    parts = chips_parts(
        jnp.concatenate([triple_weight[0], mixer_moved[0], vector_columns], 1)
    )
    expand_zero = after(expand_zero, parts[1])
    expand_zero = jnp.concatenate(
        peer_trade(
            [
                lax.dynamic_slice(
                    expand_zero, (0, jnp.bitwise_xor(spot, bits) * width), (share, width)
                )
                for bits in range(4)
            ]
        ),
        1,
    )
    feed_parts = [
        jnp.concatenate([expand_zero, shrink_moved[0]], 1),
        jnp.concatenate([expand_one, shrink_moved[1]], 1),
    ]
    early = jnp.concatenate([feed_parts[0], triple_weight[1], mixer_moved[1]], 1)
    parts[-1] = after(parts[-1], early, feed_parts[1])
    attn = chips_join(parts)
    early = chips_gather(after(early, attn))
    feed_zero, attn_one = early[:, : 2 * wide], early[:, 2 * wide :]
    attn = square_second(*square_first(attn, 2 * width))
    attn = square_pieces(*attn)

    def project(layer, hidden, pieces):
        bias = perm[:8].astype(F32) if layer == 0 else rows_of[layer][1]
        low, blocks = project_fast(layer, chips, hidden, perm, bias, pieces)
        blocks = [blocks[0]] + [chip_shift(blocks[step], step) for step in range(1, chips)]
        return low, blocks

    def attend_blocks(blocks):
        others = [core_swap(block) for block in blocks]
        mixed, logs, pieces = attend_fast(chips, blocks, others)
        pieces = [pieces[0]] + [chip_shift(pieces[step], -step) for step in range(1, chips)]
        return (blocks, others, mixed, logs), pieces

    def feed(layer, hidden, low, pieces, weights):
        rows, _, ffn_bias = rows_of[layer]
        (
            hidden, attended, normed, pre_act, act, hat_one, scale_one, hat_two, scale_two,
            sent, squares,
        ) = feed_fast(layer, chips, hidden, low, perm, rows, ffn_bias, pieces, weights)
        return (
            hidden,
            (hat_one, scale_one, hat_two, scale_two, pre_act),
            (low, attended, normed, act, core_swap(sent)),
            jnp.sum(squares[:3], -1),
        )

    low_zero, blocks = project(0, hidden_input[0], attn)
    feed_zero = after(feed_zero, *blocks)
    attn_one = square_second(*square_first(after(attn_one, *blocks), 2 * width))
    feed_one = chips_gather(after(feed_parts[1], *blocks))
    blocks[0] = after(blocks[0], attn_one[0], attn_one[2])
    attend_zero, pieces = attend_blocks(blocks)
    attn_one = [
        attn_one[0], after(attn_one[1], attend_zero[2]),
        attn_one[2], after(attn_one[3], attend_zero[2]),
    ]
    vector_pieces = [after(attn[4], attend_zero[2], attn_one[1], attn_one[3]), *attn[5:]]
    rows_of = vectors_fast(groups, perm, perm_wide, vector_pieces)
    attn_one = square_pieces(*attn_one)
    slice_pieces = [feed_zero, core_swap(feed_zero)]
    pieces[0] = after(pieces[0], slice_pieces[1], *attn_one)

    attended, normed, normed_low, hat, scale, sent, squares = mix_fast(
        chips, low_zero, low_zero, perm, rows_of[0][0], pieces, attn[4:]
    )
    norms_zero, acts_zero = (hat, scale), (low_zero, attended, None, None, core_swap(sent))
    inputs = peer_gather(normed_low)
    terms, pre, act = slice_feed_fast(rows_of[0][2], inputs, slice_pieces)
    feed_one = lax.all_gather(after(feed_one, normed), "dp", axis=0, tiled=True)
    slice_saved = (inputs, pre, act)
    hidden, hat, scale, squares = finish_fast(normed, rows_of[0][0], squares, peer_trade(terms))
    ends_zero, squares_zero = (hat, scale), jnp.sum(squares[:3], -1)

    low, blocks = project(1, hidden, attn_one)
    attend_one, pieces = attend_blocks(blocks)
    feed_one = after(feed_one, attend_one[2])
    feed_one = [feed_one, core_swap(feed_one)]
    hidden, feed_saved_one, acts_one, squares_one = feed(
        1, hidden, low, pieces, attn_one[4:] + feed_one
    )
    packs = [attn, attn_one + feed_one]
    kept = [(attend_zero, None, acts_zero), (attend_one, feed_saved_one, acts_one)]
    collected = [squares_zero, squares_one]
    elements = count * width * lax.axis_size("dp") * lax.axis_size("seq")
    hidden_output = move_back(hidden.astype(BF), perm)

    totals = jnp.stack(collected)
    sum_steps = [("seq", 1), ("seq", 2), ("seq", 4), ("dp", 1), ("dp", 2)]
    sum_steps = [step for step in sum_steps if step[1] < lax.axis_size(step[0])]

    def sum_more(totals, token):
        if sum_steps:
            axis, bit = sum_steps.pop(0)
            size = lax.axis_size(axis)
            pairs = [(i, i ^ bit) for i in range(size)]
            totals = totals + lax.ppermute(after(totals, token), axis, pairs)
        return totals

    def scatter_feed(term):
        part = lax.psum_scatter(term, "dp", scatter_dimension=0, tiled=True)
        part = lax.psum_scatter(
            part, "seq", scatter_dimension=0, tiled=True, axis_index_groups=core_groups()
        )
        return part.astype(F32)

    def back_feed(layer, grad):
        (_, feed_saved, acts), weights = kept[layer], packs[layer]
        grad_one, gave, attn_nat, sums, grads = feed_back_fast(
            layer, chips, grad, perm, perm_wide, rows_of[layer][0], feed_saved,
            weights[4:],
        )
        grads = [grads[0]] + [chip_shift(grads[step], step) for step in range(1, chips)]
        _, _, normed, act, theirs = acts
        feed_term = feed_terms_fast(normed, act, gave, theirs, core_swap(gave))
        return grad_one, attn_nat, sums, grads, feed_term

    def back_attend(layer, grads):
        blocks, others, mixed, logs = kept[layer][0]
        return attend_back_fast(chips, blocks, others, grads, mixed, logs)

    def back_combine(grad_q, near, far):
        pieces = combine_fast(chips, grad_q, near, far)
        return [pieces[0]] + [chip_shift(pieces[step], -step) for step in range(1, chips)]

    def back_project(layer, grad_one, sums, pieces):
        return project_back_fast(layer, chips, grad_one, perm, sums, pieces, packs[layer][:8])

    def back_terms(layer, project_grad, attn_nat, vector, far):
        low, attended, _, _, theirs = kept[layer][2]
        return attend_terms_fast(
            low, attended, project_grad, attn_nat, vector, theirs, *far
        )

    def swap_all(*members):
        return [core_swap(member) for member in members]

    grad_one, attn_nat, sums, grads, feed_term = back_feed(1, output_grad[0])
    totals = sum_more(totals, grad_one)
    feed_sum_one = lax.psum_scatter(feed_term, "dp", scatter_dimension=0, tiled=True)
    grads[0] = after(grads[0], feed_term, totals, hidden_output)
    grad_q, near, far = back_attend(1, grads)
    pieces = back_combine(grad_q, near, core_swap(far))
    for _ in range(2):
        totals = sum_more(totals, pieces[0])
    pieces[0] = after(pieces[0], totals)
    grad, project_grad, vector = back_project(1, grad_one, sums, pieces)
    far_one = swap_all(project_grad, attn_nat, vector)
    terms_args = (project_grad, attn_nat, vector)

    attn_terms = back_terms(1, *terms_args, far_one)
    rows = rows_of[0][0]
    grad_two, grad_low, sums = finish_back_fast(False, grad, perm, rows, *ends_zero)
    blocks = peer_gather(grad_low)
    blocks[1] = after(blocks[1], feed_sum_one, attn_terms[0])
    feed_sum_one = chips_scatter(feed_sum_one).astype(F32)
    inputs, pre, act = slice_saved
    terms, slope, gave, feed_sums = slice_back_fast(blocks, inputs, pre, act, slice_pieces)
    totals = sum_more(totals, slope)
    terms = peer_trade(terms)
    terms[0] = after(terms[0], totals)
    grad_one, attn_nat, sums, grads = mix_back_fast(
        chips, grad_two, perm, rows, *norms_zero, sums, terms, attn[4:]
    )
    grads = [grads[0]] + [chip_shift(grads[step], step) for step in range(1, chips)]
    attn_terms = [
        attn_terms[0], after(attn_terms[1], grad_one), attn_terms[2], after(attn_terms[3], grad_one)
    ]
    totals = sum_more(totals, grad_one)
    grads[0] = after(grads[0], feed_sum_one, totals)
    grad_q, near, far = back_attend(0, grads)
    feed_term = slice_terms_fast(
        perm_rows, perm_units, blocks, inputs, act, after(slope, grad_q), core_swap(gave)
    )
    feed_sum_zero = chips_scatter(feed_term)
    attn_terms[0] = after(attn_terms[0], grad_q)
    folded = square_fold(attn_terms)
    pieces = back_combine(after(grad_q, folded[0]), near, core_swap(far))
    split_one = square_split(folded)
    pieces[0] = after(pieces[0], split_one[0], feed_term)
    project_grad, vector = collect_fast(chips, perm, perm_wide, feed_sums, sums, pieces)
    far_zero = swap_all(project_grad, attn_nat, vector)
    attn_terms = list(back_terms(0, project_grad, attn_nat, vector, far_zero))
    folded = square_fold(attn_terms)
    input_grad = input_back_fast(after(grad_one, folded[0]), perm, project_grad, attn)
    split_one = [after(split_one[0], folded[0]), *split_one[1:]]
    attn_sum_one = square_total(split_one)
    feed_sum_zero = after(feed_sum_zero, folded[0])
    expand_sums = peer_trade(
        [
            lax.dynamic_slice(
                feed_sum_zero, (jnp.bitwise_xor(spot, bits) * share, 0), (share, width)
            )
            for bits in range(4)
        ]
    )
    expand_zero = jnp.concatenate(
        [
            matmul_t(
                lax.select_n(spot, *[expand_sums[index ^ other] for other in range(4)]), perm_wide
            )
            for index in range(groups)
        ],
        1,
    )
    shrink_zero = matmul_t(feed_sum_zero[:, width:], perm)
    folded = [after(folded[0], input_grad, *expand_sums, shrink_zero), *folded[1:]]
    attn_sum_zero = square_total(square_split(folded))
    terms = [(attn_sum_zero, None), (attn_sum_one, None)]
    expand_grads = [expand_zero, feed_sum_one[:, :wide]]
    shrink_grads = [shrink_zero, feed_sum_one[:, wide:].reshape(wide_share, width)]
    grad = input_grad
    root_squares = jnp.sqrt(totals / elements)
    vector_grad = jnp.stack(
        [
            (
                terms[layer][0][:, 4 * width : 4 * width + VECS]
                + terms[layer][0][:, 4 * width + 16 : 4 * width + 16 + VECS]
            ).T
            for layer in range(LAYERS)
        ]
    )
    return (
        hidden_output[None],
        grad[None],
        jnp.stack([terms[layer][0][:, : 3 * width] for layer in range(LAYERS)]),
        jnp.stack([terms[layer][0][:, 3 * width : 4 * width] for layer in range(LAYERS)]),
        jnp.stack(expand_grads),
        jnp.stack(shrink_grads),
        vector_grad,
        root_squares,
    )


def per_device(*args):
    chips = chips_of()
    if chips in (2, 4) and HEADS % chips == 0 and lax.axis_size("dp") == 4:
        return fast_device(*args)
    return plain_device(*args)


def solution(mesh):
    return jax.shard_map(
        per_device,
        mesh=mesh,
        in_specs=(
            P("dp", "seq", None),
            P(None, ("dp", "seq"), None),
            P(None, ("dp", "seq"), None),
            P(None, ("dp", "seq"), None),
            P(None, ("dp", "seq"), None),
            P(None, None, ("dp", "seq")),
            P("dp", "seq", None),
        ),
        out_specs=(
            P("dp", "seq", None),
            P("dp", "seq", None),
            P(None, ("dp", "seq"), None),
            P(None, ("dp", "seq"), None),
            P(None, ("dp", "seq"), None),
            P(None, ("dp", "seq"), None),
            P(None, None, ("dp", "seq")),
            P(),
        ),
        check_vma=False,
    )
```
